32 devices in a mesh: dp: 4 (over z), fsdp: 8 (over y, x, core).
Axes of the slice: x: 2, y: 2, z: 4, core: 2. Of those that a mesh axis runs over, the one named last changes fastest.
Arguments:
- tokens: bfloat16 [32, 448, 768], P(('dp', 'fsdp')), may hold values from -6 to 6
- enc_states: bfloat16 [32, 1500, 768], P(('dp', 'fsdp')), may hold values from -6 to 6
- cotangent: bfloat16 [32, 448, 768], P(('dp', 'fsdp')), may hold values from -6 to 6
- tok_len: int32 [32], P(('dp', 'fsdp')), may hold values from 224 to 448, as said below
- frame_count: int32 [32], P(('dp', 'fsdp')), may hold values from 750 to 1500, as said below
- attn_w: float32 [8, 768, 768], P(None, ('dp', 'fsdp'))
- attn_m: float32 [8, 768, 768], P(None, ('dp', 'fsdp')), may hold values from -40 to 40
- attn_v: float32 [8, 768, 768], P(None, ('dp', 'fsdp')), may hold values from 1.792 to 28.672
- mlp_w: float32 [2, 3072, 768], P(None, ('dp', 'fsdp')), may hold values from -0.21875 to 0.21875
- mlp_m: float32 [2, 3072, 768], P(None, ('dp', 'fsdp')), may hold values from -40 to 40
- mlp_v: float32 [2, 3072, 768], P(None, ('dp', 'fsdp')), may hold values from 1.792 to 28.672
- vec_w: float32 [17, 768], P(None, ('dp', 'fsdp'))
- vec_m: float32 [17, 768], P(None, ('dp', 'fsdp')), may hold values from -80 to 80
- vec_v: float32 [17, 768], P(None, ('dp', 'fsdp')), may hold values from 7.168 to 114.688
Outputs:
- out: bfloat16 [32, 448, 768], P(('dp', 'fsdp'))
- d_tokens: float32 [32, 448, 768], P(('dp', 'fsdp'))
- d_enc: float32 [32, 1500, 768], P(('dp', 'fsdp'))
- attn_w_new: float32 [8, 768, 768], P(None, ('dp', 'fsdp'))
- attn_m_new: float32 [8, 768, 768], P(None, ('dp', 'fsdp'))
- attn_v_new: float32 [8, 768, 768], P(None, ('dp', 'fsdp'))
- mlp_w_new: float32 [2, 3072, 768], P(None, ('dp', 'fsdp'))
- mlp_m_new: float32 [2, 3072, 768], P(None, ('dp', 'fsdp'))
- mlp_v_new: float32 [2, 3072, 768], P(None, ('dp', 'fsdp'))
- vec_w_new: float32 [17, 768], P(None, ('dp', 'fsdp'))
- vec_m_new: float32 [17, 768], P(None, ('dp', 'fsdp'))
- vec_v_new: float32 [17, 768], P(None, ('dp', 'fsdp'))
The draws below stay inside these ranges and needn't reach their ends.
Inputs may be any that keep to these rules, and one draw needn't show every extreme that they name: `tok_len`: at least 224 slots of every clip are valid, and some clip has all 448. `frame_count`: at least 750 frames of every clip are valid, and some clip has all 1500.
All inputs are finite; a program needn't handle non-finite values.
Results may differ from the reference program's by a relative error of at most 0.018.
The reference program's roundings to bfloat16 on the way count: a program that leaves them out, or rounds other values in their place, can miss the bound.
Values may be sent and summed in bfloat16 or wider, within the bound.
A program may use at most 256 MiB of HBM per device.

```python
import math
import jax
import jax.numpy as jnp
from jax import lax

D = 768
H = 12
HD = 64
FF = 3072
FRAMES = 1500
TOK = 448
STEP = 10
CLIPS = 32
NV = 17


def draw_tok_len(key, part):
    key = jax.random.fold_in(key, 3)
    first, second = jax.random.split(key)
    counts = jax.random.randint(first, (CLIPS,), TOK // 2, TOK + 1)
    chosen = jax.random.randint(second, (), 0, CLIPS)
    return jnp.where(jnp.arange(CLIPS) == chosen, TOK, counts).astype(jnp.int32)


def draw_frame_count(key, part):
    key = jax.random.fold_in(key, 4)
    first, second = jax.random.split(key)
    counts = jax.random.randint(first, (CLIPS,), FRAMES // 2, FRAMES + 1)
    chosen = jax.random.randint(second, (), 0, CLIPS)
    return jnp.where(jnp.arange(CLIPS) == chosen, FRAMES, counts).astype(jnp.int32)


def draw_attn_w(key, part):
    key = jax.random.fold_in(key, 1)
    base = jnp.clip(jax.random.normal(key, (8, D, D), jnp.float32), -6.0, 6.0)
    which = jnp.arange(8)
    factor = jnp.where((which == 3) | (which == 7), 4.0, 1.0) * D ** (-0.5)
    return base * factor[:, None, None]


def draw_vec_w(key, part):
    key = jax.random.fold_in(key, 2)
    first, second = jax.random.split(key)
    noise = jnp.clip(0.3 * jax.random.normal(first, (NV, D), jnp.float32), -1.5, 1.5)
    level = jax.random.uniform(second, (NV, D), jnp.float32, -1.0, 1.0)
    row = jnp.arange(NV)[:, None]
    is_gain = (row < 6) & (row % 2 == 0)
    return jnp.where(is_gain, 1.0 + 0.5 * level, noise)


def shard_levels(key, shape, shards, smallest, high):
    level, own = 1.0, jax.random.fold_in(key, 6)
    for position, blocks in shards:
        steps = jnp.exp(jax.random.uniform(jax.random.fold_in(own, position), (blocks,), jnp.float32, smallest / len(shards), high / len(shards)))
        level = level * jnp.repeat(steps, shape[position] // blocks).reshape([-1 if axis == position else 1 for axis in range(len(shape))])
    return level


def bell_draw(own_key, shape, deviation, most, cuts=(), dtype=jnp.bfloat16):
    array = deviation * jax.random.normal(own_key, shape, jnp.float32)
    if cuts:
        array = array * shard_levels(own_key, shape, cuts, -0.22, 0.18)
    return jnp.clip(array, -most, most).astype(dtype)


def setup_inputs(seed: int = 0) -> dict:
    streams_of = jax.random.split(jax.random.key(seed), 15)
    return {
        "tokens": bell_draw(streams_of[0], (CLIPS, TOK, D), 1.0, 6.0, ((0, 32),)),
        "enc_states": bell_draw(streams_of[1], (CLIPS, FRAMES, D), 1.0, 6.0, ((0, 32),)),
        "cotangent": bell_draw(streams_of[2], (CLIPS, TOK, D), 1.0, 6.0, ((0, 32),)),
        "tok_len": draw_tok_len(jax.random.fold_in(streams_of[14], 71), 0),
        "frame_count": draw_frame_count(jax.random.fold_in(streams_of[14], 71), 0),
        "attn_w": draw_attn_w(jax.random.fold_in(streams_of[14], 71), 0),
        "attn_m": bell_draw(streams_of[6], (8, D, D), (0.055 * (CLIPS * TOK) ** 0.5), 40.0, ((1, 32),), jnp.float32),
        "attn_v": jnp.clip(jnp.exp(math.log(28.672) - 2.7725887 * jax.random.uniform(streams_of[7], (8, D, D), jnp.float32) ** shard_levels(streams_of[7], (8, D, D), ((1, 32),), -0.2, 0.2)), 1.792, 28.672),
        "mlp_w": bell_draw(streams_of[8], (2, FF, D), D ** -0.5, 0.21875, ((1, 32),), jnp.float32),
        "mlp_m": bell_draw(streams_of[9], (2, FF, D), (0.055 * (CLIPS * TOK) ** 0.5), 40.0, ((1, 32),), jnp.float32),
        "mlp_v": jnp.clip(jnp.exp(math.log(28.672) - 2.7725887 * jax.random.uniform(streams_of[10], (2, FF, D), jnp.float32) ** shard_levels(streams_of[10], (2, FF, D), ((1, 32),), -0.2, 0.2)), 1.792, 28.672),
        "vec_w": draw_vec_w(jax.random.fold_in(streams_of[14], 71), 0),
        "vec_m": bell_draw(streams_of[12], (NV, D), (0.11 * (CLIPS * TOK) ** 0.5), 80.0, ((1, 32),), jnp.float32),
        "vec_v": jnp.clip(jnp.exp(math.log(114.688) - 2.7725887 * jax.random.uniform(streams_of[13], (NV, D), jnp.float32) ** shard_levels(streams_of[13], (NV, D), ((1, 32),), -0.2, 0.2)), 7.168, 114.688),
    }


norm_epsilon = 1e-05
beta_first = 0.9
beta_second = 0.999
adam_epsilon = 1e-08
weight_decay = 0.01
rate_attention = 0.06
rate_feedforward = 0.03
rate_vector = 0.35

@jax.custom_vjp
def low(v):
    return lax.optimization_barrier(v.astype(jnp.bfloat16)).astype(jnp.float32)

@jax.custom_vjp
def low_back(v):
    return v

def low_keep(v):
    return (low(v), None)

def low_pass(kept, grad):
    return (grad,)

def back_keep(v):
    return (v, None)

def back_low(kept, grad):
    return (low(grad),)
low.defvjp(low_keep, low_pass)
low_back.defvjp(back_keep, back_low)

def product(left, right):
    return jnp.dot(left, right, precision=lax.Precision.HIGHEST, preferred_element_type=jnp.float32)

def norm_apply(value, gain, shift):
    center = value - lax.optimization_barrier(jnp.mean(value, -1, keepdims=True))
    spread = lax.optimization_barrier(jnp.mean(center * center, -1, keepdims=True))
    return center * lax.rsqrt(spread + norm_epsilon) * gain + shift

def attend(query, keys, values, mask):
    q_heads = query.reshape(query.shape[0], H, HD)
    k_heads = keys.reshape(keys.shape[0], H, HD)
    v_heads = values.reshape(values.shape[0], H, HD)
    scores = low_back(jnp.einsum('thd,shd->hts', q_heads, k_heads, precision=lax.Precision.HIGHEST))
    scores = jnp.where(mask[None], scores, -1e+30)
    probs = low(jax.nn.softmax(scores, axis=-1))
    mixed = jnp.einsum('hts,shd->thd', probs, v_heads, precision=lax.Precision.HIGHEST)
    return mixed.reshape(query.shape[0], H * HD)

def clip_forward(wa, wm, wv, x, enc, length, frames):
    scale = HD ** (-0.5)
    place = jnp.arange(TOK)
    causal = (place[None, :] <= place[:, None]) & (place[None, :] < length)
    seen = jnp.broadcast_to(jnp.arange(FRAMES)[None, :] < frames, (TOK, FRAMES))
    first = low(norm_apply(x, wv[0], wv[1]))
    query = low(low_back((product(first, wa[0]) + wv[6]) * scale))
    keys = low(low_back(product(first, wa[1])))
    values = low(low_back(product(first, wa[2]) + wv[7]))
    mixed = low(low_back(attend(query, keys, values, causal)))
    second_in = x + low_back(product(mixed, wa[3]) + wv[8])
    second = low(norm_apply(second_in, wv[2], wv[3]))
    cross_query = low(low_back((product(second, wa[4]) + wv[9]) * scale))
    cross_keys = low(low_back(product(enc, wa[5])))
    cross_values = low(low_back(product(enc, wa[6]) + wv[10]))
    heard = low(low_back(attend(cross_query, cross_keys, cross_values, seen)))
    third_in = second_in + low_back(product(heard, wa[7]) + wv[11])
    third = low(norm_apply(third_in, wv[4], wv[5]))
    hidden_pre = low_back(product(third, wm[0].T) + wv[13:].reshape(FF))
    hidden = low(jax.nn.gelu(hidden_pre, approximate=False))
    return third_in + low_back(product(hidden, wm[1]) + wv[12])

def adam_update(weight, first, second, grad, rate):
    first_new = beta_first * first + (1.0 - beta_first) * grad
    second_new = beta_second * second + (1.0 - beta_second) * grad * grad
    ratio = first_new / (1.0 - beta_first ** STEP) / (jnp.sqrt(second_new / (1.0 - beta_second ** STEP)) + adam_epsilon)
    return (weight - rate * (ratio + weight_decay * weight), first_new, second_new)

def reference(tokens, enc_states, cotangent, tok_len, frame_count, attn_w, attn_m, attn_v, mlp_w, mlp_m, mlp_v, vec_w, vec_m, vec_v):

    def forward(attn, mlp, vecs, inputs, encoded):
        wa = low(attn)
        wm = low(mlp)
        wv = low(vecs)

        def one_clip(items):
            x, enc, length, frames = items
            return clip_forward(wa, wm, wv, x, enc, length, frames)
        return lax.map(jax.checkpoint(one_clip), (inputs, encoded, tok_len, frame_count))
    result, pullback = jax.vjp(forward, attn_w, mlp_w, vec_w, tokens.astype(jnp.float32), enc_states.astype(jnp.float32))
    place = jnp.arange(TOK)
    rows = (place[None, :] < tok_len[:, None]).astype(jnp.float32)
    grad_attn, grad_mlp, grad_vec, d_tokens, d_enc = pullback(cotangent.astype(jnp.float32) * rows[:, :, None])
    attn_new = adam_update(attn_w, attn_m, attn_v, grad_attn, rate_attention)
    mlp_new = adam_update(mlp_w, mlp_m, mlp_v, grad_mlp, rate_feedforward)
    vec_new = adam_update(vec_w, vec_m, vec_v, grad_vec, rate_vector)
    return (result.astype(jnp.bfloat16), d_tokens, d_enc, attn_new[0], attn_new[1], attn_new[2], mlp_new[0], mlp_new[1], mlp_new[2], vec_new[0], vec_new[1], vec_new[2])
```

```python
import functools
import jax
import jax.numpy as jnp
from jax import lax
from jax.experimental import pallas as pl
from jax.experimental.pallas import tpu as pltpu
from jax.sharding import PartitionSpec as P

D = 768
H = 12
HD = 64
FF = 3072
FRAMES = 1500
TOK = 448
STEP = 10
PADDED = 1536
ROWS = 24
PLANE = 4
DEPTH = 4
UNITS = 16
HALF = D // 2
BF = jnp.bfloat16
F32 = jnp.float32
MESH = pl.DeviceIdType.MESH
norm_epsilon = 1e-05
MIB = 2**20


def dot(a, b):
    return lax.dot_general(a, b, (((1,), (0,)), ((), ())), preferred_element_type=F32)


def dot_nt(a, b):
    return lax.dot_general(a, b, (((1,), (1,)), ((), ())), preferred_element_type=F32)


def dot_tn(a, b):
    return lax.dot_general(a, b, (((0,), (0,)), ((), ())), preferred_element_type=F32)


def layer_norm(v, gain, shift):
    c = v - jnp.mean(v, -1, keepdims=True)
    s = jnp.mean(c * c, -1, keepdims=True)
    return c * lax.rsqrt(s + norm_epsilon) * gain + shift


def layer_norm_back(v, gain, grad):
    c = v - jnp.mean(v, -1, keepdims=True)
    r = lax.rsqrt(jnp.mean(c * c, -1, keepdims=True) + norm_epsilon)
    xh = c * r
    t = grad * gain
    dx = r * (t - jnp.mean(t, -1, keepdims=True) - xh * jnp.mean(t * xh, -1, keepdims=True))
    return dx, jnp.sum(grad * xh, 0, keepdims=True), jnp.sum(grad, 0, keepdims=True)


def gelu_both(u):
    z = jnp.abs(u) * 0.7071067811865476
    e = jnp.exp(-0.5 * u * u)
    t = 1.0 / (1.0 + 0.3275911 * z)
    poly = t * (0.254829592 + t * (-0.284496736 + t * (1.421413741 + t * (-1.453152027 + t * 1.061405429))))
    half = 0.5 * poly * e
    phi = jnp.where(u >= 0, 1.0 - half, half)
    return u * phi, phi + u * (e * 0.3989422804014327)


def colsum(v):
    return jnp.sum(v.astype(F32), 0, keepdims=True)


def head_lanes(rows, h):
    return (lax.broadcasted_iota(jnp.int32, (rows, 128), 1) // HD) == h


class Place:
    def __init__(self):
        self.z = lax.axis_index("dp")
        f = lax.axis_index("fsdp")
        self.f = f
        self.c = f % 2
        self.p = f // 2
        x, y = self.p % 2, self.p // 2
        self.part = f + 1 - 2 * self.c
        fx, fy = f + 2 - 4 * x, f + 4 - 8 * y
        px, py = self.p + 1 - 2 * x, self.p + 2 - 4 * y
        c = self.c
        self.n1, self.n2 = fx + c * (fy - fx), fy + c * (fx - fy)
        self.p1, self.p2, self.p3 = px + c * (py - px), py + c * (px - py), 3 - self.p
        self.zto = [(self.z + d) % DEPTH for d in range(1, DEPTH)]
        self.zfrom = [(self.z + DEPTH - d) % DEPTH for d in range(1, DEPTH)]
        self.own = pl.ds(pl.multiple_of(c * HALF, 128), HALF)
        self.other = pl.ds(pl.multiple_of(HALF - c * HALF, 128), HALF)

    def greet(self):
        barrier = pltpu.get_barrier_semaphore()
        others = [(zz, self.f) for zz in self.zto]
        others += [(self.z, self.n1), (self.z, self.n2), (self.z, self.part)]
        for device in others:
            pl.semaphore_signal(barrier, inc=1, device_id=device, device_id_type=MESH)
        pl.semaphore_wait(barrier, len(others))


def remote(src, dst, send, recv, device):
    return pltpu.make_async_remote_copy(
        src_ref=src, dst_ref=dst, send_sem=send, recv_sem=recv, device_id=device, device_id_type=MESH
    )


class Gather:
    def __init__(self, place, view, send, recv):
        self.w, self.view, self.send, self.recv = place, view, send, recv

    def copy(self, k, ref, device):
        return remote(ref, ref, self.send(k), self.recv(k), device)

    def own(self, zz, p):
        return self.view(zz, p, True)

    def s1(self):
        w = self.w
        for i, zz in enumerate(w.zto):
            self.copy(i, self.own(w.z, w.p), (zz, w.f)).start()

    def s2(self):
        w = self.w
        for i, zz in enumerate(w.zfrom):
            self.copy(i, self.own(zz, w.p), (zz, w.f)).wait_recv()
        self.copy(3, self.own(None, w.p), (w.z, w.n1)).start()
        self.copy(4, self.own(None, w.p), (w.z, w.n2)).start()
        self.copy(6, self.own(None, w.p), (w.z, w.part)).start()

    def s3(self):
        w = self.w
        self.copy(3, self.own(None, w.p1), (w.z, w.n1)).wait_recv()
        self.copy(5, self.own(None, w.p1), (w.z, w.n2)).start()
        self.copy(7, self.own(None, w.p1), (w.z, w.part)).start()

    def s4(self):
        w = self.w
        self.copy(4, self.own(None, w.p2), (w.z, w.n2)).wait_recv()
        self.copy(8, self.own(None, w.p2), (w.z, w.part)).start()

    def s5(self):
        w = self.w
        self.copy(5, self.own(None, w.p3), (w.z, w.n2)).wait_recv()
        self.copy(9, self.own(None, w.p3), (w.z, w.part)).start()

    def ready(self):
        w = self.w
        for k, p in enumerate((w.p, w.p1, w.p2, w.p3)):
            self.copy(6 + k, self.view(None, p, False), (w.z, w.part)).wait_recv()

    def drain(self):
        w = self.w
        for i, zz in enumerate(w.zto):
            self.copy(i, self.own(w.z, w.p), (zz, w.f)).wait_send()
        for k, p in ((3, w.p), (4, w.p), (5, w.p1), (6, w.p), (7, w.p1), (8, w.p2), (9, w.p3)):
            self.copy(k, self.own(None, p), (w.z, w.n1)).wait_send()


def heads_forward(q_ref, k_ref, v_ref, o_ref, lse_ref, mask_fn, keys, tile, first, count):
    def pair(hp):
        lanes = pl.ds(pl.multiple_of(hp * 128, 128), 128)
        kp, vp = k_ref[:keys, lanes], v_ref[:keys, lanes]
        for i in range(TOK // tile):
            rows = pl.ds(i * tile, tile)
            qp = q_ref[rows, lanes]
            outs = []
            for h in range(2):
                s = dot_nt(jnp.where(head_lanes(tile, h), qp, jnp.zeros_like(qp)), kp)
                s = mask_fn(s, i)
                peak = jnp.max(s, -1, keepdims=True)
                expo = jnp.exp(s - peak)
                total = jnp.sum(expo, -1, keepdims=True)
                outs.append(dot(expo.astype(BF), vp) * (1.0 / total))
                lane = lax.broadcasted_iota(jnp.int32, (tile, 128), 1)
                lse_ref[rows, :] = jnp.where(lane == hp * 2 + h, peak + jnp.log(total), lse_ref[rows, :])
            o_ref[rows, lanes] = jnp.where(head_lanes(tile, 0), outs[0], outs[1]).astype(BF)

    def step(i, _):
        pair(first + i)
        return 0

    lax.fori_loop(0, count, step, 0)


def thirds(f):
    def step(j, _):
        f(pl.ds(pl.multiple_of(j * 256, 256), 256))
        return 0

    lax.fori_loop(0, 3, step, 0)


ORDER = [5, 6, 0, 1, 2, 3, 4, 7, 8, 12, 9, 13, 10, 14, 11, 15]
A1, Q, K, V_, O, A2, CQ, O2 = range(8)


def forward_kernel(
    len_ref, frames_ref, x_hbm, enc_hbm, cot_hbm, attn_hbm, mlp_hbm, vec_hbm,
    out_hbm, act_hbm, kv_hbm, lse_hbm, xs_hbm, wattn_hbm, gffn_hbm, vec_out, gv_out,
    weights, vgather, stage, x_ref, enc, cot, act, kv, lse_cols, lse_rows, xs, hm, gp, du, oacc, dacc, grads, vec, gv,
    load_sem, stage_sem, send_sem, recv_sem, vsend_sem, vrecv_sem, store_sem, gsem,
    *, comm=True,
):
    w = Place()
    length, frames = len_ref[0], frames_ref[0]
    local = lambda src, dst, sem: pltpu.make_async_copy(src, dst, sem)
    loads = [
        local(attn_hbm.at[:, :, w.own], stage.at[pl.ds(0, 8), w.c], load_sem.at[0]),
        local(mlp_hbm.at[:, :, w.own], stage.at[pl.ds(8, 8), w.c], load_sem.at[1]),
        local(vec_hbm, vgather.at[w.z, w.p, w.c], load_sem.at[2]),
        local(x_hbm, x_ref, load_sem.at[3]),
        local(enc_hbm, enc, load_sem.at[4]),
        local(cot_hbm, cot, load_sem.at[5]),
    ]
    for i in (2, 0, 1, 3, 4, 5):
        loads[i].start()
    w.greet()

    def unit_view(u):
        def view(zz, p, own):
            return weights.at[u, slice(None) if zz is None else zz, p, :, w.own if own else w.other]
        return view

    def vec_view(zz, p, own):
        return vgather.at[slice(None) if zz is None else zz, p, w.c if own else 1 - w.c]

    units = [Gather(w, unit_view(u), lambda k, u=u: send_sem.at[u, k], lambda k, u=u: recv_sem.at[u, k]) for u in ORDER]
    vecs = Gather(w, vec_view, lambda k: vsend_sem.at[k], lambda k: vrecv_sem.at[k])

    loads[2].wait()
    vecs.s1()
    parts = ((5, 2, attn_hbm, 5), (0, 5, attn_hbm, 0), (7, 1, attn_hbm, 7), (8, 8, mlp_hbm, 0))
    swaps = []
    for i, (u0, n, src, at) in enumerate(parts):
        src = src.at[pl.ds(at, n), :, w.other]
        swaps.append(remote(src, stage.at[pl.ds(u0, n), w.c], stage_sem.at[0, i], stage_sem.at[1, i], (w.z, w.part)))
        swaps[i].start()
    loads[0].wait()
    loads[1].wait()

    def cast(u):
        weights[u, w.z, w.p, :, w.own] = stage[u].reshape(2 * ROWS, HALF).astype(BF)

    for i, (u0, n, _, _) in enumerate(parts):
        swaps[i].wait_recv()
        for u in range(u0, u0 + n):
            cast(u)
        if i == 0:
            units[0].s1()
            units[1].s1()
            vecs.s2()
        if i == 1:
            units[2].s1()

    def tick(t):
        if t < UNITS:
            units[t].s2()
        if t + 3 < UNITS:
            units[t + 3].s1()
        if t >= 2 and t - 2 < UNITS:
            units[t - 2].s5()
        if t >= 1 and t - 1 < UNITS:
            units[t - 1].s3()
            units[t - 1].s4()

    stores = []

    def store(src, dst):
        c = local(src, dst, store_sem.at[len(stores)])
        c.start()
        stores.append(c)

    flat = weights
    def wcols(u, cols):
        return weights[u, :, :, :, cols].reshape(D, cols.size)

    vrow = lambda r, cols=slice(None): vec[r : r + 1, cols]

    lse_cols[...] = jnp.zeros_like(lse_cols)
    kv[:, FRAMES // 16 * 16 :, :] = jnp.zeros((2, PADDED - FRAMES // 16 * 16, D), BF)
    tick(0)
    vecs.s3()
    vecs.s4()
    vecs.s5()
    vecs.ready()
    tick(1)
    table = vgather[...].reshape(D, 128).astype(BF).astype(F32)
    vec[...] = jnp.transpose(table)[:24, :]
    lane = lax.broadcasted_iota(jnp.int32, (ROWS, 128), 1)
    blocks = []
    for chip in range(16):
        for core in range(2):
            acc = jnp.zeros((ROWS, 128), F32)
            for j in range(4):
                blk = table[(chip % 4) * 192 + core * 96 + j * ROWS :][:ROWS]
                col = jnp.sum(jnp.where(lane == 13 + chip // 4, blk, 0.0), -1, keepdims=True)
                acc = jnp.where(lane == j, col, acc)
            blocks.append(acc)
    vec[16:24, :] = jnp.transpose(jnp.concatenate(blocks, 0))[:8, :]
    loads[3].wait()
    act[A1] = layer_norm(x_ref[...].astype(F32), vrow(0), vrow(1)).astype(BF)
    tick(2)
    loads[4].wait()

    def enc_project(u, which, bias):
        for r0, r1 in ((0, 512), (512, 1024), (1024, FRAMES)):
            e = enc[r0:r1, :]

            def cols(cs):
                r = dot(e, wcols(u, cs))
                if bias is not None:
                    r = r + vrow(bias, cs)
                kv[which, r0:r1, cs] = r.astype(BF)

            thirds(cols)

    units[0].ready()
    enc_project(5, 0, None)
    tick(3)
    units[1].ready()
    enc_project(6, 1, 10)
    tick(4)

    def project(src, u, dst, bias, scale):
        def cols(cs):
            r = dot(act[src], wcols(u, cs))
            if bias is not None:
                r = r + vrow(bias, cs)
            act[dst, :, cs] = (r * scale).astype(BF)

        thirds(cols)

    units[2].ready()
    project(A1, 0, Q, 6, 0.125)
    tick(5)
    units[3].ready()
    project(A1, 1, K, None, 1.0)
    tick(6)
    units[4].ready()
    project(A1, 2, V_, 7, 1.0)

    def self_mask(s, i):
        r = lax.broadcasted_iota(jnp.int32, s.shape, 0) + i * s.shape[0]
        c = lax.broadcasted_iota(jnp.int32, s.shape, 1)
        return jnp.where((c <= r) & (c < length), s, -1e30)

    def cross_mask(s, i):
        c = lax.broadcasted_iota(jnp.int32, (1, PADDED - 640), 1) + 640
        return jnp.concatenate([s[:, :640], jnp.where(c < frames, s[:, 640:], -1e30)], axis=1)

    heads_forward(act.at[Q], act.at[K], act.at[V_], act.at[O], lse_cols.at[0], self_mask, TOK, 448, 0, 3)
    tick(7)
    heads_forward(act.at[Q], act.at[K], act.at[V_], act.at[O], lse_cols.at[0], self_mask, TOK, 448, 3, 3)
    units[5].ready()

    def residual(src, base, u, dst, bias):
        def cols(cs):
            xs[dst, :, cs] = base(cs) + dot(act[src], wcols(u, cs)) + vrow(bias, cs)

        thirds(cols)

    residual(O, lambda cs: x_ref[:, cs].astype(F32), 3, 0, 8)
    act[A2] = layer_norm(xs[0], vrow(2), vrow(3)).astype(BF)
    tick(8)
    units[6].ready()
    project(A2, 4, CQ, 9, 0.125)
    for i in range(3):
        heads_forward(act.at[CQ], kv.at[0], kv.at[1], act.at[O2], lse_cols.at[1], cross_mask, PADDED, 224, 2 * i, 2)
        tick(9 + i)
    units[7].ready()
    residual(O2, lambda cs: xs[0, :, cs], 7, 1, 11)
    a3 = layer_norm(xs[1], vrow(4), vrow(5)).astype(BF)
    act[8] = a3
    store(act.at[pl.ds(0, 8)], act_hbm)
    store(kv, kv_hbm)
    store(weights.at[pl.ds(0, 8)], wattn_hbm)
    for i in range(2):
        lse_rows[i] = jnp.transpose(lse_cols[i])[:16, :]
    store(lse_rows, lse_hbm)
    store(xs.at[0], xs_hbm.at[0])
    loads[5].wait()
    ok = lax.broadcasted_iota(jnp.int32, (TOK, 1), 0) < length
    cot[...] = jnp.where(ok, cot[...], jnp.zeros((TOK, D), BF))
    gv[...] = jnp.zeros_like(gv)
    gv[12:13, :] = colsum(cot[...])
    oacc[...] = jnp.zeros_like(oacc)
    dacc[...] = jnp.zeros_like(dacc)

    rows3 = lambda u, rs: weights.at[u].reshape(D, D)[rs, :]

    gcopies = {}
    for j in range(4):
        units[8 + 2 * j].ready()
        units[9 + 2 * j].ready()
        if j >= 2:
            gcopies[(0, j - 2)].wait()
            gcopies[(1, j - 2)].wait()

        def part(t, _):
            rs = pl.ds(pl.multiple_of(t * 256, 256), 256)
            u = dot_nt(act[8], rows3(8 + j, rs)) + vec[16 + j : 17 + j, rs]
            g, d = gelu_both(u)
            hm[:, rs] = g.astype(BF)
            gp[:, rs] = d.astype(BF)
            return 0

        lax.fori_loop(0, 3, part, 0)

        def part2(t, _):
            rs = pl.ds(pl.multiple_of(t * 256, 256), 256)
            oacc[:, rs] += dot(hm[...], wcols(12 + j, rs))
            d = (dot_nt(cot[...], rows3(12 + j, rs)) * gp[:, rs].astype(F32)).astype(BF)
            du[:, rs] = d
            gv[13 + j : 14 + j, rs] = colsum(d)
            return 0

        lax.fori_loop(0, 3, part2, 0)
        if j < 3:
            tick(12 + 2 * j)

        def part3(t, _):
            rs = pl.ds(pl.multiple_of(t * 256, 256), 256)
            grads[j % 2, 1, rs, :] = dot_tn(hm[:, rs], cot[...]).astype(BF)
            grads[j % 2, 0, rs, :] = dot_tn(du[:, rs], act[8]).astype(BF)
            dacc[:, rs] += dot(du[...], wcols(8 + j, rs))
            return 0

        lax.fori_loop(0, 3, part3, 0)
        for k in range(2):
            cp = local(grads.at[j % 2, k], gffn_hbm.at[4 * k + j], gsem.at[j % 2, k])
            cp.start()
            gcopies[(k, j)] = cp
        if j < 3:
            tick(13 + 2 * j)
    act[8] = (xs[1] + oacc[...] + vrow(12)).astype(BF)
    store(act.at[8], out_hbm)
    dx, gg, gb = layer_norm_back(xs[1], vrow(4), dacc[...])
    gv[4:5, :] = gg
    gv[5:6, :] = gb
    oacc[...] = cot[...].astype(F32) + dx
    store(oacc, xs_hbm.at[1])
    store(vec, vec_out)
    store(gv, gv_out)
    for j in (2, 3):
        gcopies[(0, j)].wait()
        gcopies[(1, j)].wait()
    for s in swaps:
        s.wait_send()
    vecs.drain()
    for u in units:
        u.drain()
    for c in stores:
        c.wait()


def call_forward(length, frames, x, enc, cot, attn_w, mlp_w, vec_t):
    any_ = pl.BlockSpec(memory_space=pl.ANY)
    smem = pl.BlockSpec(memory_space=pltpu.SMEM)
    t = lambda *s, dt=BF: jax.ShapeDtypeStruct(s, dt)
    v = pltpu.VMEM
    dma = pltpu.SemaphoreType.DMA
    return pl.pallas_call(
        forward_kernel,
        out_shape=[
            t(TOK, D), t(8, TOK, D), t(2, PADDED, D), t(2, 16, TOK, dt=F32), t(2, TOK, D, dt=F32),
            t(8, DEPTH, PLANE, 2 * ROWS, D), t(8, D, D), t(24, D, dt=F32), t(24, D, dt=F32),
        ],
        in_specs=[smem, smem] + [any_] * 6,
        out_specs=[any_] * 9,
        scratch_shapes=[
            v((UNITS, DEPTH, PLANE, 2 * ROWS, D), BF), v((DEPTH, PLANE, 2, ROWS, 128), F32), v((UNITS, 2, ROWS, HALF), F32),
            v((TOK, D), BF), v((FRAMES, D), BF), v((TOK, D), BF), v((9, TOK, D), BF), v((2, PADDED, D), BF),
            v((2, TOK, 128), F32), v((2, 16, TOK), F32), v((2, TOK, D), F32),
            v((TOK, D), BF), v((TOK, D), BF), v((TOK, D), BF), v((TOK, D), F32), v((TOK, D), F32),
            v((2, 2, D, D), BF), v((24, D), F32), v((24, D), F32),
            dma((6,)), dma((2, 4)), dma((UNITS, 10)), dma((UNITS, 10)), dma((10,)), dma((10,)), dma((12,)), dma((2, 2)),
        ],
        compiler_params=pltpu.CompilerParams(collective_id=0, has_side_effects=True, vmem_limit_bytes=63 * MIB),
        name="forward",
    )(length, frames, x, enc, cot, attn_w, mlp_w, vec_t)


beta_first = 0.9
beta_second = 0.999
adam_epsilon = 1e-08
weight_decay = 0.01
rate_attention = 0.06
rate_feedforward = 0.03
rate_vector = 0.35


def matmul(left, right):
    return jnp.dot(left, right, preferred_element_type=jnp.float32)


def inner_rows(left, right):
    return lax.dot_general(
        left, right, (((0,), (0,)), ((), ())), preferred_element_type=jnp.float32
    )


def outer_last(left, right):
    return lax.dot_general(
        left, right, (((1,), (1,)), ((), ())), preferred_element_type=jnp.float32
    )


def norm_apply(value, gain, shift):
    center = value - jnp.mean(value, -1, keepdims=True)
    spread = jnp.mean(center * center, -1, keepdims=True)
    return center * lax.rsqrt(spread + norm_epsilon) * gain + shift


def gelu_exact(value):
    return jax.nn.gelu(value, approximate=False)


def head_group():
    return 4


def grouped(value):
    width = head_group()
    return (
        value.reshape(value.shape[0], H, HD)
        .transpose(1, 0, 2)
        .reshape(H // width, width, value.shape[0], HD)
    )


def ungrouped(value):
    return value.reshape(H, value.shape[2], HD).transpose(1, 0, 2).reshape(value.shape[2], H * HD)


def attend_forward(query, keys, values, mask):

    def one_group(parts):
        q_group, k_group, v_group = parts
        scores = jnp.einsum("gtd,gsd->gts", q_group, k_group, preferred_element_type=jnp.float32)
        scores = jnp.where(mask[None], scores, -1e30)
        peak = jnp.max(scores, -1, keepdims=True)
        expo = jnp.exp(scores - peak)
        total = jnp.sum(expo, -1, keepdims=True)
        probs = (expo / total).astype(jnp.bfloat16)
        mixed = jnp.einsum("gts,gsd->gtd", probs, v_group, preferred_element_type=jnp.float32)
        return (mixed.astype(jnp.bfloat16), (peak + jnp.log(total))[..., 0])

    heads, summed = lax.map(one_group, (grouped(query), grouped(keys), grouped(values)))
    return (ungrouped(heads), summed)


def attend_backward(query, keys, values, summed, grad_out, mask):

    def one_group(parts):
        q_group, k_group, v_group, s_group, g_group = parts
        scores = jnp.einsum("gtd,gsd->gts", q_group, k_group, preferred_element_type=jnp.float32)
        probs = jnp.where(mask[None], jnp.exp(scores - s_group[..., None]), 0.0)
        grad_values = jnp.einsum(
            "gts,gtd->gsd", probs.astype(jnp.bfloat16), g_group, preferred_element_type=jnp.float32
        )
        grad_probs = jnp.einsum(
            "gtd,gsd->gts", g_group, v_group, preferred_element_type=jnp.float32
        )
        grad_scores = (
            probs * (grad_probs - jnp.sum(probs * grad_probs, -1, keepdims=True))
        ).astype(jnp.bfloat16)
        grad_query = jnp.einsum(
            "gts,gsd->gtd", grad_scores, k_group, preferred_element_type=jnp.float32
        ).astype(jnp.bfloat16)
        grad_keys = jnp.einsum(
            "gts,gtd->gsd", grad_scores, q_group, preferred_element_type=jnp.float32
        ).astype(jnp.bfloat16)
        return (grad_query, grad_keys, grad_values.astype(jnp.bfloat16))

    parts = (grouped(query), grouped(keys), grouped(values), summed, grouped(grad_out))
    grad_query, grad_keys, grad_values = lax.map(one_group, parts)
    return (ungrouped(grad_query), ungrouped(grad_keys), ungrouped(grad_values))


def make_masks(length, frames):
    place = jnp.arange(TOK)
    causal = (place[None, :] <= place[:, None]) & (place[None, :] < length)
    seen = jnp.broadcast_to(jnp.arange(FRAMES)[None, :] < frames, (TOK, FRAMES))
    return (place, causal, seen)


def clip_forward(weights, x_in, enc, length, frames):
    wa, wm, wv = weights
    vec = wv.astype(jnp.float32)
    scale = HD ** (-0.5)
    place, causal, seen = make_masks(length, frames)
    x = x_in.astype(jnp.float32)
    first = norm_apply(x, vec[0], vec[1]).astype(jnp.bfloat16)
    query = ((matmul(first, wa[0]) + vec[6]) * scale).astype(jnp.bfloat16)
    keys = matmul(first, wa[1]).astype(jnp.bfloat16)
    values = (matmul(first, wa[2]) + vec[7]).astype(jnp.bfloat16)
    mixed, summed_self = attend_forward(query, keys, values, causal)
    second_in = x + matmul(mixed, wa[3]) + vec[8]
    second = norm_apply(second_in, vec[2], vec[3]).astype(jnp.bfloat16)
    cross_query = ((matmul(second, wa[4]) + vec[9]) * scale).astype(jnp.bfloat16)
    cross_keys = matmul(enc, wa[5]).astype(jnp.bfloat16)
    cross_values = (matmul(enc, wa[6]) + vec[10]).astype(jnp.bfloat16)
    heard, summed_cross = attend_forward(cross_query, cross_keys, cross_values, seen)
    third_in = second_in + matmul(heard, wa[7]) + vec[11]
    third = norm_apply(third_in, vec[4], vec[5]).astype(jnp.bfloat16)
    hidden_pre = outer_last(third, wm[0]) + vec[13:].reshape(FF)
    hidden = gelu_exact(hidden_pre).astype(jnp.bfloat16)
    result = third_in + matmul(hidden, wm[1]) + vec[12]
    saved = (
        first,
        query,
        keys,
        values,
        mixed,
        summed_self,
        second_in,
        second,
        cross_query,
        cross_keys,
        cross_values,
        heard,
        summed_cross,
        third_in,
        third,
        hidden_pre,
        hidden,
    )
    return (result.astype(jnp.bfloat16), saved)


def clip_backward(weights, x_in, enc, length, frames, cot, saved):
    wa, wm, wv = weights
    vec = wv.astype(jnp.float32)
    scale = HD ** (-0.5)
    (
        first,
        query,
        keys,
        values,
        mixed,
        summed_self,
        second_in,
        second,
        cross_query,
        cross_keys,
        cross_values,
        heard,
        summed_cross,
        third_in,
        third,
        hidden_pre,
        hidden,
    ) = saved
    place, causal, seen = make_masks(length, frames)
    grad_y = cot.astype(jnp.float32) * (place < length).astype(jnp.float32)[:, None]
    out_three = grad_y.astype(jnp.bfloat16)
    g_down = inner_rows(hidden, out_three)
    g_b_down = jnp.sum(out_three.astype(jnp.float32), 0)
    grad_hidden = outer_last(out_three, wm[1])
    _, gelu_pull = jax.vjp(gelu_exact, hidden_pre)
    grad_pre = gelu_pull(grad_hidden)[0].astype(jnp.bfloat16)
    g_up = inner_rows(grad_pre, third)
    g_b_up = jnp.sum(grad_pre.astype(jnp.float32), 0)
    grad_third = matmul(grad_pre, wm[0])
    _, norm_pull = jax.vjp(norm_apply, third_in, vec[4], vec[5])
    part_three, g_gain_three, g_shift_three = norm_pull(grad_third)
    grad_third_in = grad_y + part_three
    out_two = grad_third_in.astype(jnp.bfloat16)
    g_cross_out = inner_rows(heard, out_two)
    g_b_cross_out = jnp.sum(out_two.astype(jnp.float32), 0)
    grad_heard = outer_last(out_two, wa[7]).astype(jnp.bfloat16)
    grad_cq, grad_ck, grad_cv = attend_backward(
        cross_query, cross_keys, cross_values, summed_cross, grad_heard, seen
    )
    grad_cq = grad_cq * scale
    g_cross_query = inner_rows(second, grad_cq)
    g_b_cross_query = jnp.sum(grad_cq.astype(jnp.float32), 0)
    g_cross_keys = inner_rows(enc, grad_ck)
    g_cross_values = inner_rows(enc, grad_cv)
    g_b_cross_values = jnp.sum(grad_cv.astype(jnp.float32), 0)
    grad_enc = outer_last(grad_ck, wa[5]) + outer_last(grad_cv, wa[6])
    grad_second = outer_last(grad_cq, wa[4])
    _, norm_pull = jax.vjp(norm_apply, second_in, vec[2], vec[3])
    part_two, g_gain_two, g_shift_two = norm_pull(grad_second)
    grad_second_in = grad_third_in + part_two
    out_one = grad_second_in.astype(jnp.bfloat16)
    g_self_out = inner_rows(mixed, out_one)
    g_b_self_out = jnp.sum(out_one.astype(jnp.float32), 0)
    grad_mixed = outer_last(out_one, wa[3]).astype(jnp.bfloat16)
    grad_q, grad_k, grad_v = attend_backward(query, keys, values, summed_self, grad_mixed, causal)
    grad_q = grad_q * scale
    g_self_query = inner_rows(first, grad_q)
    g_self_keys = inner_rows(first, grad_k)
    g_self_values = inner_rows(first, grad_v)
    g_b_self_query = jnp.sum(grad_q.astype(jnp.float32), 0)
    g_b_self_values = jnp.sum(grad_v.astype(jnp.float32), 0)
    grad_first = outer_last(grad_q, wa[0]) + outer_last(grad_k, wa[1]) + outer_last(grad_v, wa[2])
    _, norm_pull = jax.vjp(norm_apply, x_in.astype(jnp.float32), vec[0], vec[1])
    part_one, g_gain_one, g_shift_one = norm_pull(grad_first)
    grad_x = grad_second_in + part_one
    g_attn = jnp.stack(
        [
            g_self_query,
            g_self_keys,
            g_self_values,
            g_self_out,
            g_cross_query,
            g_cross_keys,
            g_cross_values,
            g_cross_out,
        ]
    )
    g_mlp = jnp.stack([g_up, g_down])
    g_vec = jnp.concatenate(
        [
            jnp.stack(
                [
                    g_gain_one,
                    g_shift_one,
                    g_gain_two,
                    g_shift_two,
                    g_gain_three,
                    g_shift_three,
                    g_b_self_query,
                    g_b_self_values,
                    g_b_self_out,
                    g_b_cross_query,
                    g_b_cross_values,
                    g_b_cross_out,
                    g_b_down,
                ]
            ),
            g_b_up.reshape(FF // D, D),
        ],
        0,
    )
    return ((g_attn, g_mlp, g_vec), grad_x, grad_enc)


def adam_update(weight, first, second, grad, rate):
    first_new = beta_first * first + (1.0 - beta_first) * grad
    second_new = beta_second * second + (1.0 - beta_second) * grad * grad
    ratio = (
        first_new
        / (1.0 - beta_first**STEP)
        / (jnp.sqrt(second_new / (1.0 - beta_second**STEP)) + adam_epsilon)
    )
    return (weight - rate * (ratio + weight_decay * weight), first_new, second_new)


def plain_body(
    tokens,
    enc_states,
    cotangent,
    tok_len,
    frame_count,
    attn_w,
    attn_m,
    attn_v,
    mlp_w,
    mlp_m,
    mlp_v,
    vec_w,
    vec_m,
    vec_v,
):
    shards = (attn_w.astype(jnp.bfloat16), mlp_w.astype(jnp.bfloat16), vec_w.astype(jnp.bfloat16))
    weights = (
        lax.all_gather(shards[0], ("dp", "fsdp"), axis=1, tiled=True),
        lax.all_gather(shards[1], ("dp", "fsdp"), axis=1, tiled=True),
        lax.all_gather(shards[2], ("dp", "fsdp"), axis=1, tiled=True),
    )

    def forward_one(items):
        x_in, enc, length, frames = items
        return clip_forward(weights, x_in, enc, length, frames)

    result, saved = lax.map(forward_one, (tokens, enc_states, tok_len, frame_count))
    back_weights = (
        lax.all_gather(shards[0], ("dp", "fsdp"), axis=1, tiled=True),
        lax.all_gather(shards[1], ("dp", "fsdp"), axis=1, tiled=True),
        lax.all_gather(shards[2], ("dp", "fsdp"), axis=1, tiled=True),
    )

    def backward_one(carry, items):
        x_in, enc, length, frames, cot, kept = items
        grads, grad_x, grad_enc = clip_backward(back_weights, x_in, enc, length, frames, cot, kept)
        return (jax.tree.map(jnp.add, carry, grads), (grad_x, grad_enc))

    zeros = (
        jnp.zeros(weights[0].shape, jnp.float32),
        jnp.zeros(weights[1].shape, jnp.float32),
        jnp.zeros(weights[2].shape, jnp.float32),
    )
    totals, (d_tokens, d_enc) = lax.scan(
        backward_one, zeros, (tokens, enc_states, tok_len, frame_count, cotangent, saved)
    )
    grad_attn, grad_mlp, grad_vec = (
        lax.psum_scatter(totals[0], ("dp", "fsdp"), scatter_dimension=1, tiled=True),
        lax.psum_scatter(totals[1], ("dp", "fsdp"), scatter_dimension=1, tiled=True),
        lax.psum_scatter(totals[2], ("dp", "fsdp"), scatter_dimension=1, tiled=True),
    )
    attn_new = adam_update(attn_w, attn_m, attn_v, grad_attn, rate_attention)
    mlp_new = adam_update(mlp_w, mlp_m, mlp_v, grad_mlp, rate_feedforward)
    vec_new = adam_update(vec_w, vec_m, vec_v, grad_vec, rate_vector)
    return (
        result,
        d_tokens,
        d_enc,
        attn_new[0],
        attn_new[1],
        attn_new[2],
        mlp_new[0],
        mlp_new[1],
        mlp_new[2],
        vec_new[0],
        vec_new[1],
        vec_new[2],
    )


def attention_backward(x, enc, length, frames, weights, act, kv, lse, xs, vec, gv):
    scale = HD ** (-0.5)
    place, causal, seen = make_masks(length, frames)
    sums = lse[:, :H].reshape(2, H // head_group(), head_group(), TOK)
    first, query, keys, values, mixed, second, cross_query, heard = [act[i] for i in range(8)]
    dx = xs[1]
    out_two = dx.astype(BF)
    g_co = inner_rows(heard, out_two)
    b_co = colsum(out_two)[0]
    gh = outer_last(out_two, weights[7]).astype(BF)
    gcq, gck, gcv = attend_backward(cross_query, kv[0, :FRAMES], kv[1, :FRAMES], sums[1], gh, seen)
    gcq = gcq * scale
    g_enc = outer_last(gck, weights[5]) + outer_last(gcv, weights[6])
    _, pull = jax.vjp(norm_apply, xs[0], vec[2], vec[3])
    part, g2, b2 = pull(outer_last(gcq, weights[4]))
    dx = dx + part
    out_one = dx.astype(BF)
    gm = outer_last(out_one, weights[3]).astype(BF)
    gq, gk, gvv = attend_backward(query, keys, values, sums[0], gm, causal)
    gq = gq * scale
    _, pull = jax.vjp(norm_apply, x.astype(F32), vec[0], vec[1])
    part, g1, b1 = pull(outer_last(gq, weights[0]) + outer_last(gk, weights[1]) + outer_last(gvv, weights[2]))
    g_attn = [
        inner_rows(first, gq), inner_rows(first, gk), inner_rows(first, gvv), inner_rows(mixed, out_one),
        inner_rows(second, gcq), inner_rows(enc, gck), inner_rows(enc, gcv), g_co,
    ]
    up = gv[13:17].reshape(4, 16, 2, ROWS).transpose(1, 2, 0, 3).reshape(4, D)
    rows = [g1, b1, g2, b2, gv[4], gv[5], colsum(gq)[0], colsum(gvv)[0], colsum(out_one)[0], colsum(gcq)[0],
            colsum(gcv)[0], b_co, gv[12]]
    return jnp.stack(g_attn), jnp.concatenate([jnp.stack(rows), up], 0), dx + part, g_enc


def fused_body(tokens, enc_states, cotangent, tok_len, frame_count, attn_w, attn_m, attn_v, mlp_w, mlp_m, mlp_v, vec_w, vec_m, vec_v):
    vec_t = jnp.pad(vec_w.T, ((0, 0), (0, 128 - vec_w.shape[0])))
    out, act, kv, lse, xs, wattn, gffn, vec, gv = call_forward(
        tok_len, frame_count, tokens[0], enc_states[0], cotangent[0], attn_w, mlp_w.reshape(8, ROWS, D), vec_t
    )
    g_attn, g_vec, d_tokens, d_enc = attention_backward(
        tokens[0], enc_states[0], tok_len[0], frame_count[0], wattn.reshape(8, D, D), act, kv, lse, xs, vec, gv
    )
    g_mlp = gffn.reshape(2, 4, 16, 2, ROWS, D).transpose(0, 2, 3, 1, 4, 5).reshape(2, FF, D)
    scatter = lambda g: lax.psum_scatter(g, ("dp", "fsdp"), scatter_dimension=1, tiled=True)
    grad_attn = scatter(g_attn.astype(BF)).astype(F32)
    grad_mlp = scatter(g_mlp).astype(F32)
    grad_vec = scatter(g_vec)
    attn_new = adam_update(attn_w, attn_m, attn_v, grad_attn, rate_attention)
    mlp_new = adam_update(mlp_w, mlp_m, mlp_v, grad_mlp, rate_feedforward)
    vec_new = adam_update(vec_w, vec_m, vec_v, grad_vec, rate_vector)
    return (out[None], d_tokens[None], d_enc[None], *attn_new, *mlp_new, *vec_new)


def solution(mesh):
    fused = mesh.shape["dp"] == DEPTH and mesh.shape["fsdp"] == 2 * PLANE
    return jax.shard_map(
        fused_body if fused else plain_body,
        mesh=mesh,
        in_specs=(
            P(("dp", "fsdp"), None, None),
            P(("dp", "fsdp"), None, None),
            P(("dp", "fsdp"), None, None),
            P(("dp", "fsdp")),
            P(("dp", "fsdp")),
            P(None, ("dp", "fsdp"), None),
            P(None, ("dp", "fsdp"), None),
            P(None, ("dp", "fsdp"), None),
            P(None, ("dp", "fsdp"), None),
            P(None, ("dp", "fsdp"), None),
            P(None, ("dp", "fsdp"), None),
            P(None, ("dp", "fsdp")),
            P(None, ("dp", "fsdp")),
            P(None, ("dp", "fsdp")),
        ),
        out_specs=(
            P(("dp", "fsdp"), None, None),
            P(("dp", "fsdp"), None, None),
            P(("dp", "fsdp"), None, None),
            P(None, ("dp", "fsdp"), None),
            P(None, ("dp", "fsdp"), None),
            P(None, ("dp", "fsdp"), None),
            P(None, ("dp", "fsdp"), None),
            P(None, ("dp", "fsdp"), None),
            P(None, ("dp", "fsdp"), None),
            P(None, ("dp", "fsdp")),
            P(None, ("dp", "fsdp")),
            P(None, ("dp", "fsdp")),
        ),
        check_vma=False,
    )
```

```python
import functools
import jax
import jax.numpy as jnp
from jax import lax
from jax.experimental import pallas as pl
from jax.experimental.pallas import tpu as pltpu
from jax.sharding import PartitionSpec as P

D = 768
H = 12
HD = 64
FF = 3072
FRAMES = 1500
TOK = 448
STEP = 10
PADDED = 1536
ROWS = 24
PLANE = 4
DEPTH = 4
UNITS = 16
HALF = D // 2
BF = jnp.bfloat16
F32 = jnp.float32
MESH = pl.DeviceIdType.MESH
norm_epsilon = 1e-05
MIB = 2**20


def dot(a, b):
    return lax.dot_general(a, b, (((1,), (0,)), ((), ())), preferred_element_type=F32)


def dot_nt(a, b):
    return lax.dot_general(a, b, (((1,), (1,)), ((), ())), preferred_element_type=F32)


def dot_tn(a, b):
    return lax.dot_general(a, b, (((0,), (0,)), ((), ())), preferred_element_type=F32)


def layer_norm(v, gain, shift):
    c = v - jnp.mean(v, -1, keepdims=True)
    s = jnp.mean(c * c, -1, keepdims=True)
    return c * lax.rsqrt(s + norm_epsilon) * gain + shift


def layer_norm_back(v, gain, grad):
    c = v - jnp.mean(v, -1, keepdims=True)
    r = lax.rsqrt(jnp.mean(c * c, -1, keepdims=True) + norm_epsilon)
    xh = c * r
    t = grad * gain
    dx = r * (t - jnp.mean(t, -1, keepdims=True) - xh * jnp.mean(t * xh, -1, keepdims=True))
    return dx, jnp.sum(grad * xh, 0, keepdims=True), jnp.sum(grad, 0, keepdims=True)


def gelu_both(u):
    z = jnp.abs(u) * 0.7071067811865476
    e = jnp.exp(-0.5 * u * u)
    t = 1.0 / (1.0 + 0.3275911 * z)
    poly = t * (0.254829592 + t * (-0.284496736 + t * (1.421413741 + t * (-1.453152027 + t * 1.061405429))))
    half = 0.5 * poly * e
    phi = jnp.where(u >= 0, 1.0 - half, half)
    return u * phi, phi + u * (e * 0.3989422804014327)


def colsum(v):
    return jnp.sum(v.astype(F32), 0, keepdims=True)


def head_lanes(rows, h):
    return (lax.broadcasted_iota(jnp.int32, (rows, 128), 1) // HD) == h


class Place:
    def __init__(self):
        self.z = lax.axis_index("dp")
        f = lax.axis_index("fsdp")
        self.f = f
        self.c = f % 2
        self.p = f // 2
        x, y = self.p % 2, self.p // 2
        self.part = f + 1 - 2 * self.c
        fx, fy = f + 2 - 4 * x, f + 4 - 8 * y
        px, py = self.p + 1 - 2 * x, self.p + 2 - 4 * y
        c = self.c
        self.n1, self.n2 = fx + c * (fy - fx), fy + c * (fx - fy)
        self.p1, self.p2, self.p3 = px + c * (py - px), py + c * (px - py), 3 - self.p
        self.zto = [(self.z + d) % DEPTH for d in range(1, DEPTH)]
        self.zfrom = [(self.z + DEPTH - d) % DEPTH for d in range(1, DEPTH)]
        self.own = pl.ds(pl.multiple_of(c * HALF, 128), HALF)
        self.other = pl.ds(pl.multiple_of(HALF - c * HALF, 128), HALF)

    def greet(self):
        barrier = pltpu.get_barrier_semaphore()
        others = [(zz, self.f) for zz in self.zto]
        others += [(self.z, self.n1), (self.z, self.n2), (self.z, self.part)]
        for device in others:
            pl.semaphore_signal(barrier, inc=1, device_id=device, device_id_type=MESH)
        pl.semaphore_wait(barrier, len(others))


def remote(src, dst, send, recv, device):
    return pltpu.make_async_remote_copy(
        src_ref=src, dst_ref=dst, send_sem=send, recv_sem=recv, device_id=device, device_id_type=MESH
    )


class Gather:
    def __init__(self, place, view, send, recv):
        self.w, self.view, self.send, self.recv = place, view, send, recv

    def copy(self, k, ref, device):
        return remote(ref, ref, self.send(k), self.recv(k), device)

    def own(self, zz, p):
        return self.view(zz, p, True)

    def s1(self):
        w = self.w
        for i, zz in enumerate(w.zto):
            self.copy(i, self.own(w.z, w.p), (zz, w.f)).start()

    def s2(self):
        w = self.w
        for i, zz in enumerate(w.zfrom):
            self.copy(i, self.own(zz, w.p), (zz, w.f)).wait_recv()
        self.copy(3, self.own(None, w.p), (w.z, w.n1)).start()
        self.copy(4, self.own(None, w.p), (w.z, w.n2)).start()
        self.copy(6, self.own(None, w.p), (w.z, w.part)).start()

    def s3(self):
        w = self.w
        self.copy(3, self.own(None, w.p1), (w.z, w.n1)).wait_recv()
        self.copy(5, self.own(None, w.p1), (w.z, w.n2)).start()
        self.copy(7, self.own(None, w.p1), (w.z, w.part)).start()

    def s4(self):
        w = self.w
        self.copy(4, self.own(None, w.p2), (w.z, w.n2)).wait_recv()
        self.copy(8, self.own(None, w.p2), (w.z, w.part)).start()

    def s5(self):
        w = self.w
        self.copy(5, self.own(None, w.p3), (w.z, w.n2)).wait_recv()
        self.copy(9, self.own(None, w.p3), (w.z, w.part)).start()

    def ready(self):
        w = self.w
        for k, p in enumerate((w.p, w.p1, w.p2, w.p3)):
            self.copy(6 + k, self.view(None, p, False), (w.z, w.part)).wait_recv()

    def drain(self):
        w = self.w
        for i, zz in enumerate(w.zto):
            self.copy(i, self.own(w.z, w.p), (zz, w.f)).wait_send()
        for k, p in ((3, w.p), (4, w.p), (5, w.p1), (6, w.p), (7, w.p1), (8, w.p2), (9, w.p3)):
            self.copy(k, self.own(None, p), (w.z, w.n1)).wait_send()


def heads_forward(q_ref, k_ref, v_ref, o_ref, lse_ref, mask_fn, keys, tile, first, count):
    def pair(hp):
        lanes = pl.ds(pl.multiple_of(hp * 128, 128), 128)
        kp, vp = k_ref[:keys, lanes], v_ref[:keys, lanes]
        for i in range(TOK // tile):
            rows = pl.ds(i * tile, tile)
            qp = q_ref[rows, lanes]
            outs = []
            for h in range(2):
                s = dot_nt(jnp.where(head_lanes(tile, h), qp, jnp.zeros_like(qp)), kp)
                s = mask_fn(s, i)
                peak = jnp.max(s, -1, keepdims=True)
                expo = jnp.exp(s - peak)
                total = jnp.sum(expo, -1, keepdims=True)
                outs.append(dot(expo.astype(BF), vp) * (1.0 / total))
                lane = lax.broadcasted_iota(jnp.int32, (tile, 128), 1)
                lse_ref[rows, :] = jnp.where(lane == hp * 2 + h, peak + jnp.log(total), lse_ref[rows, :])
            o_ref[rows, lanes] = jnp.where(head_lanes(tile, 0), outs[0], outs[1]).astype(BF)

    def step(i, _):
        pair(first + i)
        return 0

    lax.fori_loop(0, count, step, 0)


def thirds(f):
    def step(j, _):
        f(pl.ds(pl.multiple_of(j * 256, 256), 256))
        return 0

    lax.fori_loop(0, 3, step, 0)


ORDER = [5, 6, 0, 1, 2, 3, 4, 7, 8, 12, 9, 13, 10, 14, 11, 15]
A1, Q, K, V_, O, A2, CQ, O2 = range(8)


def forward_kernel(
    len_ref, frames_ref, x_hbm, enc_hbm, cot_hbm, attn_hbm, mlp_hbm, vec_hbm,
    out_hbm, act_hbm, kv_hbm, lse_hbm, xs_hbm, wattn_hbm, gffn_hbm, vec_out, gv_out,
    weights, vgather, stage, x_ref, enc, cot, act, kv, lse_cols, lse_rows, xs, hm, gp, du, oacc, dacc, grads, vec, gv,
    load_sem, stage_sem, send_sem, recv_sem, vsend_sem, vrecv_sem, store_sem, gsem,
    *, comm=True,
):
    w = Place()
    length, frames = len_ref[0], frames_ref[0]
    local = lambda src, dst, sem: pltpu.make_async_copy(src, dst, sem)
    loads = [
        local(attn_hbm.at[:, :, w.own], stage.at[pl.ds(0, 8), w.c], load_sem.at[0]),
        local(mlp_hbm.at[:, :, w.own], stage.at[pl.ds(8, 8), w.c], load_sem.at[1]),
        local(vec_hbm, vgather.at[w.z, w.p, w.c], load_sem.at[2]),
        local(x_hbm, x_ref, load_sem.at[3]),
        local(enc_hbm, enc, load_sem.at[4]),
        local(cot_hbm, cot, load_sem.at[5]),
    ]
    for i in (2, 0, 1, 3, 4, 5):
        loads[i].start()
    w.greet()

    def unit_view(u):
        def view(zz, p, own):
            return weights.at[u, slice(None) if zz is None else zz, p, :, w.own if own else w.other]
        return view

    def vec_view(zz, p, own):
        return vgather.at[slice(None) if zz is None else zz, p, w.c if own else 1 - w.c]

    units = [Gather(w, unit_view(u), lambda k, u=u: send_sem.at[u, k], lambda k, u=u: recv_sem.at[u, k]) for u in ORDER]
    vecs = Gather(w, vec_view, lambda k: vsend_sem.at[k], lambda k: vrecv_sem.at[k])

    loads[2].wait()
    vecs.s1()
    parts = ((5, 2, attn_hbm, 5), (0, 5, attn_hbm, 0), (7, 1, attn_hbm, 7), (8, 8, mlp_hbm, 0))
    swaps = []
    for i, (u0, n, src, at) in enumerate(parts):
        src = src.at[pl.ds(at, n), :, w.other]
        swaps.append(remote(src, stage.at[pl.ds(u0, n), w.c], stage_sem.at[0, i], stage_sem.at[1, i], (w.z, w.part)))
        swaps[i].start()
    loads[0].wait()
    loads[1].wait()

    def cast(u):
        weights[u, w.z, w.p, :, w.own] = stage[u].reshape(2 * ROWS, HALF).astype(BF)

    for i, (u0, n, _, _) in enumerate(parts):
        swaps[i].wait_recv()
        for u in range(u0, u0 + n):
            cast(u)
        if i == 0:
            units[0].s1()
            units[1].s1()
            vecs.s2()
        if i == 1:
            units[2].s1()

    def tick(t):
        if t < UNITS:
            units[t].s2()
        if t + 3 < UNITS:
            units[t + 3].s1()
        if t >= 2 and t - 2 < UNITS:
            units[t - 2].s5()
        if t >= 1 and t - 1 < UNITS:
            units[t - 1].s3()
            units[t - 1].s4()

    stores = []

    def store(src, dst):
        c = local(src, dst, store_sem.at[len(stores)])
        c.start()
        stores.append(c)

    flat = weights
    def wcols(u, cols):
        return weights[u, :, :, :, cols].reshape(D, cols.size)

    vrow = lambda r, cols=slice(None): vec[r : r + 1, cols]

    lse_cols[...] = jnp.zeros_like(lse_cols)
    kv[:, FRAMES // 16 * 16 :, :] = jnp.zeros((2, PADDED - FRAMES // 16 * 16, D), BF)
    tick(0)
    vecs.s3()
    vecs.s4()
    vecs.s5()
    vecs.ready()
    tick(1)
    table = vgather[...].reshape(D, 128).astype(BF).astype(F32)
    vec[...] = jnp.transpose(table)[:24, :]
    lane = lax.broadcasted_iota(jnp.int32, (ROWS, 128), 1)
    blocks = []
    for chip in range(16):
        for core in range(2):
            acc = jnp.zeros((ROWS, 128), F32)
            for j in range(4):
                blk = table[(chip % 4) * 192 + core * 96 + j * ROWS :][:ROWS]
                col = jnp.sum(jnp.where(lane == 13 + chip // 4, blk, 0.0), -1, keepdims=True)
                acc = jnp.where(lane == j, col, acc)
            blocks.append(acc)
    vec[16:24, :] = jnp.transpose(jnp.concatenate(blocks, 0))[:8, :]
    loads[3].wait()
    act[A1] = layer_norm(x_ref[...].astype(F32), vrow(0), vrow(1)).astype(BF)
    tick(2)
    loads[4].wait()

    def enc_project(u, which, bias):
        for r0, r1 in ((0, 512), (512, 1024), (1024, FRAMES)):
            e = enc[r0:r1, :]

            def cols(cs):
                r = dot(e, wcols(u, cs))
                if bias is not None:
                    r = r + vrow(bias, cs)
                kv[which, r0:r1, cs] = r.astype(BF)

            thirds(cols)

    units[0].ready()
    enc_project(5, 0, None)
    tick(3)
    units[1].ready()
    enc_project(6, 1, 10)
    tick(4)

    def project(src, u, dst, bias, scale):
        def cols(cs):
            r = dot(act[src], wcols(u, cs))
            if bias is not None:
                r = r + vrow(bias, cs)
            act[dst, :, cs] = (r * scale).astype(BF)

        thirds(cols)

    units[2].ready()
    project(A1, 0, Q, 6, 0.125)
    tick(5)
    units[3].ready()
    project(A1, 1, K, None, 1.0)
    tick(6)
    units[4].ready()
    project(A1, 2, V_, 7, 1.0)

    def self_mask(s, i):
        r = lax.broadcasted_iota(jnp.int32, s.shape, 0) + i * s.shape[0]
        c = lax.broadcasted_iota(jnp.int32, s.shape, 1)
        return jnp.where((c <= r) & (c < length), s, -1e30)

    def cross_mask(s, i):
        c = lax.broadcasted_iota(jnp.int32, (1, PADDED - 640), 1) + 640
        return jnp.concatenate([s[:, :640], jnp.where(c < frames, s[:, 640:], -1e30)], axis=1)

    heads_forward(act.at[Q], act.at[K], act.at[V_], act.at[O], lse_cols.at[0], self_mask, TOK, 448, 0, 3)
    tick(7)
    heads_forward(act.at[Q], act.at[K], act.at[V_], act.at[O], lse_cols.at[0], self_mask, TOK, 448, 3, 3)
    units[5].ready()

    def residual(src, base, u, dst, bias):
        def cols(cs):
            xs[dst, :, cs] = base(cs) + dot(act[src], wcols(u, cs)) + vrow(bias, cs)

        thirds(cols)

    residual(O, lambda cs: x_ref[:, cs].astype(F32), 3, 0, 8)
    act[A2] = layer_norm(xs[0], vrow(2), vrow(3)).astype(BF)
    tick(8)
    units[6].ready()
    project(A2, 4, CQ, 9, 0.125)
    for i in range(3):
        heads_forward(act.at[CQ], kv.at[0], kv.at[1], act.at[O2], lse_cols.at[1], cross_mask, PADDED, 224, 2 * i, 2)
        tick(9 + i)
    units[7].ready()
    residual(O2, lambda cs: xs[0, :, cs], 7, 1, 11)
    a3 = layer_norm(xs[1], vrow(4), vrow(5)).astype(BF)
    act[8] = a3
    store(act.at[pl.ds(0, 8)], act_hbm)
    store(kv, kv_hbm)
    store(weights.at[pl.ds(0, 8)], wattn_hbm)
    for i in range(2):
        lse_rows[i] = jnp.transpose(lse_cols[i])[:16, :]
    store(lse_rows, lse_hbm)
    store(xs.at[0], xs_hbm.at[0])
    loads[5].wait()
    ok = lax.broadcasted_iota(jnp.int32, (TOK, 1), 0) < length
    cot[...] = jnp.where(ok, cot[...], jnp.zeros((TOK, D), BF))
    gv[...] = jnp.zeros_like(gv)
    gv[12:13, :] = colsum(cot[...])
    oacc[...] = jnp.zeros_like(oacc)
    dacc[...] = jnp.zeros_like(dacc)

    rows3 = lambda u, rs: weights.at[u].reshape(D, D)[rs, :]

    gcopies = {}
    for j in range(4):
        units[8 + 2 * j].ready()
        units[9 + 2 * j].ready()
        if j >= 2:
            gcopies[(0, j - 2)].wait()
            gcopies[(1, j - 2)].wait()

        def part(t, _):
            rs = pl.ds(pl.multiple_of(t * 256, 256), 256)
            u = dot_nt(act[8], rows3(8 + j, rs)) + vec[16 + j : 17 + j, rs]
            g, d = gelu_both(u)
            hm[:, rs] = g.astype(BF)
            gp[:, rs] = d.astype(BF)
            return 0

        lax.fori_loop(0, 3, part, 0)

        def part2(t, _):
            rs = pl.ds(pl.multiple_of(t * 256, 256), 256)
            oacc[:, rs] += dot(hm[...], wcols(12 + j, rs))
            d = (dot_nt(cot[...], rows3(12 + j, rs)) * gp[:, rs].astype(F32)).astype(BF)
            du[:, rs] = d
            gv[13 + j : 14 + j, rs] = colsum(d)
            return 0

        lax.fori_loop(0, 3, part2, 0)
        if j < 3:
            tick(12 + 2 * j)

        def part3(t, _):
            rs = pl.ds(pl.multiple_of(t * 256, 256), 256)
            grads[j % 2, 1, rs, :] = dot_tn(hm[:, rs], cot[...]).astype(BF)
            grads[j % 2, 0, rs, :] = dot_tn(du[:, rs], act[8]).astype(BF)
            dacc[:, rs] += dot(du[...], wcols(8 + j, rs))
            return 0

        lax.fori_loop(0, 3, part3, 0)
        for k in range(2):
            cp = local(grads.at[j % 2, k], gffn_hbm.at[4 * k + j], gsem.at[j % 2, k])
            cp.start()
            gcopies[(k, j)] = cp
        if j < 3:
            tick(13 + 2 * j)
    act[8] = (xs[1] + oacc[...] + vrow(12)).astype(BF)
    store(act.at[8], out_hbm)
    dx, gg, gb = layer_norm_back(xs[1], vrow(4), dacc[...])
    gv[4:5, :] = gg
    gv[5:6, :] = gb
    oacc[...] = cot[...].astype(F32) + dx
    store(oacc, xs_hbm.at[1])
    store(vec, vec_out)
    store(gv, gv_out)
    for j in (2, 3):
        gcopies[(0, j)].wait()
        gcopies[(1, j)].wait()
    for s in swaps:
        s.wait_send()
    vecs.drain()
    for u in units:
        u.drain()
    for c in stores:
        c.wait()


def call_forward(length, frames, x, enc, cot, attn_w, mlp_w, vec_t):
    any_ = pl.BlockSpec(memory_space=pl.ANY)
    smem = pl.BlockSpec(memory_space=pltpu.SMEM)
    t = lambda *s, dt=BF: jax.ShapeDtypeStruct(s, dt)
    v = pltpu.VMEM
    dma = pltpu.SemaphoreType.DMA
    return pl.pallas_call(
        forward_kernel,
        out_shape=[
            t(TOK, D), t(8, TOK, D), t(2, PADDED, D), t(2, 16, TOK, dt=F32), t(2, TOK, D, dt=F32),
            t(8, DEPTH, PLANE, 2 * ROWS, D), t(8, D, D), t(24, D, dt=F32), t(24, D, dt=F32),
        ],
        in_specs=[smem, smem] + [any_] * 6,
        out_specs=[any_] * 9,
        scratch_shapes=[
            v((UNITS, DEPTH, PLANE, 2 * ROWS, D), BF), v((DEPTH, PLANE, 2, ROWS, 128), F32), v((UNITS, 2, ROWS, HALF), F32),
            v((TOK, D), BF), v((FRAMES, D), BF), v((TOK, D), BF), v((9, TOK, D), BF), v((2, PADDED, D), BF),
            v((2, TOK, 128), F32), v((2, 16, TOK), F32), v((2, TOK, D), F32),
            v((TOK, D), BF), v((TOK, D), BF), v((TOK, D), BF), v((TOK, D), F32), v((TOK, D), F32),
            v((2, 2, D, D), BF), v((24, D), F32), v((24, D), F32),
            dma((6,)), dma((2, 4)), dma((UNITS, 10)), dma((UNITS, 10)), dma((10,)), dma((10,)), dma((12,)), dma((2, 2)),
        ],
        compiler_params=pltpu.CompilerParams(collective_id=0, has_side_effects=True, vmem_limit_bytes=63 * MIB),
        name="forward",
    )(length, frames, x, enc, cot, attn_w, mlp_w, vec_t)


class Reduce:
    def __init__(self, place, local, r0, r1, r2, r3, send, recv, source, low, finish):
        self.w, self.local, self.r0, self.r1, self.r2, self.r3 = place, local, r0, r1, r2, r3
        self.send, self.recv, self.source, self.low, self.finish = send, recv, source, low, finish

    def copy(self, k, src, dst, device):
        return remote(src, dst, self.send(k), self.recv(k), device)

    def copies(self, stage):
        w, r0 = self.w, self.r0
        if stage == 0:
            return [self.copy(0, self.source, r0, (w.z, w.part))]
        if stage == 1:
            return [
                self.copy(1, r0.at[:, w.p2], self.r1.at[:, 0], (w.z, w.n2)),
                self.copy(2, r0.at[:, w.p3], self.r1.at[:, 1], (w.z, w.n2)),
            ]
        if stage == 2:
            return [self.copy(3, r0.at[:, w.p1], self.r2, (w.z, w.n1))]
        return [self.copy(4 + i, r0.at[zz, w.p], self.r3.at[i], (zz, w.f)) for i, zz in enumerate(w.zto)]

    def e0(self):
        for c in self.copies(0):
            c.start()

    def arrived(self, stage):
        for c in self.copies(stage):
            c.wait_recv()

    def e1(self):
        w = self.w
        self.arrived(0)
        for p in (w.p2, w.p3):
            self.r0[:, p] = (self.local(slice(None), p) + self.r0[:, p].astype(F32)).astype(self.low)
        for c in self.copies(1):
            c.start()

    def e2(self):
        w = self.w
        self.arrived(1)
        total = self.local(slice(None), w.p1) + self.r0[:, w.p1].astype(F32) + self.r1[:, 1].astype(F32)
        self.r0[:, w.p1] = total.astype(self.low)
        for c in self.copies(2):
            c.start()

    def partial(self, zz):
        w = self.w
        return (
            self.local(zz, w.p) + self.r0[zz, w.p].astype(F32) + self.r1[zz, 0].astype(F32) + self.r2[zz].astype(F32)
        )

    def e3(self, keep):
        w = self.w
        self.arrived(2)
        keep[...] = self.partial(w.z)
        for zz in w.zto:
            self.r0[zz, w.p] = self.partial(zz).astype(self.low)
        for c in self.copies(3):
            c.start()

    def e4(self, keep):
        self.arrived(3)
        self.finish(keep[...] + (self.r3[0].astype(F32) + self.r3[1].astype(F32) + self.r3[2].astype(F32)))

    def sent(self):
        for stage in range(4):
            for c in self.copies(stage):
                c.wait_send()


def head_delta(grad, mixed):
    product = grad.astype(F32) * mixed.astype(F32)
    high = product.astype(BF)
    low = (product - high.astype(F32)).astype(BF)
    pick = lax.broadcasted_iota(jnp.int32, (16, D), 1) // HD == lax.broadcasted_iota(jnp.int32, (16, D), 0)
    pick = pick.astype(F32).astype(BF)
    return dot_nt(pick, high) + dot_nt(pick, low)


def heads_backward(q_ref, k_ref, v_ref, g_ref, lse_ref, delta_ref, dq_ref, dk_ref, dv_ref, mask_fn, keys, tile, acc, first, count):
    def pair(hp):
        lanes = pl.ds(pl.multiple_of(hp * 128, 128), 128)
        qp, gp = q_ref[:, lanes], g_ref[:, lanes]
        zero = jnp.zeros_like(qp)
        qs = [jnp.where(head_lanes(TOK, h), qp, zero) for h in range(2)]
        gs = [jnp.where(head_lanes(TOK, h), gp, zero) for h in range(2)]
        lse = [lse_ref[pl.ds(hp * 2 + h, 1), :] for h in range(2)]
        delta = [delta_ref[pl.ds(hp * 2 + h, 1), :] for h in range(2)]
        for i in range(keys // tile):
            rows = pl.ds(i * tile, tile)
            kp, vp = k_ref[rows, lanes], v_ref[rows, lanes]
            dv, dk, dq = 0.0, 0.0, []
            for h in range(2):
                p = jnp.exp(mask_fn(dot_nt(kp, qs[h]), i) - lse[h])
                ds = (p * (dot_nt(vp, gs[h]) - delta[h])).astype(BF)
                dv = dv + dot(p.astype(BF), gs[h])
                dk = dk + dot(ds, qs[h])
                dq.append(dot_tn(ds, kp))
            dv_ref[rows, lanes] = dv.astype(BF)
            dk_ref[rows, lanes] = dk.astype(BF)
            a = jnp.where(head_lanes(TOK, 0), dq[0], dq[1])
            if i == 0:
                acc[...] = a
            else:
                acc[...] += a
        dq_ref[:, lanes] = (acc[...].astype(BF).astype(F32) * 0.125).astype(BF)

    def step(i, _):
        pair(first + i)
        return 0

    lax.fori_loop(0, count, step, 0)


SLOTS = 10
FINAL = [8, 9, 10, 11, 12, 13, 14, 15, 7, 4, 5, 6, 3, 0, 1, 2]


def backward_kernel(
    len_ref, frames_ref, x_hbm, enc_hbm, act_hbm, kv_hbm, lse_hbm, xs_hbm, wattn_hbm, gffn_hbm, vec_hbm, gv_hbm,
    dtok_hbm, denc_hbm, gsum_hbm, gvsum_hbm,
    grads, r0, r1, r2, r3, keep, gsum, vgrads, vr0, vr1, vr2, vr3, vkeep,
    kv, dkv, enc, act, work, x2, dx, dacc, acc, denc, wbuf, vec, gv, lse, delta,
    load_sem, send_sem, recv_sem, credit, store_sem,
):
    w = Place()
    length, frames = len_ref[0], frames_ref[0]
    loads = {}

    def load(name, src, dst):
        c = pltpu.make_async_copy(src, dst, load_sem.at[len(loads)])
        c.start()
        loads[name] = c

    def need(*names):
        for n in names:
            loads[n].wait()

    load("dx", xs_hbm.at[1], dx)
    load("o2", act_hbm.at[O2], act.at[0])
    load("wco", wattn_hbm.at[7], wbuf.at[0])
    load("g0", gffn_hbm.at[0], grads.at[0])
    load("cq", act_hbm.at[CQ], act.at[1])
    load("kv", kv_hbm, kv)
    load("lse", lse_hbm, lse)
    for u in range(1, 8):
        load("g%d" % u, gffn_hbm.at[u], grads.at[u])
    load("vec", vec_hbm, vec)
    load("gv", gv_hbm, gv)
    load("x2", xs_hbm.at[0], x2)
    load("wcq", wattn_hbm.at[4], wbuf.at[1])
    load("wck", wattn_hbm.at[5], wbuf.at[2])
    load("wcv", wattn_hbm.at[6], wbuf.at[3])
    load("enc", enc_hbm, enc)
    w.greet()

    units = []
    for u in range(UNITS):
        s = u % SLOTS

        def local(zz, p, s=s):
            return grads[s, zz, p, :, w.own].astype(F32)

        def finish(total, u=u):
            keep[u] = total.reshape(2, ROWS, HALF)
            gsum[FINAL[u], :, w.own] = keep[u, w.c]
            swap(u).start()

        src = gffn_hbm.at[u, :, :, :, w.other] if u < 8 else grads.at[s, :, :, :, w.other]
        units.append(
            Reduce(
                w, local, r0.at[s], r1.at[u], r2.at[u], r3.at[u],
                lambda k, u=u: send_sem.at[u, k], lambda k, u=u: recv_sem.at[u, k], src, BF, finish,
            )
        )

    def swap(u):
        k = FINAL[u]
        return remote(
            keep.at[u, 1 - w.c], gsum.at[k, :, w.own], send_sem.at[u, 7], recv_sem.at[u, 7], (w.z, w.part)
        )

    def swapped(u):
        ref = gsum.at[FINAL[u], :, w.other]
        remote(ref, ref, send_sem.at[u, 7], recv_sem.at[u, 7], (w.z, w.part)).wait_recv()

    def vlocal(zz, p):
        return vgrads[zz, p, w.c]

    def vfinish(total):
        vkeep[...] = total

    vecs = Reduce(
        w, vlocal, vr0, vr1, vr2, vr3, lambda k: send_sem.at[UNITS, k], lambda k: recv_sem.at[UNITS, k],
        vgrads.at[:, :, 1 - w.c], F32, vfinish,
    )

    for u in range(8):
        units[u].e0()

    def launch(u):
        if u >= SLOTS:
            pl.semaphore_wait(credit, 1)
        units[u].e0()

    def tick(t):
        if t < UNITS:
            if t < 8:
                need("g%d" % t)
            units[t].e1()
        if t == 13:
            vecs.e1()
        if 0 <= t - 1 < UNITS:
            units[t - 1].e2()
        if t == 14:
            vecs.e2()
        if 0 <= t - 2 < UNITS:
            units[t - 2].e3(keep_flat(t - 2))
        if t == 15:
            vecs.e3(vkeep)
        if 0 <= t - 3 < UNITS:
            units[t - 3].e4(keep_flat(t - 3))
        if t == 16:
            vecs.e4(vkeep)
        if 0 <= t - 4 < UNITS:
            swapped(t - 4)
        if 0 <= t - 3 < UNITS - SLOTS:
            units[t - 3].sent()
            pl.semaphore_signal(credit, inc=1, device_id=(w.z, w.part), device_id_type=MESH)

    class Flat:
        def __init__(self, u):
            self.u = u

        def __getitem__(self, _):
            return keep[self.u].reshape(2 * ROWS, HALF)

        def __setitem__(self, _, value):
            keep[self.u] = value.reshape(2, ROWS, HALF)

    keep_flat = Flat

    def weight_grad(u, a, b):
        s = u % SLOTS

        def cols(cs):
            grads[s, :, :, :, cs] = dot_tn(a(), b(cs)).astype(BF).reshape(DEPTH, PLANE, 2 * ROWS, 256)

        thirds(cols)

    vrow = lambda r: vec[r : r + 1, :]
    DR, DO, DQ, DK, DV = range(5)
    tick(0)
    need("dx", "o2", "wco")
    work[DR] = dx[...].astype(BF)
    weight_grad(8, lambda: act[0], lambda cs: work[DR, :, cs])
    launch(8)

    def times_output(slot):
        def cols(cs):
            work[DO, :, cs] = dot_nt(work[DR], wbuf[slot, cs, :]).astype(BF)

        thirds(cols)

    times_output(0)
    load("wso", wattn_hbm.at[3], wbuf.at[0])
    delta[...] = head_delta(work[DO], act[0])
    load("a2", act_hbm.at[A2], act.at[0])
    need("cq", "kv", "lse", "vec", "gv")
    gv[11:12, :] = colsum(work[DR])
    tick(1)

    def cross_mask(s, i):
        n = s.shape[0]
        if (i + 1) * n <= 750:
            return s
        f = lax.broadcasted_iota(jnp.int32, (n, 1), 0) + i * n
        return s + jnp.where(f < frames, 0.0, -1e30)

    def self_mask(s, i):
        r = lax.broadcasted_iota(jnp.int32, s.shape, 0) + i * s.shape[0]
        c = lax.broadcasted_iota(jnp.int32, s.shape, 1)
        return jnp.where((r <= c) & (r < length), s, -1e30)

    for i in range(6):
        heads_backward(
            act.at[1], kv.at[0], kv.at[1], work.at[DO], lse.at[1], delta, work.at[DQ], dkv.at[0], dkv.at[1],
            cross_mask, PADDED, 256, acc, i, 1,
        )
        tick(2 + i)
    for n, (name, src) in enumerate((("q", act_hbm.at[Q]), ("k", act_hbm.at[K]), ("v", act_hbm.at[V_]), ("o", act_hbm.at[O]), ("a1", act_hbm.at[A1]), ("x", x_hbm))):
        load(name, src, kv.at[n // 3, pl.ds(n % 3 * TOK, TOK)])
    old = lambda n: kv.at[n // 3, pl.ds(n % 3 * TOK, TOK)]
    need("a2", "enc", "wcq", "wck", "wcv", "x2")
    weight_grad(9, lambda: act[0], lambda cs: work[DQ, :, cs])
    launch(9)
    gv[9:10, :] = colsum(work[DQ])
    gv[10:11, :] = colsum(dkv[1])

    def times_back(pairs):
        def cols(cs):
            total = 0.0
            for a, slot in pairs:
                total = total + dot_nt(work[a], wbuf[slot, cs, :])
            dacc[:, cs] = total

        thirds(cols)

    times_back(((DQ, 1),))
    load("wq", wattn_hbm.at[0], wbuf.at[1])
    d2, gg, gb = layer_norm_back(x2[...], vrow(2), dacc[...])
    gv[2:3, :] = gg
    gv[3:4, :] = gb
    dx[...] += d2
    weight_grad(10, lambda: enc[...], lambda cs: dkv[0, :FRAMES, cs])
    launch(10)
    tick(8)
    weight_grad(11, lambda: enc[...], lambda cs: dkv[1, :FRAMES, cs])
    launch(11)
    work[DR] = dx[...].astype(BF)
    gv[8:9, :] = colsum(work[DR])
    need("o", "wso")
    weight_grad(12, lambda: old(3)[...], lambda cs: work[DR, :, cs])
    launch(12)
    times_output(0)
    delta[...] = head_delta(work[DO], old(3)[...])
    tick(9)
    need("q", "k", "v")
    for i in range(2):
        heads_backward(
            old(0), old(1), old(2), work.at[DO], lse.at[0], delta, work.at[DQ], work.at[DK], work.at[DV],
            self_mask, TOK, 224, acc, 3 * i, 3,
        )
        tick(10 + i)
    gv[6:7, :] = colsum(work[DQ])
    gv[7:8, :] = colsum(work[DV])
    need("a1")
    for u, b in ((13, DQ), (14, DK), (15, DV)):
        weight_grad(u, lambda: old(4)[...], lambda cs, b=b: work[b, :, cs])
        launch(u)
    stores = []

    def store(src, dst):
        c = pltpu.make_async_copy(src, dst, store_sem.at[len(stores)])
        c.start()
        stores.append(c)

    def encoder_rows(r0_, r1_):
        def cols(cs):
            denc[r0_:r1_, cs] = dot_nt(dkv[0, r0_:r1_], wbuf[2, cs, :]) + dot_nt(dkv[1, r0_:r1_], wbuf[3, cs, :])

        thirds(cols)

    encoder_rows(0, 512)
    tick(12)
    encoder_rows(512, 1024)
    encoder_rows(1024, FRAMES)
    load("wk", wattn_hbm.at[1], wbuf.at[2])
    load("wv", wattn_hbm.at[2], wbuf.at[3])
    store(denc, denc_hbm)
    need("wq", "wk", "wv", "x")
    times_back(((DQ, 1), (DK, 2), (DV, 3)))
    d1, gg, gb = layer_norm_back(old(5)[...].astype(F32), vrow(0), dacc[...])
    gv[0:1, :] = gg
    gv[1:2, :] = gb
    dx[...] += d1
    store(dx, dtok_hbm)
    table = jnp.transpose(jnp.concatenate([gv[...], jnp.zeros((104, D), F32)], 0))
    lane = lax.broadcasted_iota(jnp.int32, (ROWS, 128), 1)
    for b in range(4):
        for core in range(2):
            for j in range(4):
                at = b * 192 + core * 96 + j * ROWS
                block = jnp.where(lane < 13, table[at : at + ROWS], 0.0)
                for a in range(4):
                    src = (4 * a + b) * 48 + core * ROWS
                    col = jnp.sum(jnp.where(lane == 13 + j, table[src : src + ROWS], 0.0), -1, keepdims=True)
                    block = jnp.where(lane == 13 + a, col, block)
                n = at // ROWS
                vgrads[n // 8, n // 2 % 4, n % 2] = block
    vecs.e0()
    for t in range(13, UNITS + 4):
        tick(t)
    store(gsum, gsum_hbm)
    store(vkeep, gvsum_hbm)
    for u in range(UNITS):
        if u >= UNITS - SLOTS:
            units[u].sent()
        swap(u).wait_send()
    vecs.sent()
    for c in stores:
        c.wait()


def call_backward(length, frames, x, enc, act, kv, lse, xs, wattn, gffn, vec, gv):
    any_ = pl.BlockSpec(memory_space=pl.ANY)
    smem = pl.BlockSpec(memory_space=pltpu.SMEM)
    t = lambda *s: jax.ShapeDtypeStruct(s, F32)
    v = pltpu.VMEM
    dma = pltpu.SemaphoreType.DMA
    n, rows = DEPTH, 2 * ROWS
    return pl.pallas_call(
        backward_kernel,
        out_shape=[t(TOK, D), t(FRAMES, D), t(UNITS, ROWS, D), t(ROWS, 128)],
        in_specs=[smem, smem] + [any_] * 10,
        out_specs=[any_] * 4,
        scratch_shapes=[
            v((SLOTS, n, PLANE, rows, D), BF), v((SLOTS, n, PLANE, rows, HALF), BF), v((UNITS, n, 2, rows, HALF), BF),
            v((UNITS, n, rows, HALF), BF), v((UNITS, 3, rows, HALF), BF), v((UNITS, 2, ROWS, HALF), F32), v((UNITS, ROWS, D), F32),
            v((n, PLANE, 2, ROWS, 128), F32), v((n, PLANE, ROWS, 128), F32), v((n, 2, ROWS, 128), F32),
            v((n, ROWS, 128), F32), v((3, ROWS, 128), F32), v((ROWS, 128), F32),
            v((2, PADDED, D), BF), v((2, PADDED, D), BF), v((FRAMES, D), BF), v((2, TOK, D), BF), v((5, TOK, D), BF),
            v((TOK, D), F32), v((TOK, D), F32), v((TOK, D), F32), v((TOK, 128), F32), v((FRAMES, D), F32),
            v((4, D, D), BF), v((24, D), F32), v((24, D), F32), v((2, 16, TOK), F32), v((16, TOK), F32),
            dma((40,)), dma((UNITS + 1, 8)), dma((UNITS + 1, 8)), pltpu.SemaphoreType.REGULAR, dma((4,)),
        ],
        compiler_params=pltpu.CompilerParams(collective_id=1, has_side_effects=True, vmem_limit_bytes=63 * MIB),
        name="backward",
    )(length, frames, x, enc, act, kv, lse, xs, wattn, gffn, vec, gv)


beta_first = 0.9
beta_second = 0.999
adam_epsilon = 1e-08
weight_decay = 0.01
rate_attention = 0.06
rate_feedforward = 0.03
rate_vector = 0.35


def matmul(left, right):
    return jnp.dot(left, right, preferred_element_type=jnp.float32)


def inner_rows(left, right):
    return lax.dot_general(
        left, right, (((0,), (0,)), ((), ())), preferred_element_type=jnp.float32
    )


def outer_last(left, right):
    return lax.dot_general(
        left, right, (((1,), (1,)), ((), ())), preferred_element_type=jnp.float32
    )


def norm_apply(value, gain, shift):
    center = value - jnp.mean(value, -1, keepdims=True)
    spread = jnp.mean(center * center, -1, keepdims=True)
    return center * lax.rsqrt(spread + norm_epsilon) * gain + shift


def gelu_exact(value):
    return jax.nn.gelu(value, approximate=False)


def head_group():
    return 4


def grouped(value):
    width = head_group()
    return (
        value.reshape(value.shape[0], H, HD)
        .transpose(1, 0, 2)
        .reshape(H // width, width, value.shape[0], HD)
    )


def ungrouped(value):
    return value.reshape(H, value.shape[2], HD).transpose(1, 0, 2).reshape(value.shape[2], H * HD)


def attend_forward(query, keys, values, mask):

    def one_group(parts):
        q_group, k_group, v_group = parts
        scores = jnp.einsum("gtd,gsd->gts", q_group, k_group, preferred_element_type=jnp.float32)
        scores = jnp.where(mask[None], scores, -1e30)
        peak = jnp.max(scores, -1, keepdims=True)
        expo = jnp.exp(scores - peak)
        total = jnp.sum(expo, -1, keepdims=True)
        probs = (expo / total).astype(jnp.bfloat16)
        mixed = jnp.einsum("gts,gsd->gtd", probs, v_group, preferred_element_type=jnp.float32)
        return (mixed.astype(jnp.bfloat16), (peak + jnp.log(total))[..., 0])

    heads, summed = lax.map(one_group, (grouped(query), grouped(keys), grouped(values)))
    return (ungrouped(heads), summed)


def attend_backward(query, keys, values, summed, grad_out, mask):

    def one_group(parts):
        q_group, k_group, v_group, s_group, g_group = parts
        scores = jnp.einsum("gtd,gsd->gts", q_group, k_group, preferred_element_type=jnp.float32)
        probs = jnp.where(mask[None], jnp.exp(scores - s_group[..., None]), 0.0)
        grad_values = jnp.einsum(
            "gts,gtd->gsd", probs.astype(jnp.bfloat16), g_group, preferred_element_type=jnp.float32
        )
        grad_probs = jnp.einsum(
            "gtd,gsd->gts", g_group, v_group, preferred_element_type=jnp.float32
        )
        grad_scores = (
            probs * (grad_probs - jnp.sum(probs * grad_probs, -1, keepdims=True))
        ).astype(jnp.bfloat16)
        grad_query = jnp.einsum(
            "gts,gsd->gtd", grad_scores, k_group, preferred_element_type=jnp.float32
        ).astype(jnp.bfloat16)
        grad_keys = jnp.einsum(
            "gts,gtd->gsd", grad_scores, q_group, preferred_element_type=jnp.float32
        ).astype(jnp.bfloat16)
        return (grad_query, grad_keys, grad_values.astype(jnp.bfloat16))

    parts = (grouped(query), grouped(keys), grouped(values), summed, grouped(grad_out))
    grad_query, grad_keys, grad_values = lax.map(one_group, parts)
    return (ungrouped(grad_query), ungrouped(grad_keys), ungrouped(grad_values))


def make_masks(length, frames):
    place = jnp.arange(TOK)
    causal = (place[None, :] <= place[:, None]) & (place[None, :] < length)
    seen = jnp.broadcast_to(jnp.arange(FRAMES)[None, :] < frames, (TOK, FRAMES))
    return (place, causal, seen)


def clip_forward(weights, x_in, enc, length, frames):
    wa, wm, wv = weights
    vec = wv.astype(jnp.float32)
    scale = HD ** (-0.5)
    place, causal, seen = make_masks(length, frames)
    x = x_in.astype(jnp.float32)
    first = norm_apply(x, vec[0], vec[1]).astype(jnp.bfloat16)
    query = ((matmul(first, wa[0]) + vec[6]) * scale).astype(jnp.bfloat16)
    keys = matmul(first, wa[1]).astype(jnp.bfloat16)
    values = (matmul(first, wa[2]) + vec[7]).astype(jnp.bfloat16)
    mixed, summed_self = attend_forward(query, keys, values, causal)
    second_in = x + matmul(mixed, wa[3]) + vec[8]
    second = norm_apply(second_in, vec[2], vec[3]).astype(jnp.bfloat16)
    cross_query = ((matmul(second, wa[4]) + vec[9]) * scale).astype(jnp.bfloat16)
    cross_keys = matmul(enc, wa[5]).astype(jnp.bfloat16)
    cross_values = (matmul(enc, wa[6]) + vec[10]).astype(jnp.bfloat16)
    heard, summed_cross = attend_forward(cross_query, cross_keys, cross_values, seen)
    third_in = second_in + matmul(heard, wa[7]) + vec[11]
    third = norm_apply(third_in, vec[4], vec[5]).astype(jnp.bfloat16)
    hidden_pre = outer_last(third, wm[0]) + vec[13:].reshape(FF)
    hidden = gelu_exact(hidden_pre).astype(jnp.bfloat16)
    result = third_in + matmul(hidden, wm[1]) + vec[12]
    saved = (
        first,
        query,
        keys,
        values,
        mixed,
        summed_self,
        second_in,
        second,
        cross_query,
        cross_keys,
        cross_values,
        heard,
        summed_cross,
        third_in,
        third,
        hidden_pre,
        hidden,
    )
    return (result.astype(jnp.bfloat16), saved)


def clip_backward(weights, x_in, enc, length, frames, cot, saved):
    wa, wm, wv = weights
    vec = wv.astype(jnp.float32)
    scale = HD ** (-0.5)
    (
        first,
        query,
        keys,
        values,
        mixed,
        summed_self,
        second_in,
        second,
        cross_query,
        cross_keys,
        cross_values,
        heard,
        summed_cross,
        third_in,
        third,
        hidden_pre,
        hidden,
    ) = saved
    place, causal, seen = make_masks(length, frames)
    grad_y = cot.astype(jnp.float32) * (place < length).astype(jnp.float32)[:, None]
    out_three = grad_y.astype(jnp.bfloat16)
    g_down = inner_rows(hidden, out_three)
    g_b_down = jnp.sum(out_three.astype(jnp.float32), 0)
    grad_hidden = outer_last(out_three, wm[1])
    _, gelu_pull = jax.vjp(gelu_exact, hidden_pre)
    grad_pre = gelu_pull(grad_hidden)[0].astype(jnp.bfloat16)
    g_up = inner_rows(grad_pre, third)
    g_b_up = jnp.sum(grad_pre.astype(jnp.float32), 0)
    grad_third = matmul(grad_pre, wm[0])
    _, norm_pull = jax.vjp(norm_apply, third_in, vec[4], vec[5])
    part_three, g_gain_three, g_shift_three = norm_pull(grad_third)
    grad_third_in = grad_y + part_three
    out_two = grad_third_in.astype(jnp.bfloat16)
    g_cross_out = inner_rows(heard, out_two)
    g_b_cross_out = jnp.sum(out_two.astype(jnp.float32), 0)
    grad_heard = outer_last(out_two, wa[7]).astype(jnp.bfloat16)
    grad_cq, grad_ck, grad_cv = attend_backward(
        cross_query, cross_keys, cross_values, summed_cross, grad_heard, seen
    )
    grad_cq = grad_cq * scale
    g_cross_query = inner_rows(second, grad_cq)
    g_b_cross_query = jnp.sum(grad_cq.astype(jnp.float32), 0)
    g_cross_keys = inner_rows(enc, grad_ck)
    g_cross_values = inner_rows(enc, grad_cv)
    g_b_cross_values = jnp.sum(grad_cv.astype(jnp.float32), 0)
    grad_enc = outer_last(grad_ck, wa[5]) + outer_last(grad_cv, wa[6])
    grad_second = outer_last(grad_cq, wa[4])
    _, norm_pull = jax.vjp(norm_apply, second_in, vec[2], vec[3])
    part_two, g_gain_two, g_shift_two = norm_pull(grad_second)
    grad_second_in = grad_third_in + part_two
    out_one = grad_second_in.astype(jnp.bfloat16)
    g_self_out = inner_rows(mixed, out_one)
    g_b_self_out = jnp.sum(out_one.astype(jnp.float32), 0)
    grad_mixed = outer_last(out_one, wa[3]).astype(jnp.bfloat16)
    grad_q, grad_k, grad_v = attend_backward(query, keys, values, summed_self, grad_mixed, causal)
    grad_q = grad_q * scale
    g_self_query = inner_rows(first, grad_q)
    g_self_keys = inner_rows(first, grad_k)
    g_self_values = inner_rows(first, grad_v)
    g_b_self_query = jnp.sum(grad_q.astype(jnp.float32), 0)
    g_b_self_values = jnp.sum(grad_v.astype(jnp.float32), 0)
    grad_first = outer_last(grad_q, wa[0]) + outer_last(grad_k, wa[1]) + outer_last(grad_v, wa[2])
    _, norm_pull = jax.vjp(norm_apply, x_in.astype(jnp.float32), vec[0], vec[1])
    part_one, g_gain_one, g_shift_one = norm_pull(grad_first)
    grad_x = grad_second_in + part_one
    g_attn = jnp.stack(
        [
            g_self_query,
            g_self_keys,
            g_self_values,
            g_self_out,
            g_cross_query,
            g_cross_keys,
            g_cross_values,
            g_cross_out,
        ]
    )
    g_mlp = jnp.stack([g_up, g_down])
    g_vec = jnp.concatenate(
        [
            jnp.stack(
                [
                    g_gain_one,
                    g_shift_one,
                    g_gain_two,
                    g_shift_two,
                    g_gain_three,
                    g_shift_three,
                    g_b_self_query,
                    g_b_self_values,
                    g_b_self_out,
                    g_b_cross_query,
                    g_b_cross_values,
                    g_b_cross_out,
                    g_b_down,
                ]
            ),
            g_b_up.reshape(FF // D, D),
        ],
        0,
    )
    return ((g_attn, g_mlp, g_vec), grad_x, grad_enc)


def adam_update(weight, first, second, grad, rate):
    first_new = beta_first * first + (1.0 - beta_first) * grad
    second_new = beta_second * second + (1.0 - beta_second) * grad * grad
    ratio = (
        first_new
        / (1.0 - beta_first**STEP)
        / (jnp.sqrt(second_new / (1.0 - beta_second**STEP)) + adam_epsilon)
    )
    return (weight - rate * (ratio + weight_decay * weight), first_new, second_new)


def plain_body(
    tokens,
    enc_states,
    cotangent,
    tok_len,
    frame_count,
    attn_w,
    attn_m,
    attn_v,
    mlp_w,
    mlp_m,
    mlp_v,
    vec_w,
    vec_m,
    vec_v,
):
    shards = (attn_w.astype(jnp.bfloat16), mlp_w.astype(jnp.bfloat16), vec_w.astype(jnp.bfloat16))
    weights = (
        lax.all_gather(shards[0], ("dp", "fsdp"), axis=1, tiled=True),
        lax.all_gather(shards[1], ("dp", "fsdp"), axis=1, tiled=True),
        lax.all_gather(shards[2], ("dp", "fsdp"), axis=1, tiled=True),
    )

    def forward_one(items):
        x_in, enc, length, frames = items
        return clip_forward(weights, x_in, enc, length, frames)

    result, saved = lax.map(forward_one, (tokens, enc_states, tok_len, frame_count))
    back_weights = (
        lax.all_gather(shards[0], ("dp", "fsdp"), axis=1, tiled=True),
        lax.all_gather(shards[1], ("dp", "fsdp"), axis=1, tiled=True),
        lax.all_gather(shards[2], ("dp", "fsdp"), axis=1, tiled=True),
    )

    def backward_one(carry, items):
        x_in, enc, length, frames, cot, kept = items
        grads, grad_x, grad_enc = clip_backward(back_weights, x_in, enc, length, frames, cot, kept)
        return (jax.tree.map(jnp.add, carry, grads), (grad_x, grad_enc))

    zeros = (
        jnp.zeros(weights[0].shape, jnp.float32),
        jnp.zeros(weights[1].shape, jnp.float32),
        jnp.zeros(weights[2].shape, jnp.float32),
    )
    totals, (d_tokens, d_enc) = lax.scan(
        backward_one, zeros, (tokens, enc_states, tok_len, frame_count, cotangent, saved)
    )
    grad_attn, grad_mlp, grad_vec = (
        lax.psum_scatter(totals[0], ("dp", "fsdp"), scatter_dimension=1, tiled=True),
        lax.psum_scatter(totals[1], ("dp", "fsdp"), scatter_dimension=1, tiled=True),
        lax.psum_scatter(totals[2], ("dp", "fsdp"), scatter_dimension=1, tiled=True),
    )
    attn_new = adam_update(attn_w, attn_m, attn_v, grad_attn, rate_attention)
    mlp_new = adam_update(mlp_w, mlp_m, mlp_v, grad_mlp, rate_feedforward)
    vec_new = adam_update(vec_w, vec_m, vec_v, grad_vec, rate_vector)
    return (
        result,
        d_tokens,
        d_enc,
        attn_new[0],
        attn_new[1],
        attn_new[2],
        mlp_new[0],
        mlp_new[1],
        mlp_new[2],
        vec_new[0],
        vec_new[1],
        vec_new[2],
    )


def fused_body(tokens, enc_states, cotangent, tok_len, frame_count, attn_w, attn_m, attn_v, mlp_w, mlp_m, mlp_v, vec_w, vec_m, vec_v):
    nv = vec_w.shape[0]
    vec_t = jnp.pad(vec_w.T, ((0, 0), (0, 128 - nv)))
    out, act, kv, lse, xs, wattn, gffn, vec, gv = call_forward(
        tok_len, frame_count, tokens[0], enc_states[0], cotangent[0], attn_w, mlp_w.reshape(8, ROWS, D), vec_t
    )
    d_tokens, d_enc, gsum, gvsum = call_backward(
        tok_len, frame_count, tokens[0], enc_states[0], act, kv, lse, xs,
        wattn.reshape(8, D, D), gffn.reshape(8, DEPTH, PLANE, 2 * ROWS, D), vec, gv,
    )
    attn_new = adam_update(attn_w, attn_m, attn_v, gsum[:8], rate_attention)
    mlp_new = adam_update(mlp_w, mlp_m, mlp_v, gsum[8:].reshape(mlp_w.shape), rate_feedforward)
    vec_new = adam_update(vec_w, vec_m, vec_v, gvsum[:, :nv].T, rate_vector)
    return (out[None], d_tokens[None], d_enc[None], *attn_new, *mlp_new, *vec_new)


def solution(mesh):
    fused = mesh.shape["dp"] == DEPTH and mesh.shape["fsdp"] == 2 * PLANE
    return jax.shard_map(
        fused_body if fused else plain_body,
        mesh=mesh,
        in_specs=(
            P(("dp", "fsdp"), None, None),
            P(("dp", "fsdp"), None, None),
            P(("dp", "fsdp"), None, None),
            P(("dp", "fsdp")),
            P(("dp", "fsdp")),
            P(None, ("dp", "fsdp"), None),
            P(None, ("dp", "fsdp"), None),
            P(None, ("dp", "fsdp"), None),
            P(None, ("dp", "fsdp"), None),
            P(None, ("dp", "fsdp"), None),
            P(None, ("dp", "fsdp"), None),
            P(None, ("dp", "fsdp")),
            P(None, ("dp", "fsdp")),
            P(None, ("dp", "fsdp")),
        ),
        out_specs=(
            P(("dp", "fsdp"), None, None),
            P(("dp", "fsdp"), None, None),
            P(("dp", "fsdp"), None, None),
            P(None, ("dp", "fsdp"), None),
            P(None, ("dp", "fsdp"), None),
            P(None, ("dp", "fsdp"), None),
            P(None, ("dp", "fsdp"), None),
            P(None, ("dp", "fsdp"), None),
            P(None, ("dp", "fsdp"), None),
            P(None, ("dp", "fsdp")),
            P(None, ("dp", "fsdp")),
            P(None, ("dp", "fsdp")),
        ),
        check_vma=False,
    )
```

```python
import functools
import heapq
import jax
import jax.numpy as jnp
from jax import lax
from jax.experimental import pallas as pl
from jax.experimental.pallas import tpu as pltpu
from jax.sharding import PartitionSpec as P

D = 768
H = 12
HD = 64
FF = 3072
FRAMES = 1500
TOK = 448
STEP = 10
PADDED = 1536
ROWS = 24
PLANE = 4
DEPTH = 4
UNITS = 16
HALF = D // 2
BF = jnp.bfloat16
F32 = jnp.float32
MESH = pl.DeviceIdType.MESH
norm_epsilon = 1e-05
VMEM_LIMIT = 63 * 2**20


def dot(a, b):
    return lax.dot_general(a, b, (((1,), (0,)), ((), ())), preferred_element_type=F32)


def dot_nt(a, b):
    return lax.dot_general(a, b, (((1,), (1,)), ((), ())), preferred_element_type=F32)


def dot_tn(a, b):
    return lax.dot_general(a, b, (((0,), (0,)), ((), ())), preferred_element_type=F32)


def layer_norm(v, gain, shift):
    c = v - jnp.mean(v, -1, keepdims=True)
    s = jnp.mean(c * c, -1, keepdims=True)
    return c * lax.rsqrt(s + norm_epsilon) * gain + shift


def layer_norm_back(v, gain, grad):
    c = v - jnp.mean(v, -1, keepdims=True)
    r = lax.rsqrt(jnp.mean(c * c, -1, keepdims=True) + norm_epsilon)
    xh = c * r
    t = grad * gain
    dx = r * (t - jnp.mean(t, -1, keepdims=True) - xh * jnp.mean(t * xh, -1, keepdims=True))
    return dx, jnp.sum(grad * xh, 0, keepdims=True), jnp.sum(grad, 0, keepdims=True)


def gelu_both(u):
    z = jnp.abs(u) * 0.7071067811865476
    e = jnp.exp(-0.5 * u * u)
    t = 1.0 / (1.0 + 0.3275911 * z)
    poly = t * (0.254829592 + t * (-0.284496736 + t * (1.421413741 + t * (-1.453152027 + t * 1.061405429))))
    half = 0.5 * poly * e
    phi = jnp.where(u >= 0, 1.0 - half, half)
    return u * phi, phi + u * (e * 0.3989422804014327)


def colsum(v):
    return jnp.sum(v.astype(F32), 0, keepdims=True)


def head_lanes(rows, h):
    return (lax.broadcasted_iota(jnp.int32, (rows, 128), 1) // HD) == h


class Place:
    def __init__(self):
        self.z = lax.axis_index("dp")
        f = lax.axis_index("fsdp")
        self.f = f
        self.c = f % 2
        self.p = f // 2
        x, y = self.p % 2, self.p // 2
        self.part = f + 1 - 2 * self.c
        fx, fy = f + 2 - 4 * x, f + 4 - 8 * y
        px, py = self.p + 1 - 2 * x, self.p + 2 - 4 * y
        c = self.c
        self.n1, self.n2 = fx + c * (fy - fx), fy + c * (fx - fy)
        self.p1, self.p2, self.p3 = px + c * (py - px), py + c * (px - py), 3 - self.p
        self.zto = [(self.z + d) % DEPTH for d in range(1, DEPTH)]
        self.zfrom = [(self.z + DEPTH - d) % DEPTH for d in range(1, DEPTH)]
        self.own = pl.ds(pl.multiple_of(c * HALF, 128), HALF)
        self.other = pl.ds(pl.multiple_of(HALF - c * HALF, 128), HALF)

    def greet(self):
        barrier = pltpu.get_barrier_semaphore()
        others = [(zz, self.f) for zz in self.zto]
        others += [(self.z, self.n1), (self.z, self.n2), (self.z, self.part)]
        for device in others:
            pl.semaphore_signal(barrier, inc=1, device_id=device, device_id_type=MESH)
        pl.semaphore_wait(barrier, len(others))


def remote(src, dst, send, recv, device):
    return pltpu.make_async_remote_copy(
        src_ref=src, dst_ref=dst, send_sem=send, recv_sem=recv, device_id=device, device_id_type=MESH
    )


class Gather:
    def __init__(self, place, view, send, recv):
        self.w, self.view, self.send, self.recv = place, view, send, recv

    def copy(self, k, ref, device):
        return remote(ref, ref, self.send(k), self.recv(k), device)

    def own(self, zz, p):
        return self.view(zz, p, True)

    def s1(self):
        w = self.w
        for i, zz in enumerate(w.zto):
            self.copy(i, self.own(w.z, w.p), (zz, w.f)).start()

    def s2(self):
        w = self.w
        for i, zz in enumerate(w.zfrom):
            self.copy(i, self.own(zz, w.p), (zz, w.f)).wait_recv()
        self.copy(3, self.own(None, w.p), (w.z, w.n1)).start()
        self.copy(4, self.own(None, w.p), (w.z, w.n2)).start()
        self.copy(6, self.own(None, w.p), (w.z, w.part)).start()

    def s3(self):
        w = self.w
        self.copy(3, self.own(None, w.p1), (w.z, w.n1)).wait_recv()
        self.copy(5, self.own(None, w.p1), (w.z, w.n2)).start()
        self.copy(7, self.own(None, w.p1), (w.z, w.part)).start()

    def s4(self):
        w = self.w
        self.copy(4, self.own(None, w.p2), (w.z, w.n2)).wait_recv()
        self.copy(8, self.own(None, w.p2), (w.z, w.part)).start()

    def s5(self):
        w = self.w
        self.copy(5, self.own(None, w.p3), (w.z, w.n2)).wait_recv()
        self.copy(9, self.own(None, w.p3), (w.z, w.part)).start()

    def ready(self):
        w = self.w
        for k, p in enumerate((w.p, w.p1, w.p2, w.p3)):
            self.copy(6 + k, self.view(None, p, False), (w.z, w.part)).wait_recv()

    def drain(self):
        w = self.w
        for i, zz in enumerate(w.zto):
            self.copy(i, self.own(w.z, w.p), (zz, w.f)).wait_send()
        for k, p in ((3, w.p), (4, w.p), (5, w.p1), (6, w.p), (7, w.p1), (8, w.p2), (9, w.p3)):
            self.copy(k, self.own(None, p), (w.z, w.n1)).wait_send()


def heads_forward(q_ref, k_ref, v_ref, o_ref, lse_ref, mask_fn, keys, tile, first, count):
    def pair(hp, _):
        lanes = pl.ds(pl.multiple_of(hp * 128, 128), 128)
        kp, vp = k_ref[:keys, lanes], v_ref[:keys, lanes]
        for i in range(TOK // tile):
            rows = pl.ds(i * tile, tile)
            qp = q_ref[rows, lanes]
            outs = []
            sums = lse_ref[rows, :]
            for h in range(2):
                s = dot_nt(jnp.where(head_lanes(tile, h), qp, jnp.zeros_like(qp)), kp)
                s = mask_fn(s, i)
                peak = jnp.max(s, -1, keepdims=True)
                expo = jnp.exp(s - peak)
                total = jnp.sum(expo, -1, keepdims=True)
                outs.append(dot(expo.astype(BF), vp) * (1.0 / total))
                lane = lax.broadcasted_iota(jnp.int32, (tile, 128), 1)
                sums = jnp.where(lane == hp * 2 + h, peak + jnp.log(total), sums)
            lse_ref[rows, :] = sums
            o_ref[rows, lanes] = jnp.where(head_lanes(tile, 0), outs[0], outs[1]).astype(BF)
        return 0

    lax.fori_loop(first, first + count, pair, 0)


def thirds(f):
    for j in range(3):
        f(pl.ds(j * 256, 256))


class Reduce:
    def __init__(self, place, local, r0, r1, r2, r3, send, recv, source, low, finish):
        self.w, self.local, self.r0, self.r1, self.r2, self.r3 = place, local, r0, r1, r2, r3
        self.send, self.recv, self.source, self.low, self.finish = send, recv, source, low, finish

    def copy(self, k, src, dst, device):
        return remote(src, dst, self.send(k), self.recv(k), device)

    def copies(self, stage):
        w, r0 = self.w, self.r0
        if stage == 0:
            return [self.copy(0, self.source, r0, (w.z, w.part))]
        if stage == 1:
            return [
                self.copy(1, r0.at[:, w.p2], self.r1.at[:, 0], (w.z, w.n2)),
                self.copy(2, r0.at[:, w.p3], self.r1.at[:, 1], (w.z, w.n2)),
            ]
        if stage == 2:
            return [self.copy(3, r0.at[:, w.p1], self.r2, (w.z, w.n1))]
        return [self.copy(4 + i, r0.at[zz, w.p], self.r3.at[i], (zz, w.f)) for i, zz in enumerate(w.zto)]

    def e0(self):
        for c in self.copies(0):
            c.start()

    def arrived(self, stage):
        for c in self.copies(stage):
            c.wait_recv()

    def e1(self):
        w = self.w
        self.arrived(0)
        for p in (w.p2, w.p3):
            self.r0[:, p] = (self.local(slice(None), p) + self.r0[:, p].astype(F32)).astype(self.low)
        for c in self.copies(1):
            c.start()

    def e2(self):
        w = self.w
        self.arrived(1)
        total = self.local(slice(None), w.p1) + self.r0[:, w.p1].astype(F32) + self.r1[:, 1].astype(F32)
        self.r0[:, w.p1] = total.astype(self.low)
        for c in self.copies(2):
            c.start()

    def partial(self, zz):
        w = self.w
        return (
            self.local(zz, w.p) + self.r0[zz, w.p].astype(F32) + self.r1[zz, 0].astype(F32) + self.r2[zz].astype(F32)
        )

    def e3(self, keep):
        w = self.w
        self.arrived(2)
        keep[...] = self.partial(w.z)
        for zz in w.zto:
            self.r0[zz, w.p] = self.partial(zz).astype(self.low)
        for c in self.copies(3):
            c.start()

    def e4(self, keep):
        self.arrived(3)
        self.finish(keep[...] + (self.r3[0].astype(F32) + self.r3[1].astype(F32) + self.r3[2].astype(F32)))

    def sent(self):
        for stage in range(4):
            for c in self.copies(stage):
                c.wait_send()


def head_delta(grad, mixed):
    product = grad.astype(F32) * mixed.astype(F32)
    high = product.astype(BF)
    low = (product - high.astype(F32)).astype(BF)
    pick = lax.broadcasted_iota(jnp.int32, (16, D), 1) // HD == lax.broadcasted_iota(jnp.int32, (16, D), 0)
    pick = pick.astype(F32).astype(BF)
    return dot_nt(pick, high) + dot_nt(pick, low)


def heads_backward(q_ref, k_ref, v_ref, g_ref, lse_ref, delta_ref, mask_fn, keys, tile, acc, first, count):
    def pair(hp, _):
        lanes = pl.ds(pl.multiple_of(hp * 128, 128), 128)
        qp, gp = q_ref[:, lanes], g_ref[:, lanes]
        zero = jnp.zeros_like(qp)
        qs = [jnp.where(head_lanes(TOK, h), qp, zero) for h in range(2)]
        gs = [jnp.where(head_lanes(TOK, h), gp, zero) for h in range(2)]
        lse = [lse_ref[pl.ds(hp * 2 + h, 1), :] for h in range(2)]
        delta = [delta_ref[pl.ds(hp * 2 + h, 1), :] for h in range(2)]
        for i in range(keys // tile):
            rows = pl.ds(i * tile, tile)
            kp, vp = k_ref[rows, lanes], v_ref[rows, lanes]
            ps, ds = [], []
            for h in range(2):
                p = jnp.exp(mask_fn(dot_nt(kp, qs[h]), i) - lse[h])
                ds.append((p * (dot_nt(vp, gs[h]) - delta[h])).astype(BF))
                ps.append(p.astype(BF))
            dv = dot(ps[0], gs[0]) + dot(ps[1], gs[1])
            dk = dot(ds[0], qs[0]) + dot(ds[1], qs[1])
            v_ref[rows, lanes] = dv.astype(BF)
            k_ref[rows, lanes] = dk.astype(BF)
            a = jnp.where(head_lanes(TOK, 0), dot_tn(ds[0], kp), dot_tn(ds[1], kp))
            if i == 0:
                acc[...] = a
            else:
                acc[...] += a
        q_ref[:, lanes] = (acc[...].astype(BF).astype(F32) * 0.125).astype(BF)
        return 0

    lax.fori_loop(first, first + count, pair, 0)


class Plan:
    def __init__(self):
        self.now, self.queue, self.count = 0.0, [], 0

    def at(self, time, event, cost=0.1):
        heapq.heappush(self.queue, (time, self.count, event, cost))
        self.count += 1

    def step(self):
        time, _, event, cost = heapq.heappop(self.queue)
        self.now = max(self.now, time) + cost
        event()

    def until(self, time):
        while self.queue and self.queue[0][0] <= time:
            self.step()
        self.now = max(self.now, time)

    def work(self, cost, compute):
        self.until(self.now)
        compute()
        self.now += cost


PACE = 5.0
FIRST = 9.0
AHEAD = 3.0
HOP1, HOP2, LAND = 4.0, 9.0, 11.0
SUM_START = 84.0
SUM_HOPS = (6.0, 4.0, 3.5, 3.5)


ORDER = [5, 6, 0, 1, 2, 3, 4, 7, 8, 12, 9, 13, 10, 14, 11, 15]
A1, Q, K, V_, O, A2, CQ, O2, A3 = range(9)
DO = A3
SLOTS = 8
SUMS = [(12, 12), (8, 8), (13, 13), (9, 9), (14, 14), (10, 10), (15, 15), (11, 11), (7, 7), (4, 4), (5, 12), (6, 8), (3, 3), (0, 0), (1, 1), (2, 2)]


def block_kernel(
    len_ref, frames_ref, x_hbm, enc_hbm, cot_hbm, attn_hbm, mlp_hbm, vec_hbm,
    out_hbm, dtok_hbm, denc_hbm, gsum_hbm, gvsum_hbm,
    weights, vgather, stage, r0, r1, r2, r3, vr0, vr1, vr2, vr3, vkeep, vsmall, vpad,
    x_ref, enc, cot, act, kv, lse_cols, lse, delta, xs, hm, gp, oacc, dacc, acc, denc, vec, gv,
    load_sem, stage_sem, send_sem, recv_sem, vsend_sem, vrecv_sem, rsend_sem, rrecv_sem, credit, store_sem, denc_sem, own_sem,
):
    w = Place()
    length, frames = len_ref[0], frames_ref[0]
    local = lambda src, dst, sem: pltpu.make_async_copy(src, dst, sem)
    loads = [
        local(attn_hbm.at[:, :, w.own], stage.at[pl.ds(0, 8), w.c], load_sem.at[0]),
        local(mlp_hbm.at[:, :, w.own], stage.at[pl.ds(8, 8), w.c], load_sem.at[1]),
        local(vec_hbm, vsmall, load_sem.at[2]),
        local(x_hbm, x_ref, load_sem.at[3]),
        local(enc_hbm, enc, load_sem.at[4]),
        local(cot_hbm, cot, load_sem.at[5]),
    ]
    for i in (2, 0, 1, 3, 4, 5):
        loads[i].start()
    nv, nc = vsmall.shape
    vpad[...] = jnp.zeros_like(vpad)
    loads[2].wait()
    vpad[:nv, :nc] = vsmall[...]
    vgather[w.z, w.p, w.c] = jnp.transpose(vpad[...])[:ROWS]
    w.greet()

    def unit_view(u):
        def view(zz, p, own):
            return weights.at[u, slice(None) if zz is None else zz, p, :, w.own if own else w.other]

        return view

    def vec_view(zz, p, own):
        return vgather.at[slice(None) if zz is None else zz, p, w.c if own else 1 - w.c]

    units = [Gather(w, unit_view(u), lambda k, u=u: send_sem.at[u, k], lambda k, u=u: recv_sem.at[u, k]) for u in ORDER]
    by_weight = {u: units[i] for i, u in enumerate(ORDER)}
    vecs = Gather(w, vec_view, lambda k: vsend_sem.at[0, k], lambda k: vrecv_sem.at[0, k])

    plan = Plan()
    vecs.s1()
    parts = ((5, 2, attn_hbm, 5), (0, 5, attn_hbm, 0), (7, 1, attn_hbm, 7), (8, 8, mlp_hbm, 0))
    swaps = []
    for i, (u0, n, src, at) in enumerate(parts):
        src = src.at[pl.ds(at, n), :, w.other]
        swaps.append(remote(src, stage.at[pl.ds(u0, n), w.c], stage_sem.at[0, i], stage_sem.at[1, i], (w.z, w.part)))
        swaps[i].start()
    loads[0].wait()
    loads[1].wait()
    arrived = set()

    def start_unit(i):
        u = ORDER[i]
        k = 0 if u in (5, 6) else 1 if u < 5 else 2 if u == 7 else 3
        if k not in arrived:
            swaps[k].wait_recv()
            arrived.add(k)
        weights[u, w.z, w.p, :, w.own] = stage[u].reshape(2 * ROWS, HALF).astype(BF)
        units[i].s1()

    def first_hop(i):
        units[i].s3()
        units[i].s4()

    for i in range(UNITS):
        begin = FIRST + PACE * i
        plan.at(begin - AHEAD - PACE - 0.2, functools.partial(start_unit, i))
        plan.at(begin - AHEAD, units[i].s2)
        plan.at(begin + HOP1, functools.partial(first_hop, i))
        plan.at(begin + HOP2, units[i].s5)
    plan.at(3.0, vecs.s2)

    def vec_hop():
        vecs.s3()
        vecs.s4()

    plan.at(6.1, vec_hop)
    plan.at(9.1, vecs.s5)

    def ready(i):
        plan.until(FIRST + PACE * i + LAND)
        units[i].ready()

    def keep_of(u):
        class Keep:
            def __getitem__(self, _):
                return stage[u].reshape(2 * ROWS, HALF)

            def __setitem__(self, _, value):
                stage[u] = value.reshape(2, ROWS, HALF)

        return Keep()

    def final_swap(u):
        return remote(stage.at[u, 1 - w.c], gsum_hbm.at[u, :, w.own], rsend_sem.at[u, 7], rrecv_sem.at[u, 7], (w.z, w.part))

    def final_own(u):
        return local(stage.at[u, w.c], gsum_hbm.at[u, :, w.own], own_sem.at[u])

    def final_wait(u):
        ref = gsum_hbm.at[u, :, w.other]
        remote(ref, ref, rsend_sem.at[u, 7], rrecv_sem.at[u, 7], (w.z, w.part)).wait_recv()

    sums = []
    for r, (u, at) in enumerate(SUMS):

        def own_grad(zz, p, at=at):
            return weights[at, zz, p, :, w.own].astype(F32)

        def finish(total, u=u):
            stage[u] = total.reshape(2, ROWS, HALF)
            final_swap(u).start()
            final_own(u).start()

        sums.append(
            Reduce(
                w, own_grad, r0.at[r % SLOTS], r1.at[u], r2.at[u], r3.at[u],
                lambda k, u=u: rsend_sem.at[u, k], lambda k, u=u: rrecv_sem.at[u, k],
                weights.at[at, :, :, :, w.other], BF, finish,
            )
        )

    def vfinish(total):
        vkeep[...] = total

    vsums = Reduce(
        w, lambda zz, p: vgather[zz, p, w.c], vr0, vr1, vr2, vr3, lambda k: vsend_sem.at[1, k], lambda k: vrecv_sem.at[1, k],
        vgather.at[:, :, 1 - w.c], F32, vfinish,
    )

    recycled = set()
    sums_begin = [SUM_START]

    def launch(r):
        if r >= SLOTS:
            while r - SLOTS not in recycled:
                plan.step()
            pl.semaphore_wait(credit, 1)
        sums[r].e0()
        begin = max(plan.now + 2.0, sums_begin[0])
        sums_begin[0] = begin + PACE
        u = SUMS[r][0]

        def recycle():
            sums[r].e4(keep_of(u))
            if r < UNITS - SLOTS:
                sums[r].sent()
                pl.semaphore_signal(credit, inc=1, device_id=(w.z, w.part), device_id_type=MESH)
                recycled.add(r)

        steps = (sums[r].e1, sums[r].e2, lambda: sums[r].e3(keep_of(u)), recycle, lambda: final_wait(u))
        for k, event in enumerate(steps):
            plan.at(begin + sum(SUM_HOPS[:k]), event, 0.3)

    stores = []

    def store(src, dst):
        c = local(src, dst, store_sem.at[len(stores)])
        c.start()
        stores.append(c)

    def wcols(u, cols):
        return weights[u, :, :, :, cols].reshape(D, cols.size)

    def wrows(u, rows):
        return weights.at[u].reshape(D, D)[rows, :]

    def weight_grad(at, a, b):
        def cols(cs):
            weights[at, :, :, :, cs] = dot_tn(a(), b(cs)).astype(BF).reshape(DEPTH, PLANE, 2 * ROWS, 256)

        thirds(cols)

    vrow = lambda r, cols=slice(None): vec[r : r + 1, cols]

    lse_cols[...] = jnp.zeros_like(lse_cols)
    kv[:, FRAMES // 16 * 16 :, :] = jnp.zeros((2, PADDED - FRAMES // 16 * 16, D), BF)
    loads[4].wait()
    plan.until(12.0)
    vecs.ready()
    table = vgather[...].reshape(D, 128).astype(BF).astype(F32)
    vec[...] = jnp.transpose(table)[:24, :]
    lane = lax.broadcasted_iota(jnp.int32, (ROWS, 128), 1)
    source = lax.broadcasted_iota(jnp.int32, (128, 128), 0)
    spread = [dot(table.astype(BF), (source == 13 + a).astype(F32).astype(BF)) for a in range(4)]
    blocks = []
    for chip in range(16):
        for core in range(2):
            block = jnp.zeros((ROWS, 128), F32)
            for j in range(4):
                at = (chip % 4) * 192 + core * 96 + j * ROWS
                block = jnp.where(lane == j, spread[chip // 4][at : at + ROWS], block)
            blocks.append(block)
    vec[16:24, :] = jnp.transpose(jnp.concatenate(blocks, 0))[:8, :]
    loads[3].wait()
    act[A1] = layer_norm(x_ref[...].astype(F32), vrow(0), vrow(1)).astype(BF)
    plan.now += 4.0

    def enc_project(u, which, bias, a, b):
        def cols(cs):
            r = dot(enc[a:b, :], wcols(u, cs))
            if bias is not None:
                r = r + vrow(bias, cs)
            kv[which, a:b, cs] = r.astype(BF)

        thirds(cols)

    for i, (u, bias) in enumerate(((5, None), (6, 10))):
        ready(i)
        for a, b in ((0, 512), (512, 1024), (1024, FRAMES)):
            plan.work(0.8, functools.partial(enc_project, u, i, bias, a, b))

    def project(src, u, dst, bias, scale):
        def cols(cs):
            r = dot(act[src], wcols(u, cs))
            if bias is not None:
                r = r + vrow(bias, cs)
            act[dst, :, cs] = (r * scale).astype(BF)

        thirds(cols)

    for i, args in ((2, (A1, 0, Q, 6, 0.125)), (3, (A1, 1, K, None, 1.0)), (4, (A1, 2, V_, 7, 1.0))):
        ready(i)
        plan.work(0.7, functools.partial(project, *args))

    def self_mask(s, i):
        r = lax.broadcasted_iota(jnp.int32, s.shape, 0) + i * s.shape[0]
        c = lax.broadcasted_iota(jnp.int32, s.shape, 1)
        return jnp.where((c <= r) & (c < length), s, -1e30)

    def cross_mask(s, i):
        c = lax.broadcasted_iota(jnp.int32, (1, PADDED - 640), 1) + 640
        return jnp.concatenate([s[:, :640], jnp.where(c < frames, s[:, 640:], -1e30)], axis=1)

    def self_pairs(i):
        heads_forward(act.at[Q], act.at[K], act.at[V_], act.at[O], lse_cols, self_mask, TOK, 448, 2 * i, 2)

    for i in range(3):
        plan.work(1.7, functools.partial(self_pairs, i))
    lse[0] = jnp.transpose(lse_cols[...])[:16, :]
    ready(5)

    def residual(src, base, u, dst, bias):
        def cols(cs):
            xs[dst, :, cs] = base(cs) + dot(act[src], wcols(u, cs)) + vrow(bias, cs)

        thirds(cols)

    def norm(src, dst, row):
        act[dst] = layer_norm(xs[src], vrow(row), vrow(row + 1)).astype(BF)

    plan.work(0.8, lambda: residual(O, lambda cs: x_ref[:, cs].astype(F32), 3, 0, 8))
    plan.work(0.8, lambda: norm(0, A2, 2))
    ready(6)
    plan.work(0.7, lambda: project(A2, 4, CQ, 9, 0.125))

    def cross_pair(i):
        heads_forward(act.at[CQ], kv.at[0], kv.at[1], act.at[O2], lse_cols, cross_mask, PADDED, 224, i, 1)

    for i in range(6):
        plan.work(2.2, functools.partial(cross_pair, i))
    ready(7)
    plan.work(0.8, lambda: residual(O2, lambda cs: xs[0, :, cs], 7, 1, 11))
    plan.work(0.8, lambda: norm(1, A3, 4))
    lse[1] = jnp.transpose(lse_cols[...])[:16, :]
    loads[5].wait()
    ok = lax.broadcasted_iota(jnp.int32, (TOK, 1), 0) < length
    cot[...] = jnp.where(ok, cot[...], jnp.zeros((TOK, D), BF))
    gv[...] = jnp.zeros_like(gv)
    gv[12:13, :] = colsum(cot[...])
    oacc[...] = jnp.zeros_like(oacc)
    dacc[...] = jnp.zeros_like(dacc)
    for j in range(4):
        ready(8 + 2 * j)

        def hidden(rs):
            u = dot_nt(act[A3], wrows(8 + j, rs)) + vec[16 + j : 17 + j, rs]
            g, d = gelu_both(u)
            hm[:, rs] = g.astype(BF)
            gp[:, rs] = d.astype(BF)

        plan.work(1.5, lambda: thirds(hidden))
        ready(9 + 2 * j)

        def down(rs):
            oacc[:, rs] += dot(hm[...], wcols(12 + j, rs))
            d = (dot_nt(cot[...], wrows(12 + j, rs)) * gp[:, rs].astype(F32)).astype(BF)
            gp[:, rs] = d
            gv[13 + j : 14 + j, rs] = colsum(d)

        plan.work(1.4, lambda: thirds(down))

        def back(rs):
            dacc[:, rs] += dot(gp[...], wcols(8 + j, rs))

        plan.work(0.7, lambda: thirds(back))
        by_weight[12 + j].drain()
        plan.work(0.7, lambda: weight_grad(12 + j, lambda: hm[...], lambda cs: cot[:, cs]))
        launch(2 * j)
        by_weight[8 + j].drain()
        plan.work(0.7, lambda: weight_grad(8 + j, lambda: gp[...], lambda cs: act[A3, :, cs]))
        launch(2 * j + 1)
    hm[...] = (xs[1] + oacc[...] + vrow(12)).astype(BF)
    store(hm, out_hbm)
    dx = oacc
    dpart, gg, gb = layer_norm_back(xs[1], vrow(4), dacc[...])
    gv[4:5, :] = gg
    gv[5:6, :] = gb
    dx[...] = cot[...].astype(F32) + dpart
    dr = cot
    dr[...] = dx[...].astype(BF)
    plan.now += 2.0

    def times_output(u):
        def cols(cs):
            act[DO, :, cs] = dot_nt(dr[...], wrows(u, cs)).astype(BF)

        thirds(cols)

    plan.work(0.7, lambda: times_output(7))
    by_weight[7].drain()
    plan.work(0.7, lambda: weight_grad(7, lambda: act[O2], lambda cs: dr[:, cs]))
    launch(8)
    plan.now += 1.0
    delta[...] = head_delta(act[DO], act[O2])
    gv[11:12, :] = colsum(dr[...])

    def cross_mask_t(s, i):
        n = s.shape[0]
        if (i + 1) * n <= 750:
            return s
        f = lax.broadcasted_iota(jnp.int32, (n, 1), 0) + i * n
        return s + jnp.where(f < frames, 0.0, -1e30)

    def self_mask_t(s, i):
        r = lax.broadcasted_iota(jnp.int32, s.shape, 0) + i * s.shape[0]
        c = lax.broadcasted_iota(jnp.int32, s.shape, 1)
        return jnp.where((r <= c) & (r < length), s, -1e30)

    def cross_pair_back(i):
        heads_backward(
            act.at[CQ], kv.at[0], kv.at[1], act.at[DO], lse.at[1], delta, cross_mask_t, PADDED, 256, acc, i, 1
        )

    for i in range(6):
        plan.work(3.9, functools.partial(cross_pair_back, i))

    def times_back(pairs):
        def cols(cs):
            total = 0.0
            for a, u in pairs:
                total = total + dot_nt(act[a], wrows(u, cs))
            dacc[:, cs] = total

        thirds(cols)

    plan.work(0.7, lambda: times_back(((CQ, 4),)))
    by_weight[4].drain()
    plan.work(0.7, lambda: weight_grad(4, lambda: act[A2], lambda cs: act[CQ, :, cs]))
    launch(9)
    while not recycled >= {0, 1}:
        plan.step()
    plan.work(2.0, lambda: weight_grad(12, lambda: enc[...], lambda cs: kv[0, :FRAMES, cs]))
    launch(10)
    plan.work(2.0, lambda: weight_grad(8, lambda: enc[...], lambda cs: kv[1, :FRAMES, cs]))
    launch(11)
    gv[9:10, :] = colsum(act[CQ])
    gv[10:11, :] = colsum(kv[1])
    dpart, gg, gb = layer_norm_back(xs[0], vrow(2), dacc[...])
    gv[2:3, :] = gg
    gv[3:4, :] = gb
    dx[...] += dpart
    dr[...] = dx[...].astype(BF)
    gv[8:9, :] = colsum(dr[...])
    plan.now += 2.0
    plan.work(0.7, lambda: times_output(3))
    by_weight[3].drain()
    plan.work(0.7, lambda: weight_grad(3, lambda: act[O], lambda cs: dr[:, cs]))
    launch(12)
    delta[...] = head_delta(act[DO], act[O])
    plan.now += 0.5
    def self_pairs_back(i):
        heads_backward(
            act.at[Q], act.at[K], act.at[V_], act.at[DO], lse.at[0], delta, self_mask_t, TOK, 224, acc, 2 * i, 2
        )

    for i in range(3):
        plan.work(2.4, functools.partial(self_pairs_back, i))
    plan.work(1.8, lambda: times_back(((Q, 0), (K, 1), (V_, 2))))
    for r, a in ((13, Q), (14, K), (15, V_)):
        u = SUMS[r][0]
        by_weight[u].drain()
        plan.work(0.7, lambda: weight_grad(u, lambda: act[A1], lambda cs, a=a: act[a, :, cs]))
        launch(r)
    gv[6:7, :] = colsum(act[Q])
    gv[7:8, :] = colsum(act[V_])
    dpart, gg, gb = layer_norm_back(x_ref[...].astype(F32), vrow(0), dacc[...])
    gv[0:1, :] = gg
    gv[1:2, :] = gb
    dx[...] += dpart
    store(dx, dtok_hbm)
    vecs.drain()
    table = jnp.transpose(jnp.concatenate([gv[...], jnp.zeros((104, D), F32)], 0))
    high = table.astype(BF)
    rest = table - high.astype(F32)
    mid = rest.astype(BF)
    low = (rest - mid.astype(F32)).astype(BF)
    spread = []
    for j in range(4):
        pick = (source == 13 + j).astype(F32).astype(BF)
        spread.append(dot(high, pick) + (dot(mid, pick) + dot(low, pick)))
    for b in range(4):
        for core in range(2):
            for j in range(4):
                at = b * 192 + core * 96 + j * ROWS
                block = jnp.where(lane < 13, table[at : at + ROWS], 0.0)
                for a in range(4):
                    src = (4 * a + b) * 48 + core * ROWS
                    block = jnp.where(lane == 13 + a, spread[j][src : src + ROWS], block)
                n = at // ROWS
                vgather[n // 8, n // 2 % 4, n % 2] = block
    plan.now += 4.0
    vsums.e0()
    for k, event in enumerate((vsums.e1, vsums.e2, lambda: vsums.e3(vkeep), lambda: vsums.e4(vkeep))):
        plan.at(plan.now + 2.0 + 3.5 * k, event, 0.3)

    chunks = [(a, min(a + 128, FRAMES)) for a in range(0, FRAMES, 128)]
    outs = {}

    def encoder_chunk(i):
        a, b = chunks[i]
        if i >= 2:
            outs[i - 2].wait()
        for k in range(3):
            cs = pl.ds(k * 256, 256)
            v = dot_nt(kv[0, a:b], wrows(5, cs)) + dot_nt(kv[1, a:b], wrows(6, cs))
            for h in range(2):
                denc[i % 2, pl.ds(2 * k + h, b - a, stride=6), :] = v[:, h * 128 : (h + 1) * 128]
        c = local(denc.at[i % 2, pl.ds(0, 6 * (b - a))], denc_hbm.at[pl.ds(6 * a, 6 * (b - a))], denc_sem.at[i % 2])
        c.start()
        outs[i] = c

    for i in range(len(chunks)):
        plan.work(0.45, functools.partial(encoder_chunk, i))
    while plan.queue:
        plan.step()
    vpad[:ROWS, :] = vkeep[...]
    vsmall[...] = jnp.transpose(vpad[...])[:nv, :nc]
    store(vsmall, gvsum_hbm)
    for c in swaps:
        c.wait_send()
    for u in (5, 6):
        by_weight[u].drain()
    for r, (u, _) in enumerate(SUMS):
        if r >= UNITS - SLOTS:
            sums[r].sent()
        final_swap(u).wait_send()
        final_own(u).wait()
    vsums.sent()
    outs[10].wait()
    outs[11].wait()
    for c in stores:
        c.wait()


def call_block(length, frames, x, enc, cot, attn_w, mlp_w, vec_w):
    any_ = pl.BlockSpec(memory_space=pl.ANY)
    smem = pl.BlockSpec(memory_space=pltpu.SMEM)
    t = lambda *s, dt=F32: jax.ShapeDtypeStruct(s, dt)
    v = pltpu.VMEM
    dma = pltpu.SemaphoreType.DMA
    n, rows = DEPTH, 2 * ROWS
    return pl.pallas_call(
        block_kernel,
        out_shape=[t(TOK, D, dt=BF), t(TOK, D), t(FRAMES * 6, 128), t(UNITS, ROWS, D), t(*vec_w.shape)],
        in_specs=[smem, smem] + [any_] * 6,
        out_specs=[any_] * 5,
        scratch_shapes=[
            v((UNITS, n, PLANE, rows, D), BF), v((n, PLANE, 2, ROWS, 128), F32), v((UNITS, 2, ROWS, HALF), F32),
            v((SLOTS, n, PLANE, rows, HALF), BF), v((UNITS, n, 2, rows, HALF), BF), v((UNITS, n, rows, HALF), BF),
            v((UNITS, 3, rows, HALF), BF),
            v((n, PLANE, ROWS, 128), F32), v((n, 2, ROWS, 128), F32), v((n, ROWS, 128), F32), v((3, ROWS, 128), F32),
            v((ROWS, 128), F32), v(vec_w.shape, F32), v((128, 128), F32),
            v((TOK, D), BF), v((FRAMES, D), BF), v((TOK, D), BF), v((9, TOK, D), BF), v((2, PADDED, D), BF),
            v((TOK, 128), F32), v((2, 16, TOK), F32), v((16, TOK), F32), v((2, TOK, D), F32),
            v((TOK, D), BF), v((TOK, D), BF), v((TOK, D), F32), v((TOK, D), F32), v((TOK, 128), F32),
            v((2, 128 * 6, 128), F32), v((24, D), F32), v((24, D), F32),
            dma((6,)), dma((2, 4)), dma((UNITS, 10)), dma((UNITS, 10)), dma((2, 10)), dma((2, 10)),
            dma((UNITS, 8)), dma((UNITS, 8)), pltpu.SemaphoreType.REGULAR, dma((4,)), dma((2,)), dma((UNITS,)),
        ],
        compiler_params=pltpu.CompilerParams(collective_id=0, has_side_effects=True, vmem_limit_bytes=VMEM_LIMIT),
        name="block",
    )(length, frames, x, enc, cot, attn_w, mlp_w, vec_w)


beta_first = 0.9
beta_second = 0.999
adam_epsilon = 1e-08
weight_decay = 0.01
rate_attention = 0.06
rate_feedforward = 0.03
rate_vector = 0.35


def matmul(left, right):
    return jnp.dot(left, right, preferred_element_type=jnp.float32)


def inner_rows(left, right):
    return lax.dot_general(
        left, right, (((0,), (0,)), ((), ())), preferred_element_type=jnp.float32
    )


def outer_last(left, right):
    return lax.dot_general(
        left, right, (((1,), (1,)), ((), ())), preferred_element_type=jnp.float32
    )


def norm_apply(value, gain, shift):
    center = value - jnp.mean(value, -1, keepdims=True)
    spread = jnp.mean(center * center, -1, keepdims=True)
    return center * lax.rsqrt(spread + norm_epsilon) * gain + shift


def gelu_exact(value):
    return jax.nn.gelu(value, approximate=False)


def head_group():
    return 4


def grouped(value):
    width = head_group()
    return (
        value.reshape(value.shape[0], H, HD)
        .transpose(1, 0, 2)
        .reshape(H // width, width, value.shape[0], HD)
    )


def ungrouped(value):
    return value.reshape(H, value.shape[2], HD).transpose(1, 0, 2).reshape(value.shape[2], H * HD)


def attend_forward(query, keys, values, mask):

    def one_group(parts):
        q_group, k_group, v_group = parts
        scores = jnp.einsum("gtd,gsd->gts", q_group, k_group, preferred_element_type=jnp.float32)
        scores = jnp.where(mask[None], scores, -1e30)
        peak = jnp.max(scores, -1, keepdims=True)
        expo = jnp.exp(scores - peak)
        total = jnp.sum(expo, -1, keepdims=True)
        probs = (expo / total).astype(jnp.bfloat16)
        mixed = jnp.einsum("gts,gsd->gtd", probs, v_group, preferred_element_type=jnp.float32)
        return (mixed.astype(jnp.bfloat16), (peak + jnp.log(total))[..., 0])

    heads, summed = lax.map(one_group, (grouped(query), grouped(keys), grouped(values)))
    return (ungrouped(heads), summed)


def attend_backward(query, keys, values, summed, grad_out, mask):

    def one_group(parts):
        q_group, k_group, v_group, s_group, g_group = parts
        scores = jnp.einsum("gtd,gsd->gts", q_group, k_group, preferred_element_type=jnp.float32)
        probs = jnp.where(mask[None], jnp.exp(scores - s_group[..., None]), 0.0)
        grad_values = jnp.einsum(
            "gts,gtd->gsd", probs.astype(jnp.bfloat16), g_group, preferred_element_type=jnp.float32
        )
        grad_probs = jnp.einsum(
            "gtd,gsd->gts", g_group, v_group, preferred_element_type=jnp.float32
        )
        grad_scores = (
            probs * (grad_probs - jnp.sum(probs * grad_probs, -1, keepdims=True))
        ).astype(jnp.bfloat16)
        grad_query = jnp.einsum(
            "gts,gsd->gtd", grad_scores, k_group, preferred_element_type=jnp.float32
        ).astype(jnp.bfloat16)
        grad_keys = jnp.einsum(
            "gts,gtd->gsd", grad_scores, q_group, preferred_element_type=jnp.float32
        ).astype(jnp.bfloat16)
        return (grad_query, grad_keys, grad_values.astype(jnp.bfloat16))

    parts = (grouped(query), grouped(keys), grouped(values), summed, grouped(grad_out))
    grad_query, grad_keys, grad_values = lax.map(one_group, parts)
    return (ungrouped(grad_query), ungrouped(grad_keys), ungrouped(grad_values))


def make_masks(length, frames):
    place = jnp.arange(TOK)
    causal = (place[None, :] <= place[:, None]) & (place[None, :] < length)
    seen = jnp.broadcast_to(jnp.arange(FRAMES)[None, :] < frames, (TOK, FRAMES))
    return (place, causal, seen)


def clip_forward(weights, x_in, enc, length, frames):
    wa, wm, wv = weights
    vec = wv.astype(jnp.float32)
    scale = HD ** (-0.5)
    place, causal, seen = make_masks(length, frames)
    x = x_in.astype(jnp.float32)
    first = norm_apply(x, vec[0], vec[1]).astype(jnp.bfloat16)
    query = ((matmul(first, wa[0]) + vec[6]) * scale).astype(jnp.bfloat16)
    keys = matmul(first, wa[1]).astype(jnp.bfloat16)
    values = (matmul(first, wa[2]) + vec[7]).astype(jnp.bfloat16)
    mixed, summed_self = attend_forward(query, keys, values, causal)
    second_in = x + matmul(mixed, wa[3]) + vec[8]
    second = norm_apply(second_in, vec[2], vec[3]).astype(jnp.bfloat16)
    cross_query = ((matmul(second, wa[4]) + vec[9]) * scale).astype(jnp.bfloat16)
    cross_keys = matmul(enc, wa[5]).astype(jnp.bfloat16)
    cross_values = (matmul(enc, wa[6]) + vec[10]).astype(jnp.bfloat16)
    heard, summed_cross = attend_forward(cross_query, cross_keys, cross_values, seen)
    third_in = second_in + matmul(heard, wa[7]) + vec[11]
    third = norm_apply(third_in, vec[4], vec[5]).astype(jnp.bfloat16)
    hidden_pre = outer_last(third, wm[0]) + vec[13:].reshape(FF)
    hidden = gelu_exact(hidden_pre).astype(jnp.bfloat16)
    result = third_in + matmul(hidden, wm[1]) + vec[12]
    saved = (
        first,
        query,
        keys,
        values,
        mixed,
        summed_self,
        second_in,
        second,
        cross_query,
        cross_keys,
        cross_values,
        heard,
        summed_cross,
        third_in,
        third,
        hidden_pre,
        hidden,
    )
    return (result.astype(jnp.bfloat16), saved)


def clip_backward(weights, x_in, enc, length, frames, cot, saved):
    wa, wm, wv = weights
    vec = wv.astype(jnp.float32)
    scale = HD ** (-0.5)
    (
        first,
        query,
        keys,
        values,
        mixed,
        summed_self,
        second_in,
        second,
        cross_query,
        cross_keys,
        cross_values,
        heard,
        summed_cross,
        third_in,
        third,
        hidden_pre,
        hidden,
    ) = saved
    place, causal, seen = make_masks(length, frames)
    grad_y = cot.astype(jnp.float32) * (place < length).astype(jnp.float32)[:, None]
    out_three = grad_y.astype(jnp.bfloat16)
    g_down = inner_rows(hidden, out_three)
    g_b_down = jnp.sum(out_three.astype(jnp.float32), 0)
    grad_hidden = outer_last(out_three, wm[1])
    _, gelu_pull = jax.vjp(gelu_exact, hidden_pre)
    grad_pre = gelu_pull(grad_hidden)[0].astype(jnp.bfloat16)
    g_up = inner_rows(grad_pre, third)
    g_b_up = jnp.sum(grad_pre.astype(jnp.float32), 0)
    grad_third = matmul(grad_pre, wm[0])
    _, norm_pull = jax.vjp(norm_apply, third_in, vec[4], vec[5])
    part_three, g_gain_three, g_shift_three = norm_pull(grad_third)
    grad_third_in = grad_y + part_three
    out_two = grad_third_in.astype(jnp.bfloat16)
    g_cross_out = inner_rows(heard, out_two)
    g_b_cross_out = jnp.sum(out_two.astype(jnp.float32), 0)
    grad_heard = outer_last(out_two, wa[7]).astype(jnp.bfloat16)
    grad_cq, grad_ck, grad_cv = attend_backward(
        cross_query, cross_keys, cross_values, summed_cross, grad_heard, seen
    )
    grad_cq = grad_cq * scale
    g_cross_query = inner_rows(second, grad_cq)
    g_b_cross_query = jnp.sum(grad_cq.astype(jnp.float32), 0)
    g_cross_keys = inner_rows(enc, grad_ck)
    g_cross_values = inner_rows(enc, grad_cv)
    g_b_cross_values = jnp.sum(grad_cv.astype(jnp.float32), 0)
    grad_enc = outer_last(grad_ck, wa[5]) + outer_last(grad_cv, wa[6])
    grad_second = outer_last(grad_cq, wa[4])
    _, norm_pull = jax.vjp(norm_apply, second_in, vec[2], vec[3])
    part_two, g_gain_two, g_shift_two = norm_pull(grad_second)
    grad_second_in = grad_third_in + part_two
    out_one = grad_second_in.astype(jnp.bfloat16)
    g_self_out = inner_rows(mixed, out_one)
    g_b_self_out = jnp.sum(out_one.astype(jnp.float32), 0)
    grad_mixed = outer_last(out_one, wa[3]).astype(jnp.bfloat16)
    grad_q, grad_k, grad_v = attend_backward(query, keys, values, summed_self, grad_mixed, causal)
    grad_q = grad_q * scale
    g_self_query = inner_rows(first, grad_q)
    g_self_keys = inner_rows(first, grad_k)
    g_self_values = inner_rows(first, grad_v)
    g_b_self_query = jnp.sum(grad_q.astype(jnp.float32), 0)
    g_b_self_values = jnp.sum(grad_v.astype(jnp.float32), 0)
    grad_first = outer_last(grad_q, wa[0]) + outer_last(grad_k, wa[1]) + outer_last(grad_v, wa[2])
    _, norm_pull = jax.vjp(norm_apply, x_in.astype(jnp.float32), vec[0], vec[1])
    part_one, g_gain_one, g_shift_one = norm_pull(grad_first)
    grad_x = grad_second_in + part_one
    g_attn = jnp.stack(
        [
            g_self_query,
            g_self_keys,
            g_self_values,
            g_self_out,
            g_cross_query,
            g_cross_keys,
            g_cross_values,
            g_cross_out,
        ]
    )
    g_mlp = jnp.stack([g_up, g_down])
    g_vec = jnp.concatenate(
        [
            jnp.stack(
                [
                    g_gain_one,
                    g_shift_one,
                    g_gain_two,
                    g_shift_two,
                    g_gain_three,
                    g_shift_three,
                    g_b_self_query,
                    g_b_self_values,
                    g_b_self_out,
                    g_b_cross_query,
                    g_b_cross_values,
                    g_b_cross_out,
                    g_b_down,
                ]
            ),
            g_b_up.reshape(FF // D, D),
        ],
        0,
    )
    return ((g_attn, g_mlp, g_vec), grad_x, grad_enc)


def adam_update(weight, first, second, grad, rate):
    first_new = beta_first * first + (1.0 - beta_first) * grad
    second_new = beta_second * second + (1.0 - beta_second) * grad * grad
    ratio = (
        first_new
        / (1.0 - beta_first**STEP)
        / (jnp.sqrt(second_new / (1.0 - beta_second**STEP)) + adam_epsilon)
    )
    return (weight - rate * (ratio + weight_decay * weight), first_new, second_new)


def plain_body(
    tokens,
    enc_states,
    cotangent,
    tok_len,
    frame_count,
    attn_w,
    attn_m,
    attn_v,
    mlp_w,
    mlp_m,
    mlp_v,
    vec_w,
    vec_m,
    vec_v,
):
    shards = (attn_w.astype(jnp.bfloat16), mlp_w.astype(jnp.bfloat16), vec_w.astype(jnp.bfloat16))
    weights = (
        lax.all_gather(shards[0], ("dp", "fsdp"), axis=1, tiled=True),
        lax.all_gather(shards[1], ("dp", "fsdp"), axis=1, tiled=True),
        lax.all_gather(shards[2], ("dp", "fsdp"), axis=1, tiled=True),
    )

    def forward_one(items):
        x_in, enc, length, frames = items
        return clip_forward(weights, x_in, enc, length, frames)

    result, saved = lax.map(forward_one, (tokens, enc_states, tok_len, frame_count))
    back_weights = (
        lax.all_gather(shards[0], ("dp", "fsdp"), axis=1, tiled=True),
        lax.all_gather(shards[1], ("dp", "fsdp"), axis=1, tiled=True),
        lax.all_gather(shards[2], ("dp", "fsdp"), axis=1, tiled=True),
    )

    def backward_one(carry, items):
        x_in, enc, length, frames, cot, kept = items
        grads, grad_x, grad_enc = clip_backward(back_weights, x_in, enc, length, frames, cot, kept)
        return (jax.tree.map(jnp.add, carry, grads), (grad_x, grad_enc))

    zeros = (
        jnp.zeros(weights[0].shape, jnp.float32),
        jnp.zeros(weights[1].shape, jnp.float32),
        jnp.zeros(weights[2].shape, jnp.float32),
    )
    totals, (d_tokens, d_enc) = lax.scan(
        backward_one, zeros, (tokens, enc_states, tok_len, frame_count, cotangent, saved)
    )
    grad_attn, grad_mlp, grad_vec = (
        lax.psum_scatter(totals[0], ("dp", "fsdp"), scatter_dimension=1, tiled=True),
        lax.psum_scatter(totals[1], ("dp", "fsdp"), scatter_dimension=1, tiled=True),
        lax.psum_scatter(totals[2], ("dp", "fsdp"), scatter_dimension=1, tiled=True),
    )
    attn_new = adam_update(attn_w, attn_m, attn_v, grad_attn, rate_attention)
    mlp_new = adam_update(mlp_w, mlp_m, mlp_v, grad_mlp, rate_feedforward)
    vec_new = adam_update(vec_w, vec_m, vec_v, grad_vec, rate_vector)
    return (
        result,
        d_tokens,
        d_enc,
        attn_new[0],
        attn_new[1],
        attn_new[2],
        mlp_new[0],
        mlp_new[1],
        mlp_new[2],
        vec_new[0],
        vec_new[1],
        vec_new[2],
    )


def fused_body(tokens, enc_states, cotangent, tok_len, frame_count, attn_w, attn_m, attn_v, mlp_w, mlp_m, mlp_v, vec_w, vec_m, vec_v):
    out, d_tokens, d_enc, gsum, grad_vec = call_block(
        tok_len, frame_count, tokens[0], enc_states[0], cotangent[0], attn_w, mlp_w.reshape(8, ROWS, D), vec_w
    )
    attn_new = adam_update(attn_w, attn_m, attn_v, gsum[:8], rate_attention)
    mlp_new = adam_update(mlp_w, mlp_m, mlp_v, gsum[8:].reshape(mlp_w.shape), rate_feedforward)
    vec_new = adam_update(vec_w, vec_m, vec_v, grad_vec, rate_vector)
    return (out[None], d_tokens[None], d_enc.reshape(enc_states.shape), *attn_new, *mlp_new, *vec_new)


def solution(mesh):
    fused = mesh.shape["dp"] == DEPTH and mesh.shape["fsdp"] == 2 * PLANE
    return jax.shard_map(
        fused_body if fused else plain_body,
        mesh=mesh,
        in_specs=(
            P(("dp", "fsdp"), None, None),
            P(("dp", "fsdp"), None, None),
            P(("dp", "fsdp"), None, None),
            P(("dp", "fsdp")),
            P(("dp", "fsdp")),
            P(None, ("dp", "fsdp"), None),
            P(None, ("dp", "fsdp"), None),
            P(None, ("dp", "fsdp"), None),
            P(None, ("dp", "fsdp"), None),
            P(None, ("dp", "fsdp"), None),
            P(None, ("dp", "fsdp"), None),
            P(None, ("dp", "fsdp")),
            P(None, ("dp", "fsdp")),
            P(None, ("dp", "fsdp")),
        ),
        out_specs=(
            P(("dp", "fsdp"), None, None),
            P(("dp", "fsdp"), None, None),
            P(("dp", "fsdp"), None, None),
            P(None, ("dp", "fsdp"), None),
            P(None, ("dp", "fsdp"), None),
            P(None, ("dp", "fsdp"), None),
            P(None, ("dp", "fsdp"), None),
            P(None, ("dp", "fsdp"), None),
            P(None, ("dp", "fsdp"), None),
            P(None, ("dp", "fsdp")),
            P(None, ("dp", "fsdp")),
            P(None, ("dp", "fsdp")),
        ),
        check_vma=False,
    )
```

```python
import functools
import heapq
import jax
import jax.numpy as jnp
from jax import lax
from jax.experimental import pallas as pl
from jax.experimental.pallas import tpu as pltpu
from jax.sharding import PartitionSpec as P

D = 768
H = 12
HD = 64
FF = 3072
FRAMES = 1500
TOK = 448
STEP = 10
PADDED = 1536
ROWS = 24
PLANE = 4
DEPTH = 4
UNITS = 16
HALF = D // 2
BF = jnp.bfloat16
F32 = jnp.float32
MESH = pl.DeviceIdType.MESH
norm_epsilon = 1e-05
VMEM_LIMIT = 63 * 2**20


def dot(a, b):
    return lax.dot_general(a, b, (((1,), (0,)), ((), ())), preferred_element_type=F32)


def dot_nt(a, b):
    return lax.dot_general(a, b, (((1,), (1,)), ((), ())), preferred_element_type=F32)


def dot_tn(a, b):
    return lax.dot_general(a, b, (((0,), (0,)), ((), ())), preferred_element_type=F32)


def layer_norm(v, gain, shift):
    c = v - jnp.mean(v, -1, keepdims=True)
    s = jnp.mean(c * c, -1, keepdims=True)
    return c * lax.rsqrt(s + norm_epsilon) * gain + shift


def layer_norm_back(v, gain, grad):
    c = v - jnp.mean(v, -1, keepdims=True)
    r = lax.rsqrt(jnp.mean(c * c, -1, keepdims=True) + norm_epsilon)
    xh = c * r
    t = grad * gain
    dx = r * (t - jnp.mean(t, -1, keepdims=True) - xh * jnp.mean(t * xh, -1, keepdims=True))
    return dx, jnp.sum(grad * xh, 0, keepdims=True), jnp.sum(grad, 0, keepdims=True)


def gelu_both(u):
    z = jnp.abs(u) * 0.7071067811865476
    e = jnp.exp(-0.5 * u * u)
    t = 1.0 / (1.0 + 0.3275911 * z)
    poly = t * (0.254829592 + t * (-0.284496736 + t * (1.421413741 + t * (-1.453152027 + t * 1.061405429))))
    half = 0.5 * poly * e
    phi = jnp.where(u >= 0, 1.0 - half, half)
    return u * phi, phi + u * (e * 0.3989422804014327)


def colsum(v):
    return jnp.sum(v.astype(F32), 0, keepdims=True)


def head_lanes(rows, h):
    return (lax.broadcasted_iota(jnp.int32, (rows, 128), 1) // HD) == h


class Place:
    def __init__(self):
        self.z = lax.axis_index("dp")
        f = lax.axis_index("fsdp")
        self.f = f
        self.c = f % 2
        self.p = f // 2
        x, y = self.p % 2, self.p // 2
        self.part = f + 1 - 2 * self.c
        fx, fy = f + 2 - 4 * x, f + 4 - 8 * y
        px, py = self.p + 1 - 2 * x, self.p + 2 - 4 * y
        c = self.c
        self.n1, self.n2 = fx + c * (fy - fx), fy + c * (fx - fy)
        self.p1, self.p2, self.p3 = px + c * (py - px), py + c * (px - py), 3 - self.p
        self.zto = [(self.z + d) % DEPTH for d in range(1, DEPTH)]
        self.zfrom = [(self.z + DEPTH - d) % DEPTH for d in range(1, DEPTH)]
        self.own = pl.ds(pl.multiple_of(c * HALF, 128), HALF)
        self.other = pl.ds(pl.multiple_of(HALF - c * HALF, 128), HALF)

    def greet(self):
        barrier = pltpu.get_barrier_semaphore()
        others = [(zz, self.f) for zz in self.zto]
        others += [(self.z, self.n1), (self.z, self.n2), (self.z, self.part)]
        for device in others:
            pl.semaphore_signal(barrier, inc=1, device_id=device, device_id_type=MESH)
        pl.semaphore_wait(barrier, len(others))


def remote(src, dst, send, recv, device):
    return pltpu.make_async_remote_copy(
        src_ref=src, dst_ref=dst, send_sem=send, recv_sem=recv, device_id=device, device_id_type=MESH
    )


class Gather:
    def __init__(self, place, view, send, recv):
        self.w, self.view, self.send, self.recv = place, view, send, recv

    def copy(self, k, ref, device):
        return remote(ref, ref, self.send(k), self.recv(k), device)

    def own(self, zz, p):
        return self.view(zz, p, True)

    def s1(self):
        w = self.w
        for i, zz in enumerate(w.zto):
            self.copy(i, self.own(w.z, w.p), (zz, w.f)).start()

    def s2(self):
        w = self.w
        for i, zz in enumerate(w.zfrom):
            self.copy(i, self.own(zz, w.p), (zz, w.f)).wait_recv()
        self.copy(3, self.own(None, w.p), (w.z, w.n1)).start()
        self.copy(4, self.own(None, w.p), (w.z, w.n2)).start()
        self.copy(6, self.own(None, w.p), (w.z, w.part)).start()

    def s3(self):
        w = self.w
        self.copy(3, self.own(None, w.p1), (w.z, w.n1)).wait_recv()
        self.copy(5, self.own(None, w.p1), (w.z, w.n2)).start()
        self.copy(7, self.own(None, w.p1), (w.z, w.part)).start()

    def s4(self):
        w = self.w
        self.copy(4, self.own(None, w.p2), (w.z, w.n2)).wait_recv()
        self.copy(8, self.own(None, w.p2), (w.z, w.part)).start()

    def s5(self):
        w = self.w
        self.copy(5, self.own(None, w.p3), (w.z, w.n2)).wait_recv()
        self.copy(9, self.own(None, w.p3), (w.z, w.part)).start()

    def ready(self):
        w = self.w
        for k, p in enumerate((w.p, w.p1, w.p2, w.p3)):
            self.copy(6 + k, self.view(None, p, False), (w.z, w.part)).wait_recv()

    def drain(self):
        w = self.w
        for i, zz in enumerate(w.zto):
            self.copy(i, self.own(w.z, w.p), (zz, w.f)).wait_send()
        for k, p in ((3, w.p), (4, w.p), (5, w.p1), (6, w.p), (7, w.p1), (8, w.p2), (9, w.p3)):
            self.copy(k, self.own(None, p), (w.z, w.n1)).wait_send()


def heads_forward(q_ref, k_ref, v_ref, o_ref, lse_ref, mask_fn, keys, tile, first, count):
    def pair(hp, _):
        lanes = pl.ds(pl.multiple_of(hp * 128, 128), 128)
        kp, vp = k_ref[:keys, lanes], v_ref[:keys, lanes]
        for i in range(TOK // tile):
            rows = pl.ds(i * tile, tile)
            qp = q_ref[rows, lanes]
            outs = []
            sums = lse_ref[rows, :]
            for h in range(2):
                s = dot_nt(jnp.where(head_lanes(tile, h), qp, jnp.zeros_like(qp)), kp)
                s = mask_fn(s, i)
                peak = jnp.max(s, -1, keepdims=True)
                expo = jnp.exp(s - peak)
                total = jnp.sum(expo, -1, keepdims=True)
                outs.append(dot(expo.astype(BF), vp) * (1.0 / total))
                lane = lax.broadcasted_iota(jnp.int32, (tile, 128), 1)
                sums = jnp.where(lane == hp * 2 + h, peak + jnp.log(total), sums)
            lse_ref[rows, :] = sums
            o_ref[rows, lanes] = jnp.where(head_lanes(tile, 0), outs[0], outs[1]).astype(BF)
        return 0

    lax.fori_loop(first, first + count, pair, 0)


def thirds(f):
    for j in range(3):
        f(pl.ds(j * 256, 256))


class Reduce:
    def __init__(self, place, local, r0, r1, r2, r3, send, recv, source, low, finish):
        self.w, self.local, self.r0, self.r1, self.r2, self.r3 = place, local, r0, r1, r2, r3
        self.send, self.recv, self.source, self.low, self.finish = send, recv, source, low, finish

    def copy(self, k, src, dst, device):
        return remote(src, dst, self.send(k), self.recv(k), device)

    def copies(self, stage):
        w, r0 = self.w, self.r0
        if stage == 0:
            return [self.copy(0, self.source, r0, (w.z, w.part))]
        if stage == 1:
            return [
                self.copy(1, r0.at[:, w.p2], self.r1.at[:, 0], (w.z, w.n2)),
                self.copy(2, r0.at[:, w.p3], self.r1.at[:, 1], (w.z, w.n2)),
            ]
        if stage == 2:
            return [self.copy(3, r0.at[:, w.p1], self.r2, (w.z, w.n1))]
        return [self.copy(4 + i, r0.at[zz, w.p], self.r3.at[i], (zz, w.f)) for i, zz in enumerate(w.zto)]

    def e0(self):
        for c in self.copies(0):
            c.start()

    def arrived(self, stage):
        for c in self.copies(stage):
            c.wait_recv()

    def e1(self):
        w = self.w
        self.arrived(0)
        for p in (w.p2, w.p3):
            self.r0[:, p] = (self.local(slice(None), p) + self.r0[:, p].astype(F32)).astype(self.low)
        for c in self.copies(1):
            c.start()

    def e2(self):
        w = self.w
        self.arrived(1)
        total = self.local(slice(None), w.p1) + self.r0[:, w.p1].astype(F32) + self.r1[:, 1].astype(F32)
        self.r0[:, w.p1] = total.astype(self.low)
        for c in self.copies(2):
            c.start()

    def partial(self, zz):
        w = self.w
        return (
            self.local(zz, w.p) + self.r0[zz, w.p].astype(F32) + self.r1[zz, 0].astype(F32) + self.r2[zz].astype(F32)
        )

    def e3(self, keep):
        w = self.w
        self.arrived(2)
        keep[...] = self.partial(w.z)
        for zz in w.zto:
            self.r0[zz, w.p] = self.partial(zz).astype(self.low)
        for c in self.copies(3):
            c.start()

    def e4(self, keep):
        self.arrived(3)
        self.finish(keep[...] + (self.r3[0].astype(F32) + self.r3[1].astype(F32) + self.r3[2].astype(F32)))

    def sent(self):
        for stage in range(4):
            for c in self.copies(stage):
                c.wait_send()


def head_delta(grad, mixed):
    product = grad.astype(F32) * mixed.astype(F32)
    high = product.astype(BF)
    low = (product - high.astype(F32)).astype(BF)
    pick = lax.broadcasted_iota(jnp.int32, (16, D), 1) // HD == lax.broadcasted_iota(jnp.int32, (16, D), 0)
    pick = pick.astype(F32).astype(BF)
    return dot_nt(pick, high) + dot_nt(pick, low)


def heads_backward(q_ref, k_ref, v_ref, g_ref, lse_ref, delta_ref, mask_fn, keys, tile, acc, first, count):
    def pair(hp, _):
        lanes = pl.ds(pl.multiple_of(hp * 128, 128), 128)
        qp, gp = q_ref[:, lanes], g_ref[:, lanes]
        zero = jnp.zeros_like(qp)
        qs = [jnp.where(head_lanes(TOK, h), qp, zero) for h in range(2)]
        gs = [jnp.where(head_lanes(TOK, h), gp, zero) for h in range(2)]
        lse = [lse_ref[pl.ds(hp * 2 + h, 1), :] for h in range(2)]
        delta = [delta_ref[pl.ds(hp * 2 + h, 1), :] for h in range(2)]
        for i in range(keys // tile):
            rows = pl.ds(i * tile, tile)
            kp, vp = k_ref[rows, lanes], v_ref[rows, lanes]
            ps, ds = [], []
            for h in range(2):
                p = jnp.exp(mask_fn(dot_nt(kp, qs[h]), i) - lse[h])
                ds.append((p * (dot_nt(vp, gs[h]) - delta[h])).astype(BF))
                ps.append(p.astype(BF))
            dv = dot(ps[0], gs[0]) + dot(ps[1], gs[1])
            dk = dot(ds[0], qs[0]) + dot(ds[1], qs[1])
            v_ref[rows, lanes] = dv.astype(BF)
            k_ref[rows, lanes] = dk.astype(BF)
            a = jnp.where(head_lanes(TOK, 0), dot_tn(ds[0], kp), dot_tn(ds[1], kp))
            if i == 0:
                acc[...] = a
            else:
                acc[...] += a
        q_ref[:, lanes] = (acc[...].astype(BF).astype(F32) * 0.125).astype(BF)
        return 0

    lax.fori_loop(first, first + count, pair, 0)


class Plan:
    def __init__(self):
        self.now, self.queue, self.count = 0.0, [], 0

    def at(self, time, event, cost=0.15):
        heapq.heappush(self.queue, (time, self.count, event, cost))
        self.count += 1

    def step(self):
        time, _, event, cost = heapq.heappop(self.queue)
        self.now = max(self.now, time) + cost
        event()

    def until(self, time):
        while self.queue and self.queue[0][0] <= time:
            self.step()
        self.now = max(self.now, time)

    def work(self, cost, compute):
        self.until(self.now)
        compute()
        self.now += cost

    def thirds(self, cost, compute):
        for j in range(3):
            self.work(cost / 3, lambda: compute(pl.ds(j * 256, 256)))


PACE = 5.0
FIRST = 9.0
AHEAD = 3.0
HOP1, HOP2, LAND = 4.0, 9.05, 11.0
SUM_START = 84.0
SUM_PACE = 5.0
SUM_HOPS = (9.0, 7.0, 5.0, 4.0)


ORDER = [5, 6, 0, 1, 2, 3, 4, 7, 8, 12, 9, 13, 10, 14, 11, 15]
A1, Q, K, V_, O, A2, CQ, O2, A3 = range(9)
DO = A3
SLOTS = 8
SUMS = [(12, 12), (8, 8), (13, 13), (9, 9), (14, 14), (10, 10), (15, 15), (11, 11), (7, 7), (4, 4), (5, 12), (6, 8), (3, 3), (0, 0), (1, 1), (2, 2)]


def block_kernel(
    len_ref, frames_ref, x_hbm, enc_hbm, cot_hbm, attn_hbm, mlp_hbm, vec_hbm,
    out_hbm, dtok_hbm, denc_hbm, gsum_hbm, gvsum_hbm,
    weights, vgather, stage, r0, r1, r2, r3, vr0, vr1, vr2, vr3, vkeep, vsmall, vpad,
    enc, cot, act, kv, lse, delta, xs, hm, gp, oacc, dacc, denc, vec, gv,
    load_sem, stage_sem, send_sem, recv_sem, vsend_sem, vrecv_sem, rsend_sem, rrecv_sem, credit, store_sem, denc_sem, own_sem,
):
    w = Place()
    length, frames = len_ref[0], frames_ref[0]
    x_ref, lse_cols, acc = hm, dacc.at[:, :128], xs.at[1, :, :128]
    local = lambda src, dst, sem: pltpu.make_async_copy(src, dst, sem)
    loads = [
        local(attn_hbm.at[:, :, w.own], stage.at[pl.ds(0, 8), w.c], load_sem.at[0]),
        local(mlp_hbm.at[:, :, w.own], stage.at[pl.ds(8, 8), w.c], load_sem.at[1]),
        local(vec_hbm, vsmall, load_sem.at[2]),
        local(x_hbm, x_ref, load_sem.at[3]),
        local(enc_hbm, enc, load_sem.at[4]),
        local(cot_hbm, cot, load_sem.at[5]),
    ]
    for i in (2, 0, 1, 3, 4, 5):
        loads[i].start()
    nv, nc = vsmall.shape
    vpad[...] = jnp.zeros_like(vpad)
    loads[2].wait()
    vpad[:nv, :nc] = vsmall[...]
    vgather[w.z, w.p, w.c] = jnp.transpose(vpad[...])[:ROWS]
    w.greet()

    def unit_view(u):
        def view(zz, p, own):
            return weights.at[u, slice(None) if zz is None else zz, p, :, w.own if own else w.other]

        return view

    def vec_view(zz, p, own):
        return vgather.at[slice(None) if zz is None else zz, p, w.c if own else 1 - w.c]

    units = [Gather(w, unit_view(u), lambda k, u=u: send_sem.at[u, k], lambda k, u=u: recv_sem.at[u, k]) for u in ORDER]
    by_weight = {u: units[i] for i, u in enumerate(ORDER)}
    vecs = Gather(w, vec_view, lambda k: vsend_sem.at[0, k], lambda k: vrecv_sem.at[0, k])

    plan = Plan()
    vecs.s1()
    parts = ((5, 2, attn_hbm, 5), (0, 5, attn_hbm, 0), (7, 1, attn_hbm, 7), (8, 8, mlp_hbm, 0))
    swaps = []
    for i, (u0, n, src, at) in enumerate(parts):
        src = src.at[pl.ds(at, n), :, w.other]
        swaps.append(remote(src, stage.at[pl.ds(u0, n), w.c], stage_sem.at[0, i], stage_sem.at[1, i], (w.z, w.part)))
        swaps[i].start()
    loads[0].wait()
    loads[1].wait()
    arrived = set()

    def start_unit(i):
        u = ORDER[i]
        k = 0 if u in (5, 6) else 1 if u < 5 else 2 if u == 7 else 3
        if k not in arrived:
            swaps[k].wait_recv()
            arrived.add(k)
        weights[u, w.z, w.p, :, w.own] = stage[u].reshape(2 * ROWS, HALF).astype(BF)
        units[i].s1()

    def first_hop(i):
        units[i].s3()
        units[i].s4()

    for i in range(UNITS):
        begin = FIRST + PACE * i
        plan.at(begin - AHEAD - PACE - 0.2 if i > 2 else 0.0, functools.partial(start_unit, i))
        plan.at(begin - AHEAD, units[i].s2)
        plan.at(begin + HOP1, functools.partial(first_hop, i))
        plan.at(begin + HOP2, units[i].s5)
    plan.at(FIRST - AHEAD + 0.05, vecs.s2)

    def vec_hop():
        vecs.s3()
        vecs.s4()

    plan.at(FIRST - AHEAD + PACE + 0.05, vec_hop)
    plan.at(FIRST - AHEAD + 2 * PACE + 0.05, vecs.s5)

    def ready(i):
        plan.until(FIRST + PACE * i + LAND)
        units[i].ready()

    def keep_of(u):
        class Keep:
            def __getitem__(self, _):
                return stage[u].reshape(2 * ROWS, HALF)

            def __setitem__(self, _, value):
                stage[u] = value.reshape(2, ROWS, HALF)

        return Keep()

    def final_swap(u):
        return remote(stage.at[u, 1 - w.c], gsum_hbm.at[u, :, w.own], rsend_sem.at[u, 7], rrecv_sem.at[u, 7], (w.z, w.part))

    def final_own(u):
        return local(stage.at[u, w.c], gsum_hbm.at[u, :, w.own], own_sem.at[u])

    def final_wait(u):
        ref = gsum_hbm.at[u, :, w.other]
        remote(ref, ref, rsend_sem.at[u, 7], rrecv_sem.at[u, 7], (w.z, w.part)).wait_recv()

    sums = []
    for r, (u, at) in enumerate(SUMS):

        def own_grad(zz, p, at=at):
            return weights[at, zz, p, :, w.own].astype(F32)

        def finish(total, u=u):
            stage[u] = total.reshape(2, ROWS, HALF)
            final_swap(u).start()
            final_own(u).start()

        sums.append(
            Reduce(
                w, own_grad, r0.at[r % SLOTS], r1.at[u], r2.at[u], r3.at[u],
                lambda k, u=u: rsend_sem.at[u, k], lambda k, u=u: rrecv_sem.at[u, k],
                weights.at[at, :, :, :, w.other], BF, finish,
            )
        )

    def vfinish(total):
        vkeep[...] = total

    vsums = Reduce(
        w, lambda zz, p: vgather[zz, p, w.c], vr0, vr1, vr2, vr3, lambda k: vsend_sem.at[1, k], lambda k: vrecv_sem.at[1, k],
        vgather.at[:, :, 1 - w.c], F32, vfinish,
    )

    recycled = set()
    sums_begin = [SUM_START]

    def launch(r):
        if r >= SLOTS:
            while r - SLOTS not in recycled:
                plan.step()
            pl.semaphore_wait(credit, 1)
        sums[r].e0()
        begin = max(plan.now + 2.0, sums_begin[0])
        sums_begin[0] = begin + SUM_PACE
        u = SUMS[r][0]

        def recycle():
            sums[r].e4(keep_of(u))
            if r < UNITS - SLOTS:
                sums[r].sent()
                pl.semaphore_signal(credit, inc=1, device_id=(w.z, w.part), device_id_type=MESH)
                recycled.add(r)

        steps = (sums[r].e1, sums[r].e2, lambda: sums[r].e3(keep_of(u)), recycle, lambda: final_wait(u))
        for k, event in enumerate(steps):
            plan.at(begin + sum(SUM_HOPS[:k]), event, 0.3)

    stores = []

    def store(src, dst):
        c = local(src, dst, store_sem.at[len(stores)])
        c.start()
        stores.append(c)

    def wcols(u, cols):
        return weights[u, :, :, :, cols].reshape(D, cols.size)

    def wrows(u, rows):
        return weights.at[u].reshape(D, D)[rows, :]

    def weight_grad(at, a, b):
        def cols(cs):
            weights[at, :, :, :, cs] = dot_tn(a(), b(cs)).astype(BF).reshape(DEPTH, PLANE, 2 * ROWS, 256)

        thirds(cols)

    vrow = lambda r, cols=slice(None): vec[r : r + 1, cols]

    lse_cols[...] = jnp.zeros((TOK, 128), F32)
    kv[:, FRAMES // 16 * 16 :, :] = jnp.zeros((2, PADDED - FRAMES // 16 * 16, D), BF)
    loads[4].wait()

    def enc_project(u, which, bias, a, b):
        def cols(cs):
            r = dot(enc[a:b, :], wcols(u, cs))
            if bias is not None:
                r = r + vrow(bias, cs)
            kv[which, a:b, cs] = r.astype(BF)

        thirds(cols)

    parts = ((0, 512), (512, 1024), (1024, FRAMES))
    ready(0)
    for a, b in parts:
        plan.work(0.95, functools.partial(enc_project, 5, 0, None, a, b))
    vecs.ready()
    table = vgather[...].reshape(D, 128).astype(BF).astype(F32)
    vec[...] = jnp.transpose(table)[:24, :]
    lane = lax.broadcasted_iota(jnp.int32, (ROWS, 128), 1)
    source = lax.broadcasted_iota(jnp.int32, (128, 128), 0)
    spread = [dot(table.astype(BF), (source == 13 + a).astype(F32).astype(BF)) for a in range(4)]
    blocks = []
    for chip in range(16):
        for core in range(2):
            block = jnp.zeros((ROWS, 128), F32)
            for j in range(4):
                at = (chip % 4) * 192 + core * 96 + j * ROWS
                block = jnp.where(lane == j, spread[chip // 4][at : at + ROWS], block)
            blocks.append(block)
    vec[16:24, :] = jnp.transpose(jnp.concatenate(blocks, 0))[:8, :]
    loads[3].wait()
    act[A1] = layer_norm(x_ref[...].astype(F32), vrow(0), vrow(1)).astype(BF)
    plan.now += 3.0
    ready(1)
    for a, b in parts:
        plan.work(0.95, functools.partial(enc_project, 6, 1, 10, a, b))

    def project(src, u, dst, bias, scale):
        def cols(cs):
            r = dot(act[src], wcols(u, cs))
            if bias is not None:
                r = r + vrow(bias, cs)
            act[dst, :, cs] = (r * scale).astype(BF)

        thirds(cols)

    for i, args in ((2, (A1, 0, Q, 6, 0.125)), (3, (A1, 1, K, None, 1.0)), (4, (A1, 2, V_, 7, 1.0))):
        ready(i)
        plan.work(0.75, functools.partial(project, *args))

    def self_mask(s, i):
        r = lax.broadcasted_iota(jnp.int32, s.shape, 0) + i * s.shape[0]
        c = lax.broadcasted_iota(jnp.int32, s.shape, 1)
        return jnp.where((c <= r) & (c < length), s, -1e30)

    def cross_mask(s, i):
        c = lax.broadcasted_iota(jnp.int32, (1, PADDED - 640), 1) + 640
        return jnp.concatenate([s[:, :640], jnp.where(c < frames, s[:, 640:], -1e30)], axis=1)

    def self_pairs(i):
        heads_forward(act.at[Q], act.at[K], act.at[V_], act.at[O], lse_cols, self_mask, TOK, 448, 2 * i, 2)

    for i in range(3):
        plan.work(2.1, functools.partial(self_pairs, i))
    lse[0] = jnp.transpose(lse_cols[...])[:16, :]
    ready(5)

    def residual(src, base, u, dst, bias):
        def cols(cs):
            xs[dst, :, cs] = base(cs) + dot(act[src], wcols(u, cs)) + vrow(bias, cs)

        thirds(cols)

    def norm(src, dst, row):
        act[dst] = layer_norm(xs[src], vrow(row), vrow(row + 1)).astype(BF)

    plan.work(0.8, lambda: residual(O, lambda cs: x_ref[:, cs].astype(F32), 3, 0, 8))
    plan.work(0.8, lambda: norm(0, A2, 2))
    ready(6)
    plan.work(0.7, lambda: project(A2, 4, CQ, 9, 0.125))

    def cross_pair(i):
        heads_forward(act.at[CQ], kv.at[0], kv.at[1], act.at[O2], lse_cols, cross_mask, PADDED, 224, i, 1)

    for i in range(6):
        plan.work(2.55, functools.partial(cross_pair, i))
    ready(7)
    plan.work(0.8, lambda: residual(O2, lambda cs: xs[0, :, cs], 7, 1, 11))
    plan.work(0.8, lambda: norm(1, A3, 4))
    lse[1] = jnp.transpose(lse_cols[...])[:16, :]
    loads[5].wait()
    ok = lax.broadcasted_iota(jnp.int32, (TOK, 1), 0) < length
    cot[...] = jnp.where(ok, cot[...], jnp.zeros((TOK, D), BF))
    gv[...] = jnp.zeros_like(gv)
    gv[12:13, :] = colsum(cot[...])
    oacc[...] = jnp.zeros_like(oacc)
    dacc[...] = jnp.zeros_like(dacc)
    for j in range(4):
        ready(8 + 2 * j)

        def hidden(rs):
            u = dot_nt(act[A3], wrows(8 + j, rs)) + vec[16 + j : 17 + j, rs]
            g, d = gelu_both(u)
            hm[:, rs] = g.astype(BF)
            gp[:, rs] = d.astype(BF)

        plan.thirds(2.1, hidden)
        ready(9 + 2 * j)

        def down(rs):
            oacc[:, rs] += dot(hm[...], wcols(12 + j, rs))
            d = (dot_nt(cot[...], wrows(12 + j, rs)) * gp[:, rs].astype(F32)).astype(BF)
            gp[:, rs] = d
            gv[13 + j : 14 + j, rs] = colsum(d)

        plan.thirds(1.7, down)

        def back(rs):
            dacc[:, rs] += dot(gp[...], wcols(8 + j, rs))

        plan.work(0.9, lambda: thirds(back))
        by_weight[12 + j].drain()
        plan.work(0.85, lambda: weight_grad(12 + j, lambda: hm[...], lambda cs: cot[:, cs]))
        launch(2 * j)
        by_weight[8 + j].drain()
        plan.work(0.85, lambda: weight_grad(8 + j, lambda: gp[...], lambda cs: act[A3, :, cs]))
        launch(2 * j + 1)
    hm[...] = (xs[1] + oacc[...] + vrow(12)).astype(BF)
    store(hm, out_hbm)
    again = local(x_hbm, gp, load_sem.at[3])
    again.start()
    dx = oacc
    dpart, gg, gb = layer_norm_back(xs[1], vrow(4), dacc[...])
    gv[4:5, :] = gg
    gv[5:6, :] = gb
    dx[...] = cot[...].astype(F32) + dpart
    dr = cot
    dr[...] = dx[...].astype(BF)
    plan.now += 2.0

    def times_output(u):
        def cols(cs):
            act[DO, :, cs] = dot_nt(dr[...], wrows(u, cs)).astype(BF)

        thirds(cols)

    plan.work(0.7, lambda: times_output(7))
    by_weight[7].drain()
    plan.work(0.7, lambda: weight_grad(7, lambda: act[O2], lambda cs: dr[:, cs]))
    launch(8)
    plan.now += 1.0
    delta[...] = head_delta(act[DO], act[O2])
    gv[11:12, :] = colsum(dr[...])

    def cross_mask_t(s, i):
        n = s.shape[0]
        if (i + 1) * n <= 750:
            return s
        f = lax.broadcasted_iota(jnp.int32, (n, 1), 0) + i * n
        return s + jnp.where(f < frames, 0.0, -1e30)

    def self_mask_t(s, i):
        r = lax.broadcasted_iota(jnp.int32, s.shape, 0) + i * s.shape[0]
        c = lax.broadcasted_iota(jnp.int32, s.shape, 1)
        return jnp.where((r <= c) & (r < length), s, -1e30)

    def cross_pair_back(i):
        heads_backward(
            act.at[CQ], kv.at[0], kv.at[1], act.at[DO], lse.at[1], delta, cross_mask_t, PADDED, 256, acc, i, 1
        )

    for i in range(6):
        plan.work(3.9, functools.partial(cross_pair_back, i))

    def times_back(pairs):
        def cols(cs):
            total = 0.0
            for a, u in pairs:
                total = total + dot_nt(act[a], wrows(u, cs))
            dacc[:, cs] = total

        thirds(cols)

    plan.work(0.7, lambda: times_back(((CQ, 4),)))
    by_weight[4].drain()
    plan.work(0.7, lambda: weight_grad(4, lambda: act[A2], lambda cs: act[CQ, :, cs]))
    launch(9)
    while not recycled >= {0, 1}:
        plan.step()
    plan.work(2.0, lambda: weight_grad(12, lambda: enc[...], lambda cs: kv[0, :FRAMES, cs]))
    launch(10)
    plan.work(2.0, lambda: weight_grad(8, lambda: enc[...], lambda cs: kv[1, :FRAMES, cs]))
    launch(11)
    gv[9:10, :] = colsum(act[CQ])
    gv[10:11, :] = colsum(kv[1])
    dpart, gg, gb = layer_norm_back(xs[0], vrow(2), dacc[...])
    gv[2:3, :] = gg
    gv[3:4, :] = gb
    dx[...] += dpart
    dr[...] = dx[...].astype(BF)
    gv[8:9, :] = colsum(dr[...])
    plan.now += 2.0
    plan.work(0.7, lambda: times_output(3))
    by_weight[3].drain()
    plan.work(0.7, lambda: weight_grad(3, lambda: act[O], lambda cs: dr[:, cs]))
    launch(12)
    delta[...] = head_delta(act[DO], act[O])
    plan.now += 0.5
    def self_pairs_back(i):
        heads_backward(
            act.at[Q], act.at[K], act.at[V_], act.at[DO], lse.at[0], delta, self_mask_t, TOK, 224, acc, 2 * i, 2
        )

    for i in range(3):
        plan.work(2.4, functools.partial(self_pairs_back, i))
    plan.work(1.8, lambda: times_back(((Q, 0), (K, 1), (V_, 2))))
    for r, a in ((13, Q), (14, K), (15, V_)):
        u = SUMS[r][0]
        by_weight[u].drain()
        plan.work(0.7, lambda: weight_grad(u, lambda: act[A1], lambda cs, a=a: act[a, :, cs]))
        launch(r)
    gv[6:7, :] = colsum(act[Q])
    gv[7:8, :] = colsum(act[V_])
    again.wait()
    dpart, gg, gb = layer_norm_back(gp[...].astype(F32), vrow(0), dacc[...])
    gv[0:1, :] = gg
    gv[1:2, :] = gb
    dx[...] += dpart
    store(dx, dtok_hbm)
    vecs.drain()
    table = jnp.transpose(jnp.concatenate([gv[...], jnp.zeros((104, D), F32)], 0))
    high = table.astype(BF)
    rest = table - high.astype(F32)
    mid = rest.astype(BF)
    low = (rest - mid.astype(F32)).astype(BF)
    spread = []
    for j in range(4):
        pick = (source == 13 + j).astype(F32).astype(BF)
        spread.append(dot(high, pick) + (dot(mid, pick) + dot(low, pick)))
    for b in range(4):
        for core in range(2):
            for j in range(4):
                at = b * 192 + core * 96 + j * ROWS
                block = jnp.where(lane < 13, table[at : at + ROWS], 0.0)
                for a in range(4):
                    src = (4 * a + b) * 48 + core * ROWS
                    block = jnp.where(lane == 13 + a, spread[j][src : src + ROWS], block)
                n = at // ROWS
                vgather[n // 8, n // 2 % 4, n % 2] = block
    plan.now += 4.0
    vsums.e0()
    for k, event in enumerate((vsums.e1, vsums.e2, lambda: vsums.e3(vkeep), lambda: vsums.e4(vkeep))):
        plan.at(plan.now + 2.0 + 3.5 * k, event, 0.3)

    chunks = [(a, min(a + 128, FRAMES)) for a in range(0, FRAMES, 128)]
    outs = {}

    def encoder_chunk(i):
        a, b = chunks[i]
        if i >= 2:
            outs[i - 2].wait()
        for k in range(3):
            cs = pl.ds(k * 256, 256)
            v = dot_nt(kv[0, a:b], wrows(5, cs)) + dot_nt(kv[1, a:b], wrows(6, cs))
            for h in range(2):
                denc[i % 2, pl.ds(2 * k + h, b - a, stride=6), :] = v[:, h * 128 : (h + 1) * 128]
        c = local(denc.at[i % 2, pl.ds(0, 6 * (b - a))], denc_hbm.at[pl.ds(6 * a, 6 * (b - a))], denc_sem.at[i % 2])
        c.start()
        outs[i] = c

    for i in range(len(chunks)):
        plan.work(0.45, functools.partial(encoder_chunk, i))
    while plan.queue:
        plan.step()
    vpad[:ROWS, :] = vkeep[...]
    vsmall[...] = jnp.transpose(vpad[...])[:nv, :nc]
    store(vsmall, gvsum_hbm)
    for c in swaps:
        c.wait_send()
    for u in (5, 6):
        by_weight[u].drain()
    for r, (u, _) in enumerate(SUMS):
        if r >= UNITS - SLOTS:
            sums[r].sent()
        final_swap(u).wait_send()
        final_own(u).wait()
    vsums.sent()
    outs[10].wait()
    outs[11].wait()
    for c in stores:
        c.wait()


def call_block(length, frames, x, enc, cot, attn_w, mlp_w, vec_w):
    any_ = pl.BlockSpec(memory_space=pl.ANY)
    smem = pl.BlockSpec(memory_space=pltpu.SMEM)
    t = lambda *s, dt=F32: jax.ShapeDtypeStruct(s, dt)
    v = pltpu.VMEM
    dma = pltpu.SemaphoreType.DMA
    n, rows = DEPTH, 2 * ROWS
    return pl.pallas_call(
        block_kernel,
        out_shape=[t(TOK, D, dt=BF), t(TOK, D), t(FRAMES * 6, 128), t(UNITS, ROWS, D), t(*vec_w.shape)],
        in_specs=[smem, smem] + [any_] * 6,
        out_specs=[any_] * 5,
        scratch_shapes=[
            v((UNITS, n, PLANE, rows, D), BF), v((n, PLANE, 2, ROWS, 128), F32), v((UNITS, 2, ROWS, HALF), F32),
            v((SLOTS, n, PLANE, rows, HALF), BF), v((UNITS, n, 2, rows, HALF), BF), v((UNITS, n, rows, HALF), BF),
            v((UNITS, 3, rows, HALF), BF),
            v((n, PLANE, ROWS, 128), F32), v((n, 2, ROWS, 128), F32), v((n, ROWS, 128), F32), v((3, ROWS, 128), F32),
            v((ROWS, 128), F32), v(vec_w.shape, F32), v((128, 128), F32),
            v((FRAMES, D), BF), v((TOK, D), BF), v((9, TOK, D), BF), v((2, PADDED, D), BF),
            v((2, 16, TOK), F32), v((16, TOK), F32), v((2, TOK, D), F32),
            v((TOK, D), BF), v((TOK, D), BF), v((TOK, D), F32), v((TOK, D), F32),
            v((2, 128 * 6, 128), F32), v((24, D), F32), v((24, D), F32),
            dma((6,)), dma((2, 4)), dma((UNITS, 10)), dma((UNITS, 10)), dma((2, 10)), dma((2, 10)),
            dma((UNITS, 8)), dma((UNITS, 8)), pltpu.SemaphoreType.REGULAR, dma((4,)), dma((2,)), dma((UNITS,)),
        ],
        compiler_params=pltpu.CompilerParams(collective_id=0, has_side_effects=True, vmem_limit_bytes=VMEM_LIMIT),
        name="block",
    )(length, frames, x, enc, cot, attn_w, mlp_w, vec_w)


beta_first = 0.9
beta_second = 0.999
adam_epsilon = 1e-08
weight_decay = 0.01
rate_attention = 0.06
rate_feedforward = 0.03
rate_vector = 0.35


def matmul(left, right):
    return jnp.dot(left, right, preferred_element_type=jnp.float32)


def inner_rows(left, right):
    return lax.dot_general(
        left, right, (((0,), (0,)), ((), ())), preferred_element_type=jnp.float32
    )


def outer_last(left, right):
    return lax.dot_general(
        left, right, (((1,), (1,)), ((), ())), preferred_element_type=jnp.float32
    )


def norm_apply(value, gain, shift):
    center = value - jnp.mean(value, -1, keepdims=True)
    spread = jnp.mean(center * center, -1, keepdims=True)
    return center * lax.rsqrt(spread + norm_epsilon) * gain + shift


def gelu_exact(value):
    return jax.nn.gelu(value, approximate=False)


def head_group():
    return 4


def grouped(value):
    width = head_group()
    return (
        value.reshape(value.shape[0], H, HD)
        .transpose(1, 0, 2)
        .reshape(H // width, width, value.shape[0], HD)
    )


def ungrouped(value):
    return value.reshape(H, value.shape[2], HD).transpose(1, 0, 2).reshape(value.shape[2], H * HD)


def attend_forward(query, keys, values, mask):

    def one_group(parts):
        q_group, k_group, v_group = parts
        scores = jnp.einsum("gtd,gsd->gts", q_group, k_group, preferred_element_type=jnp.float32)
        scores = jnp.where(mask[None], scores, -1e30)
        peak = jnp.max(scores, -1, keepdims=True)
        expo = jnp.exp(scores - peak)
        total = jnp.sum(expo, -1, keepdims=True)
        probs = (expo / total).astype(jnp.bfloat16)
        mixed = jnp.einsum("gts,gsd->gtd", probs, v_group, preferred_element_type=jnp.float32)
        return (mixed.astype(jnp.bfloat16), (peak + jnp.log(total))[..., 0])

    heads, summed = lax.map(one_group, (grouped(query), grouped(keys), grouped(values)))
    return (ungrouped(heads), summed)


def attend_backward(query, keys, values, summed, grad_out, mask):

    def one_group(parts):
        q_group, k_group, v_group, s_group, g_group = parts
        scores = jnp.einsum("gtd,gsd->gts", q_group, k_group, preferred_element_type=jnp.float32)
        probs = jnp.where(mask[None], jnp.exp(scores - s_group[..., None]), 0.0)
        grad_values = jnp.einsum(
            "gts,gtd->gsd", probs.astype(jnp.bfloat16), g_group, preferred_element_type=jnp.float32
        )
        grad_probs = jnp.einsum(
            "gtd,gsd->gts", g_group, v_group, preferred_element_type=jnp.float32
        )
        grad_scores = (
            probs * (grad_probs - jnp.sum(probs * grad_probs, -1, keepdims=True))
        ).astype(jnp.bfloat16)
        grad_query = jnp.einsum(
            "gts,gsd->gtd", grad_scores, k_group, preferred_element_type=jnp.float32
        ).astype(jnp.bfloat16)
        grad_keys = jnp.einsum(
            "gts,gtd->gsd", grad_scores, q_group, preferred_element_type=jnp.float32
        ).astype(jnp.bfloat16)
        return (grad_query, grad_keys, grad_values.astype(jnp.bfloat16))

    parts = (grouped(query), grouped(keys), grouped(values), summed, grouped(grad_out))
    grad_query, grad_keys, grad_values = lax.map(one_group, parts)
    return (ungrouped(grad_query), ungrouped(grad_keys), ungrouped(grad_values))


def make_masks(length, frames):
    place = jnp.arange(TOK)
    causal = (place[None, :] <= place[:, None]) & (place[None, :] < length)
    seen = jnp.broadcast_to(jnp.arange(FRAMES)[None, :] < frames, (TOK, FRAMES))
    return (place, causal, seen)


def clip_forward(weights, x_in, enc, length, frames):
    wa, wm, wv = weights
    vec = wv.astype(jnp.float32)
    scale = HD ** (-0.5)
    place, causal, seen = make_masks(length, frames)
    x = x_in.astype(jnp.float32)
    first = norm_apply(x, vec[0], vec[1]).astype(jnp.bfloat16)
    query = ((matmul(first, wa[0]) + vec[6]) * scale).astype(jnp.bfloat16)
    keys = matmul(first, wa[1]).astype(jnp.bfloat16)
    values = (matmul(first, wa[2]) + vec[7]).astype(jnp.bfloat16)
    mixed, summed_self = attend_forward(query, keys, values, causal)
    second_in = x + matmul(mixed, wa[3]) + vec[8]
    second = norm_apply(second_in, vec[2], vec[3]).astype(jnp.bfloat16)
    cross_query = ((matmul(second, wa[4]) + vec[9]) * scale).astype(jnp.bfloat16)
    cross_keys = matmul(enc, wa[5]).astype(jnp.bfloat16)
    cross_values = (matmul(enc, wa[6]) + vec[10]).astype(jnp.bfloat16)
    heard, summed_cross = attend_forward(cross_query, cross_keys, cross_values, seen)
    third_in = second_in + matmul(heard, wa[7]) + vec[11]
    third = norm_apply(third_in, vec[4], vec[5]).astype(jnp.bfloat16)
    hidden_pre = outer_last(third, wm[0]) + vec[13:].reshape(FF)
    hidden = gelu_exact(hidden_pre).astype(jnp.bfloat16)
    result = third_in + matmul(hidden, wm[1]) + vec[12]
    saved = (
        first,
        query,
        keys,
        values,
        mixed,
        summed_self,
        second_in,
        second,
        cross_query,
        cross_keys,
        cross_values,
        heard,
        summed_cross,
        third_in,
        third,
        hidden_pre,
        hidden,
    )
    return (result.astype(jnp.bfloat16), saved)


def clip_backward(weights, x_in, enc, length, frames, cot, saved):
    wa, wm, wv = weights
    vec = wv.astype(jnp.float32)
    scale = HD ** (-0.5)
    (
        first,
        query,
        keys,
        values,
        mixed,
        summed_self,
        second_in,
        second,
        cross_query,
        cross_keys,
        cross_values,
        heard,
        summed_cross,
        third_in,
        third,
        hidden_pre,
        hidden,
    ) = saved
    place, causal, seen = make_masks(length, frames)
    grad_y = cot.astype(jnp.float32) * (place < length).astype(jnp.float32)[:, None]
    out_three = grad_y.astype(jnp.bfloat16)
    g_down = inner_rows(hidden, out_three)
    g_b_down = jnp.sum(out_three.astype(jnp.float32), 0)
    grad_hidden = outer_last(out_three, wm[1])
    _, gelu_pull = jax.vjp(gelu_exact, hidden_pre)
    grad_pre = gelu_pull(grad_hidden)[0].astype(jnp.bfloat16)
    g_up = inner_rows(grad_pre, third)
    g_b_up = jnp.sum(grad_pre.astype(jnp.float32), 0)
    grad_third = matmul(grad_pre, wm[0])
    _, norm_pull = jax.vjp(norm_apply, third_in, vec[4], vec[5])
    part_three, g_gain_three, g_shift_three = norm_pull(grad_third)
    grad_third_in = grad_y + part_three
    out_two = grad_third_in.astype(jnp.bfloat16)
    g_cross_out = inner_rows(heard, out_two)
    g_b_cross_out = jnp.sum(out_two.astype(jnp.float32), 0)
    grad_heard = outer_last(out_two, wa[7]).astype(jnp.bfloat16)
    grad_cq, grad_ck, grad_cv = attend_backward(
        cross_query, cross_keys, cross_values, summed_cross, grad_heard, seen
    )
    grad_cq = grad_cq * scale
    g_cross_query = inner_rows(second, grad_cq)
    g_b_cross_query = jnp.sum(grad_cq.astype(jnp.float32), 0)
    g_cross_keys = inner_rows(enc, grad_ck)
    g_cross_values = inner_rows(enc, grad_cv)
    g_b_cross_values = jnp.sum(grad_cv.astype(jnp.float32), 0)
    grad_enc = outer_last(grad_ck, wa[5]) + outer_last(grad_cv, wa[6])
    grad_second = outer_last(grad_cq, wa[4])
    _, norm_pull = jax.vjp(norm_apply, second_in, vec[2], vec[3])
    part_two, g_gain_two, g_shift_two = norm_pull(grad_second)
    grad_second_in = grad_third_in + part_two
    out_one = grad_second_in.astype(jnp.bfloat16)
    g_self_out = inner_rows(mixed, out_one)
    g_b_self_out = jnp.sum(out_one.astype(jnp.float32), 0)
    grad_mixed = outer_last(out_one, wa[3]).astype(jnp.bfloat16)
    grad_q, grad_k, grad_v = attend_backward(query, keys, values, summed_self, grad_mixed, causal)
    grad_q = grad_q * scale
    g_self_query = inner_rows(first, grad_q)
    g_self_keys = inner_rows(first, grad_k)
    g_self_values = inner_rows(first, grad_v)
    g_b_self_query = jnp.sum(grad_q.astype(jnp.float32), 0)
    g_b_self_values = jnp.sum(grad_v.astype(jnp.float32), 0)
    grad_first = outer_last(grad_q, wa[0]) + outer_last(grad_k, wa[1]) + outer_last(grad_v, wa[2])
    _, norm_pull = jax.vjp(norm_apply, x_in.astype(jnp.float32), vec[0], vec[1])
    part_one, g_gain_one, g_shift_one = norm_pull(grad_first)
    grad_x = grad_second_in + part_one
    g_attn = jnp.stack(
        [
            g_self_query,
            g_self_keys,
            g_self_values,
            g_self_out,
            g_cross_query,
            g_cross_keys,
            g_cross_values,
            g_cross_out,
        ]
    )
    g_mlp = jnp.stack([g_up, g_down])
    g_vec = jnp.concatenate(
        [
            jnp.stack(
                [
                    g_gain_one,
                    g_shift_one,
                    g_gain_two,
                    g_shift_two,
                    g_gain_three,
                    g_shift_three,
                    g_b_self_query,
                    g_b_self_values,
                    g_b_self_out,
                    g_b_cross_query,
                    g_b_cross_values,
                    g_b_cross_out,
                    g_b_down,
                ]
            ),
            g_b_up.reshape(FF // D, D),
        ],
        0,
    )
    return ((g_attn, g_mlp, g_vec), grad_x, grad_enc)


def adam_update(weight, first, second, grad, rate):
    first_new = beta_first * first + (1.0 - beta_first) * grad
    second_new = beta_second * second + (1.0 - beta_second) * grad * grad
    ratio = (
        first_new
        / (1.0 - beta_first**STEP)
        / (jnp.sqrt(second_new / (1.0 - beta_second**STEP)) + adam_epsilon)
    )
    return (weight - rate * (ratio + weight_decay * weight), first_new, second_new)


def plain_body(
    tokens,
    enc_states,
    cotangent,
    tok_len,
    frame_count,
    attn_w,
    attn_m,
    attn_v,
    mlp_w,
    mlp_m,
    mlp_v,
    vec_w,
    vec_m,
    vec_v,
):
    shards = (attn_w.astype(jnp.bfloat16), mlp_w.astype(jnp.bfloat16), vec_w.astype(jnp.bfloat16))
    weights = (
        lax.all_gather(shards[0], ("dp", "fsdp"), axis=1, tiled=True),
        lax.all_gather(shards[1], ("dp", "fsdp"), axis=1, tiled=True),
        lax.all_gather(shards[2], ("dp", "fsdp"), axis=1, tiled=True),
    )

    def forward_one(items):
        x_in, enc, length, frames = items
        return clip_forward(weights, x_in, enc, length, frames)

    result, saved = lax.map(forward_one, (tokens, enc_states, tok_len, frame_count))
    back_weights = (
        lax.all_gather(shards[0], ("dp", "fsdp"), axis=1, tiled=True),
        lax.all_gather(shards[1], ("dp", "fsdp"), axis=1, tiled=True),
        lax.all_gather(shards[2], ("dp", "fsdp"), axis=1, tiled=True),
    )

    def backward_one(carry, items):
        x_in, enc, length, frames, cot, kept = items
        grads, grad_x, grad_enc = clip_backward(back_weights, x_in, enc, length, frames, cot, kept)
        return (jax.tree.map(jnp.add, carry, grads), (grad_x, grad_enc))

    zeros = (
        jnp.zeros(weights[0].shape, jnp.float32),
        jnp.zeros(weights[1].shape, jnp.float32),
        jnp.zeros(weights[2].shape, jnp.float32),
    )
    totals, (d_tokens, d_enc) = lax.scan(
        backward_one, zeros, (tokens, enc_states, tok_len, frame_count, cotangent, saved)
    )
    grad_attn, grad_mlp, grad_vec = (
        lax.psum_scatter(totals[0], ("dp", "fsdp"), scatter_dimension=1, tiled=True),
        lax.psum_scatter(totals[1], ("dp", "fsdp"), scatter_dimension=1, tiled=True),
        lax.psum_scatter(totals[2], ("dp", "fsdp"), scatter_dimension=1, tiled=True),
    )
    attn_new = adam_update(attn_w, attn_m, attn_v, grad_attn, rate_attention)
    mlp_new = adam_update(mlp_w, mlp_m, mlp_v, grad_mlp, rate_feedforward)
    vec_new = adam_update(vec_w, vec_m, vec_v, grad_vec, rate_vector)
    return (
        result,
        d_tokens,
        d_enc,
        attn_new[0],
        attn_new[1],
        attn_new[2],
        mlp_new[0],
        mlp_new[1],
        mlp_new[2],
        vec_new[0],
        vec_new[1],
        vec_new[2],
    )


def fused_body(tokens, enc_states, cotangent, tok_len, frame_count, attn_w, attn_m, attn_v, mlp_w, mlp_m, mlp_v, vec_w, vec_m, vec_v):
    out, d_tokens, d_enc, gsum, grad_vec = call_block(
        tok_len, frame_count, tokens[0], enc_states[0], cotangent[0], attn_w, mlp_w.reshape(8, ROWS, D), vec_w
    )
    attn_new = adam_update(attn_w, attn_m, attn_v, gsum[:8], rate_attention)
    mlp_new = adam_update(mlp_w, mlp_m, mlp_v, gsum[8:].reshape(mlp_w.shape), rate_feedforward)
    vec_new = adam_update(vec_w, vec_m, vec_v, grad_vec, rate_vector)
    return (out[None], d_tokens[None], d_enc.reshape(enc_states.shape), *attn_new, *mlp_new, *vec_new)


def solution(mesh):
    fused = mesh.shape["dp"] == DEPTH and mesh.shape["fsdp"] == 2 * PLANE
    return jax.shard_map(
        fused_body if fused else plain_body,
        mesh=mesh,
        in_specs=(
            P(("dp", "fsdp"), None, None),
            P(("dp", "fsdp"), None, None),
            P(("dp", "fsdp"), None, None),
            P(("dp", "fsdp")),
            P(("dp", "fsdp")),
            P(None, ("dp", "fsdp"), None),
            P(None, ("dp", "fsdp"), None),
            P(None, ("dp", "fsdp"), None),
            P(None, ("dp", "fsdp"), None),
            P(None, ("dp", "fsdp"), None),
            P(None, ("dp", "fsdp"), None),
            P(None, ("dp", "fsdp")),
            P(None, ("dp", "fsdp")),
            P(None, ("dp", "fsdp")),
        ),
        out_specs=(
            P(("dp", "fsdp"), None, None),
            P(("dp", "fsdp"), None, None),
            P(("dp", "fsdp"), None, None),
            P(None, ("dp", "fsdp"), None),
            P(None, ("dp", "fsdp"), None),
            P(None, ("dp", "fsdp"), None),
            P(None, ("dp", "fsdp"), None),
            P(None, ("dp", "fsdp"), None),
            P(None, ("dp", "fsdp"), None),
            P(None, ("dp", "fsdp")),
            P(None, ("dp", "fsdp")),
            P(None, ("dp", "fsdp")),
        ),
        check_vma=False,
    )
```

```python
import functools
import heapq
import jax
import jax.numpy as jnp
from jax import lax
from jax.experimental import pallas as pl
from jax.experimental.pallas import tpu as pltpu
from jax.sharding import PartitionSpec as P

D = 768
H = 12
HD = 64
FF = 3072
FRAMES = 1500
TOK = 448
STEP = 10
PADDED = 1536
ROWS = 24
PLANE = 4
DEPTH = 4
UNITS = 16
HALF = D // 2
BF = jnp.bfloat16
F32 = jnp.float32
MESH = pl.DeviceIdType.MESH
norm_epsilon = 1e-05
VMEM_LIMIT = 63 * 2**20


def dot(a, b):
    return lax.dot_general(a, b, (((1,), (0,)), ((), ())), preferred_element_type=F32)


def dot_nt(a, b):
    return lax.dot_general(a, b, (((1,), (1,)), ((), ())), preferred_element_type=F32)


def dot_tn(a, b):
    return lax.dot_general(a, b, (((0,), (0,)), ((), ())), preferred_element_type=F32)


def layer_norm(v, gain, shift):
    c = v - jnp.mean(v, -1, keepdims=True)
    s = jnp.mean(c * c, -1, keepdims=True)
    return c * lax.rsqrt(s + norm_epsilon) * gain + shift


def layer_norm_back(v, gain, grad):
    c = v - jnp.mean(v, -1, keepdims=True)
    r = lax.rsqrt(jnp.mean(c * c, -1, keepdims=True) + norm_epsilon)
    xh = c * r
    t = grad * gain
    dx = r * (t - jnp.mean(t, -1, keepdims=True) - xh * jnp.mean(t * xh, -1, keepdims=True))
    return dx, jnp.sum(grad * xh, 0, keepdims=True), jnp.sum(grad, 0, keepdims=True)


def gelu_both(u):
    z = jnp.abs(u) * 0.7071067811865476
    e = jnp.exp(-0.5 * u * u)
    t = 1.0 / (1.0 + 0.3275911 * z)
    poly = t * (0.254829592 + t * (-0.284496736 + t * (1.421413741 + t * (-1.453152027 + t * 1.061405429))))
    half = 0.5 * poly * e
    phi = jnp.where(u >= 0, 1.0 - half, half)
    return u * phi, phi + u * (e * 0.3989422804014327)


def colsum(v):
    return jnp.sum(v.astype(F32), 0, keepdims=True)


def head_lanes(rows, h):
    return (lax.broadcasted_iota(jnp.int32, (rows, 128), 1) // HD) == h


class Place:
    def __init__(self):
        self.z = lax.axis_index("dp")
        f = lax.axis_index("fsdp")
        self.f = f
        self.c = f % 2
        self.p = f // 2
        x, y = self.p % 2, self.p // 2
        self.part = f + 1 - 2 * self.c
        fx, fy = f + 2 - 4 * x, f + 4 - 8 * y
        px, py = self.p + 1 - 2 * x, self.p + 2 - 4 * y
        c = self.c
        self.n1, self.n2 = fx + c * (fy - fx), fy + c * (fx - fy)
        self.p1, self.p2, self.p3 = px + c * (py - px), py + c * (px - py), 3 - self.p
        self.zto = [(self.z + d) % DEPTH for d in range(1, DEPTH)]
        self.zfrom = [(self.z + DEPTH - d) % DEPTH for d in range(1, DEPTH)]
        self.own = pl.ds(pl.multiple_of(c * HALF, 128), HALF)
        self.other = pl.ds(pl.multiple_of(HALF - c * HALF, 128), HALF)

    def greet(self):
        barrier = pltpu.get_barrier_semaphore()
        others = [(zz, self.f) for zz in self.zto]
        others += [(self.z, self.n1), (self.z, self.n2), (self.z, self.part)]
        for device in others:
            pl.semaphore_signal(barrier, inc=1, device_id=device, device_id_type=MESH)
        pl.semaphore_wait(barrier, len(others))


def remote(src, dst, send, recv, device):
    return pltpu.make_async_remote_copy(
        src_ref=src, dst_ref=dst, send_sem=send, recv_sem=recv, device_id=device, device_id_type=MESH
    )


class Gather:
    def __init__(self, place, view, send, recv):
        self.w, self.view, self.send, self.recv = place, view, send, recv

    def copy(self, k, ref, device):
        return remote(ref, ref, self.send(k), self.recv(k), device)

    def own(self, zz, p):
        return self.view(zz, p, True)

    def s1(self):
        w = self.w
        for i, zz in enumerate(w.zto):
            self.copy(i, self.own(w.z, w.p), (zz, w.f)).start()

    def s2(self):
        w = self.w
        for i, zz in enumerate(w.zfrom):
            self.copy(i, self.own(zz, w.p), (zz, w.f)).wait_recv()
        self.copy(3, self.own(None, w.p), (w.z, w.n1)).start()
        self.copy(4, self.own(None, w.p), (w.z, w.n2)).start()
        self.copy(6, self.own(None, w.p), (w.z, w.part)).start()

    def s3(self):
        w = self.w
        self.copy(3, self.own(None, w.p1), (w.z, w.n1)).wait_recv()
        self.copy(5, self.own(None, w.p1), (w.z, w.n2)).start()
        self.copy(7, self.own(None, w.p1), (w.z, w.part)).start()

    def s4(self):
        w = self.w
        self.copy(4, self.own(None, w.p2), (w.z, w.n2)).wait_recv()
        self.copy(8, self.own(None, w.p2), (w.z, w.part)).start()

    def s5(self):
        w = self.w
        self.copy(5, self.own(None, w.p3), (w.z, w.n2)).wait_recv()
        self.copy(9, self.own(None, w.p3), (w.z, w.part)).start()

    def ready(self):
        w = self.w
        for k, p in enumerate((w.p, w.p1, w.p2, w.p3)):
            self.copy(6 + k, self.view(None, p, False), (w.z, w.part)).wait_recv()

    def drain(self):
        w = self.w
        for i, zz in enumerate(w.zto):
            self.copy(i, self.own(w.z, w.p), (zz, w.f)).wait_send()
        for k, p in ((3, w.p), (4, w.p), (5, w.p1), (6, w.p), (7, w.p1), (8, w.p2), (9, w.p3)):
            self.copy(k, self.own(None, p), (w.z, w.n1)).wait_send()


def heads_forward(q_ref, k_ref, v_ref, o_ref, lse_ref, mask_fn, keys, tile, first, count):
    def pair(hp, _):
        lanes = pl.ds(pl.multiple_of(hp * 128, 128), 128)
        kp, vp = k_ref[:keys, lanes], v_ref[:keys, lanes]
        for i in range(TOK // tile):
            rows = pl.ds(i * tile, tile)
            qp = q_ref[rows, lanes]
            sums = lse_ref[rows, :]
            lane = lax.broadcasted_iota(jnp.int32, (tile, 128), 1)
            scores = []
            for h in range(2):
                s = dot_nt(jnp.where(head_lanes(tile, h), qp, jnp.zeros_like(qp)), kp)
                scores.append(mask_fn(s, i))
            expos, totals = [], []
            for h in range(2):
                peak = jnp.max(scores[h], -1, keepdims=True)
                expo = jnp.exp(scores[h] - peak)
                totals.append(jnp.sum(expo, -1, keepdims=True))
                expos.append(expo.astype(BF))
                sums = jnp.where(lane == hp * 2 + h, peak + jnp.log(totals[h]), sums)
            outs = [dot(expos[h], vp) * (1.0 / totals[h]) for h in range(2)]
            lse_ref[rows, :] = sums
            o_ref[rows, lanes] = jnp.where(head_lanes(tile, 0), outs[0], outs[1]).astype(BF)
        return 0

    lax.fori_loop(first, first + count, pair, 0)


def thirds(f):
    for j in range(3):
        f(pl.ds(j * 256, 256))


class Reduce:
    def __init__(self, place, local, r0, r1, r2, r3, send, recv, source, low, finish):
        self.w, self.local, self.r0, self.r1, self.r2, self.r3 = place, local, r0, r1, r2, r3
        self.send, self.recv, self.source, self.low, self.finish = send, recv, source, low, finish

    def copy(self, k, src, dst, device):
        return remote(src, dst, self.send(k), self.recv(k), device)

    def copies(self, stage):
        w, r0 = self.w, self.r0
        if stage == 0:
            return [self.copy(0, self.source, r0, (w.z, w.part))]
        if stage == 1:
            return [
                self.copy(1, r0.at[:, w.p2], self.r1.at[:, 0], (w.z, w.n2)),
                self.copy(2, r0.at[:, w.p3], self.r1.at[:, 1], (w.z, w.n2)),
            ]
        if stage == 2:
            return [self.copy(3, r0.at[:, w.p1], self.r2, (w.z, w.n1))]
        return [self.copy(4 + i, r0.at[zz, w.p], self.r3.at[i], (zz, w.f)) for i, zz in enumerate(w.zto)]

    def e0(self):
        for c in self.copies(0):
            c.start()

    def arrived(self, stage):
        for c in self.copies(stage):
            c.wait_recv()

    def e1(self):
        w = self.w
        self.arrived(0)
        for p in (w.p2, w.p3):
            self.r0[:, p] = (self.local(slice(None), p) + self.r0[:, p].astype(F32)).astype(self.low)
        for c in self.copies(1):
            c.start()

    def e2(self):
        w = self.w
        self.arrived(1)
        total = self.local(slice(None), w.p1) + self.r0[:, w.p1].astype(F32) + self.r1[:, 1].astype(F32)
        self.r0[:, w.p1] = total.astype(self.low)
        for c in self.copies(2):
            c.start()

    def partial(self, zz):
        w = self.w
        return (
            self.local(zz, w.p) + self.r0[zz, w.p].astype(F32) + self.r1[zz, 0].astype(F32) + self.r2[zz].astype(F32)
        )

    def e3(self, keep):
        w = self.w
        self.arrived(2)
        keep[...] = self.partial(w.z)
        for zz in w.zto:
            self.r0[zz, w.p] = self.partial(zz).astype(self.low)
        for c in self.copies(3):
            c.start()

    def e4(self, keep):
        self.arrived(3)
        self.finish(keep[...] + (self.r3[0].astype(F32) + self.r3[1].astype(F32) + self.r3[2].astype(F32)))

    def sent(self):
        for stage in range(4):
            for c in self.copies(stage):
                c.wait_send()


def head_delta(grad, mixed):
    product = grad.astype(F32) * mixed.astype(F32)
    high = product.astype(BF)
    low = (product - high.astype(F32)).astype(BF)
    pick = lax.broadcasted_iota(jnp.int32, (16, D), 1) // HD == lax.broadcasted_iota(jnp.int32, (16, D), 0)
    pick = pick.astype(F32).astype(BF)
    return dot_nt(pick, high) + dot_nt(pick, low)


def heads_backward(q_ref, k_ref, v_ref, g_ref, lse_ref, delta_ref, mask_fn, keys, tile, acc, first, count):
    def pair(hp, _):
        lanes = pl.ds(pl.multiple_of(hp * 128, 128), 128)
        qp, gp = q_ref[:, lanes], g_ref[:, lanes]
        zero = jnp.zeros_like(qp)
        qs = [jnp.where(head_lanes(TOK, h), qp, zero) for h in range(2)]
        gs = [jnp.where(head_lanes(TOK, h), gp, zero) for h in range(2)]
        lse = [lse_ref[pl.ds(hp * 2 + h, 1), :] for h in range(2)]
        delta = [delta_ref[pl.ds(hp * 2 + h, 1), :] for h in range(2)]
        for i in range(keys // tile):
            rows = pl.ds(i * tile, tile)
            kp, vp = k_ref[rows, lanes], v_ref[rows, lanes]
            ps, ds = [], []
            for h in range(2):
                p = jnp.exp(mask_fn(dot_nt(kp, qs[h]), i) - lse[h])
                ds.append((p * (dot_nt(vp, gs[h]) - delta[h])).astype(BF))
                ps.append(p.astype(BF))
            dv = dot(ps[0], gs[0]) + dot(ps[1], gs[1])
            dk = dot(ds[0], qs[0]) + dot(ds[1], qs[1])
            v_ref[rows, lanes] = dv.astype(BF)
            k_ref[rows, lanes] = dk.astype(BF)
            a = jnp.where(head_lanes(TOK, 0), dot_tn(ds[0], kp), dot_tn(ds[1], kp))
            if i == 0:
                acc[...] = a
            else:
                acc[...] += a
        q_ref[:, lanes] = (acc[...].astype(BF).astype(F32) * 0.125).astype(BF)
        return 0

    lax.fori_loop(first, first + count, pair, 0)


class Plan:
    def __init__(self):
        self.now, self.queue, self.count = 0.0, [], 0

    def at(self, time, event, cost=0.15):
        heapq.heappush(self.queue, (time, self.count, event, cost))
        self.count += 1

    def step(self):
        time, _, event, cost = heapq.heappop(self.queue)
        self.now = max(self.now, time) + cost
        event()

    def until(self, time):
        while self.queue and self.queue[0][0] <= time:
            self.step()
        self.now = max(self.now, time)

    def work(self, cost, compute):
        self.until(self.now)
        compute()
        self.now += cost

    def thirds(self, cost, compute):
        for j in range(3):
            self.work(cost / 3, lambda: compute(pl.ds(j * 256, 256)))


PACE = 5.0
FIRST = 9.0
AHEAD = 3.0
HOP1, HOP2, LAND = 4.0, 9.05, 11.0
SUM_START = 84.0
SUM_PACE = 5.0
SUM_HOPS = (9.0, 7.0, 5.0, 4.0)


ORDER = [5, 6, 0, 1, 2, 3, 4, 7, 8, 12, 9, 13, 10, 14, 11, 15]
A1, Q, K, V_, O, A2, CQ, O2, A3 = range(9)
DO = A3
SLOTS = 8
SUMS = [(12, 12), (8, 8), (13, 13), (9, 9), (14, 14), (10, 10), (15, 15), (11, 11), (7, 7), (4, 4), (5, 12), (6, 8), (3, 3), (0, 0), (1, 1), (2, 2)]


def block_kernel(
    len_ref, frames_ref, x_hbm, enc_hbm, cot_hbm, attn_hbm, mlp_hbm, vec_hbm,
    out_hbm, dtok_hbm, denc_hbm, gsum_hbm, gvsum_hbm,
    weights, vgather, stage, r0, r1, r2, r3, vr0, vr1, vr2, vr3, vkeep, vsmall, vpad,
    enc, cot, act, kv, lse, delta, xs, hm, gp, oacc, dacc, denc, vec, gv,
    load_sem, stage_sem, send_sem, recv_sem, vsend_sem, vrecv_sem, rsend_sem, rrecv_sem, credit, store_sem, denc_sem, own_sem,
):
    w = Place()
    length, frames = len_ref[0], frames_ref[0]
    x_ref, lse_cols, acc = hm, dacc.at[:, :128], xs.at[1, :, :128]
    local = lambda src, dst, sem: pltpu.make_async_copy(src, dst, sem)
    loads = [
        local(attn_hbm.at[:, :, w.own], stage.at[pl.ds(0, 8), w.c], load_sem.at[0]),
        local(mlp_hbm.at[:, :, w.own], stage.at[pl.ds(8, 8), w.c], load_sem.at[1]),
        local(vec_hbm, vsmall, load_sem.at[2]),
        local(x_hbm, x_ref, load_sem.at[3]),
        local(enc_hbm, enc, load_sem.at[4]),
        local(cot_hbm, cot, load_sem.at[5]),
    ]
    for i in (2, 0, 1, 3, 4, 5):
        loads[i].start()
    nv, nc = vsmall.shape
    vpad[...] = jnp.zeros_like(vpad)
    loads[2].wait()
    vpad[:nv, :nc] = vsmall[...]
    vgather[w.z, w.p, w.c] = jnp.transpose(vpad[...])[:ROWS]
    w.greet()

    def unit_view(u):
        def view(zz, p, own):
            return weights.at[u, slice(None) if zz is None else zz, p, :, w.own if own else w.other]

        return view

    def vec_view(zz, p, own):
        return vgather.at[slice(None) if zz is None else zz, p, w.c if own else 1 - w.c]

    units = [Gather(w, unit_view(u), lambda k, u=u: send_sem.at[u, k], lambda k, u=u: recv_sem.at[u, k]) for u in ORDER]
    by_weight = {u: units[i] for i, u in enumerate(ORDER)}
    vecs = Gather(w, vec_view, lambda k: vsend_sem.at[0, k], lambda k: vrecv_sem.at[0, k])

    plan = Plan()
    vecs.s1()
    parts = ((5, 2, attn_hbm, 5), (0, 5, attn_hbm, 0), (7, 1, attn_hbm, 7), (8, 8, mlp_hbm, 0))
    swaps = []
    for i, (u0, n, src, at) in enumerate(parts):
        src = src.at[pl.ds(at, n), :, w.other]
        swaps.append(remote(src, stage.at[pl.ds(u0, n), w.c], stage_sem.at[0, i], stage_sem.at[1, i], (w.z, w.part)))
        swaps[i].start()
    loads[0].wait()
    loads[1].wait()
    arrived = set()

    def start_unit(i):
        u = ORDER[i]
        k = 0 if u in (5, 6) else 1 if u < 5 else 2 if u == 7 else 3
        if k not in arrived:
            swaps[k].wait_recv()
            arrived.add(k)
        weights[u, w.z, w.p, :, w.own] = stage[u].reshape(2 * ROWS, HALF).astype(BF)
        units[i].s1()

    def first_hop(i):
        units[i].s3()
        units[i].s4()

    for i in range(UNITS):
        begin = FIRST + PACE * i
        plan.at(begin - AHEAD - PACE - 0.2 if i > 2 else 0.0, functools.partial(start_unit, i))
        plan.at(begin - AHEAD, units[i].s2)
        plan.at(begin + HOP1, functools.partial(first_hop, i))
        plan.at(begin + HOP2, units[i].s5)
    plan.at(FIRST - AHEAD + 0.05, vecs.s2)

    def vec_hop():
        vecs.s3()
        vecs.s4()

    plan.at(FIRST - AHEAD + PACE + 0.05, vec_hop)
    plan.at(FIRST - AHEAD + 2 * PACE + 0.05, vecs.s5)

    def ready(i):
        plan.until(FIRST + PACE * i + LAND)
        units[i].ready()

    def keep_of(u):
        class Keep:
            def __getitem__(self, _):
                return stage[u].reshape(2 * ROWS, HALF)

            def __setitem__(self, _, value):
                stage[u] = value.reshape(2, ROWS, HALF)

        return Keep()

    def final_swap(u):
        return remote(stage.at[u, 1 - w.c], gsum_hbm.at[u, :, w.own], rsend_sem.at[u, 7], rrecv_sem.at[u, 7], (w.z, w.part))

    def final_own(u):
        return local(stage.at[u, w.c], gsum_hbm.at[u, :, w.own], own_sem.at[u])

    def final_wait(u):
        ref = gsum_hbm.at[u, :, w.other]
        remote(ref, ref, rsend_sem.at[u, 7], rrecv_sem.at[u, 7], (w.z, w.part)).wait_recv()

    sums = []
    for r, (u, at) in enumerate(SUMS):

        def own_grad(zz, p, at=at):
            return weights[at, zz, p, :, w.own].astype(F32)

        def finish(total, u=u):
            stage[u] = total.reshape(2, ROWS, HALF)
            final_swap(u).start()
            final_own(u).start()

        sums.append(
            Reduce(
                w, own_grad, r0.at[r % SLOTS], r1.at[u], r2.at[u], r3.at[u],
                lambda k, u=u: rsend_sem.at[u, k], lambda k, u=u: rrecv_sem.at[u, k],
                weights.at[at, :, :, :, w.other], BF, finish,
            )
        )

    def vfinish(total):
        vkeep[...] = total

    vsums = Reduce(
        w, lambda zz, p: vgather[zz, p, w.c], vr0, vr1, vr2, vr3, lambda k: vsend_sem.at[1, k], lambda k: vrecv_sem.at[1, k],
        vgather.at[:, :, 1 - w.c], F32, vfinish,
    )

    recycled = set()
    sums_begin = [SUM_START]

    def launch(r):
        if r >= SLOTS:
            while r - SLOTS not in recycled:
                plan.step()
            pl.semaphore_wait(credit, 1)
        sums[r].e0()
        begin = max(plan.now + 2.0, sums_begin[0])
        sums_begin[0] = begin + SUM_PACE
        u = SUMS[r][0]

        def recycle():
            sums[r].e4(keep_of(u))
            if r < UNITS - SLOTS:
                sums[r].sent()
                pl.semaphore_signal(credit, inc=1, device_id=(w.z, w.part), device_id_type=MESH)
                recycled.add(r)

        steps = (sums[r].e1, sums[r].e2, lambda: sums[r].e3(keep_of(u)), recycle, lambda: final_wait(u))
        for k, event in enumerate(steps):
            plan.at(begin + sum(SUM_HOPS[:k]), event, 0.3)

    stores = []

    def store(src, dst):
        c = local(src, dst, store_sem.at[len(stores)])
        c.start()
        stores.append(c)

    def wcols(u, cols):
        return weights[u, :, :, :, cols].reshape(D, cols.size)

    def wrows(u, rows):
        return weights.at[u].reshape(D, D)[rows, :]

    def weight_grad(at, a, b):
        def cols(cs):
            weights[at, :, :, :, cs] = dot_tn(a(), b(cs)).astype(BF).reshape(DEPTH, PLANE, 2 * ROWS, 256)

        thirds(cols)

    vrow = lambda r, cols=slice(None): vec[r : r + 1, cols]

    lse_cols[...] = jnp.zeros((TOK, 128), F32)
    kv[:, FRAMES // 16 * 16 :, :] = jnp.zeros((2, PADDED - FRAMES // 16 * 16, D), BF)
    loads[4].wait()

    def enc_project(u, which, bias, a, b):
        def cols(cs):
            r = dot(enc[a:b, :], wcols(u, cs))
            if bias is not None:
                r = r + vrow(bias, cs)
            kv[which, a:b, cs] = r.astype(BF)

        thirds(cols)

    parts = ((0, 512), (512, 1024), (1024, FRAMES))
    ready(0)
    for a, b in parts:
        plan.work(0.95, functools.partial(enc_project, 5, 0, None, a, b))
    vecs.ready()
    table = vgather[...].reshape(D, 128).astype(BF).astype(F32)
    vec[...] = jnp.transpose(table)[:24, :]
    lane = lax.broadcasted_iota(jnp.int32, (ROWS, 128), 1)
    source = lax.broadcasted_iota(jnp.int32, (128, 128), 0)
    spread = [dot(table.astype(BF), (source == 13 + a).astype(F32).astype(BF)) for a in range(4)]
    blocks = []
    for chip in range(16):
        for core in range(2):
            block = jnp.zeros((ROWS, 128), F32)
            for j in range(4):
                at = (chip % 4) * 192 + core * 96 + j * ROWS
                block = jnp.where(lane == j, spread[chip // 4][at : at + ROWS], block)
            blocks.append(block)
    vec[16:24, :] = jnp.transpose(jnp.concatenate(blocks, 0))[:8, :]
    loads[3].wait()
    act[A1] = layer_norm(x_ref[...].astype(F32), vrow(0), vrow(1)).astype(BF)
    plan.now += 3.0
    ready(1)
    for a, b in parts:
        plan.work(0.95, functools.partial(enc_project, 6, 1, 10, a, b))

    def project(src, u, dst, bias, scale):
        def cols(cs):
            r = dot(act[src], wcols(u, cs))
            if bias is not None:
                r = r + vrow(bias, cs)
            act[dst, :, cs] = (r * scale).astype(BF)

        thirds(cols)

    for i, args in ((2, (A1, 0, Q, 6, 0.125)), (3, (A1, 1, K, None, 1.0)), (4, (A1, 2, V_, 7, 1.0))):
        ready(i)
        plan.work(0.75, functools.partial(project, *args))

    def self_mask(s, i):
        r = lax.broadcasted_iota(jnp.int32, s.shape, 0) + i * s.shape[0]
        c = lax.broadcasted_iota(jnp.int32, s.shape, 1)
        return jnp.where((c <= r) & (c < length), s, -1e30)

    def cross_mask(s, i):
        c = lax.broadcasted_iota(jnp.int32, (1, PADDED - 640), 1) + 640
        return jnp.concatenate([s[:, :640], jnp.where(c < frames, s[:, 640:], -1e30)], axis=1)

    def self_pairs(i):
        heads_forward(act.at[Q], act.at[K], act.at[V_], act.at[O], lse_cols, self_mask, TOK, 448, 2 * i, 2)

    for i in range(3):
        plan.work(2.1, functools.partial(self_pairs, i))
    lse[0] = jnp.transpose(lse_cols[...])[:16, :]
    ready(5)

    def residual(src, base, u, dst, bias):
        def cols(cs):
            xs[dst, :, cs] = base(cs) + dot(act[src], wcols(u, cs)) + vrow(bias, cs)

        thirds(cols)

    def norm(src, dst, row):
        act[dst] = layer_norm(xs[src], vrow(row), vrow(row + 1)).astype(BF)

    plan.work(0.8, lambda: residual(O, lambda cs: x_ref[:, cs].astype(F32), 3, 0, 8))
    plan.work(0.8, lambda: norm(0, A2, 2))
    ready(6)
    plan.work(0.7, lambda: project(A2, 4, CQ, 9, 0.125))

    def cross_pair(i):
        heads_forward(act.at[CQ], kv.at[0], kv.at[1], act.at[O2], lse_cols, cross_mask, PADDED, 224, i, 1)

    for i in range(6):
        plan.work(2.55, functools.partial(cross_pair, i))
    ready(7)
    plan.work(0.8, lambda: residual(O2, lambda cs: xs[0, :, cs], 7, 1, 11))
    plan.work(0.8, lambda: norm(1, A3, 4))
    lse[1] = jnp.transpose(lse_cols[...])[:16, :]
    loads[5].wait()
    ok = lax.broadcasted_iota(jnp.int32, (TOK, 1), 0) < length
    cot[...] = jnp.where(ok, cot[...], jnp.zeros((TOK, D), BF))
    gv[...] = jnp.zeros_like(gv)
    gv[12:13, :] = colsum(cot[...])
    oacc[...] = jnp.zeros_like(oacc)
    dacc[...] = jnp.zeros_like(dacc)
    for j in range(4):
        ready(8 + 2 * j)

        def hidden(rs):
            u = dot_nt(act[A3], wrows(8 + j, rs)) + vec[16 + j : 17 + j, rs]
            g, d = gelu_both(u)
            hm[:, rs] = g.astype(BF)
            gp[:, rs] = d.astype(BF)

        plan.thirds(2.1, hidden)
        ready(9 + 2 * j)

        def down(rs):
            oacc[:, rs] += dot(hm[...], wcols(12 + j, rs))
            d = (dot_nt(cot[...], wrows(12 + j, rs)) * gp[:, rs].astype(F32)).astype(BF)
            gp[:, rs] = d
            gv[13 + j : 14 + j, rs] = colsum(d)

        plan.thirds(1.7, down)

        def back(rs):
            dacc[:, rs] += dot(gp[...], wcols(8 + j, rs))

        plan.work(0.9, lambda: thirds(back))
        by_weight[12 + j].drain()
        plan.work(0.85, lambda: weight_grad(12 + j, lambda: hm[...], lambda cs: cot[:, cs]))
        launch(2 * j)
        by_weight[8 + j].drain()
        plan.work(0.85, lambda: weight_grad(8 + j, lambda: gp[...], lambda cs: act[A3, :, cs]))
        launch(2 * j + 1)
    hm[...] = (xs[1] + oacc[...] + vrow(12)).astype(BF)
    store(hm, out_hbm)
    again = local(x_hbm, gp, load_sem.at[3])
    again.start()
    dx = oacc
    dpart, gg, gb = layer_norm_back(xs[1], vrow(4), dacc[...])
    gv[4:5, :] = gg
    gv[5:6, :] = gb
    dx[...] = cot[...].astype(F32) + dpart
    dr = cot
    dr[...] = dx[...].astype(BF)
    plan.now += 2.0

    def times_output(u):
        def cols(cs):
            act[DO, :, cs] = dot_nt(dr[...], wrows(u, cs)).astype(BF)

        thirds(cols)

    plan.work(0.7, lambda: times_output(7))
    by_weight[7].drain()
    plan.work(0.7, lambda: weight_grad(7, lambda: act[O2], lambda cs: dr[:, cs]))
    launch(8)
    plan.now += 1.0
    delta[...] = head_delta(act[DO], act[O2])
    gv[11:12, :] = colsum(dr[...])

    def cross_mask_t(s, i):
        n = s.shape[0]
        if (i + 1) * n <= 750:
            return s
        f = lax.broadcasted_iota(jnp.int32, (n, 1), 0) + i * n
        return s + jnp.where(f < frames, 0.0, -1e30)

    def self_mask_t(s, i):
        r = lax.broadcasted_iota(jnp.int32, s.shape, 0) + i * s.shape[0]
        c = lax.broadcasted_iota(jnp.int32, s.shape, 1)
        return jnp.where((r <= c) & (r < length), s, -1e30)

    def cross_pair_back(i):
        heads_backward(
            act.at[CQ], kv.at[0], kv.at[1], act.at[DO], lse.at[1], delta, cross_mask_t, PADDED, 256, acc, i, 1
        )

    for i in range(6):
        plan.work(3.9, functools.partial(cross_pair_back, i))

    def times_back(pairs):
        def cols(cs):
            total = 0.0
            for a, u in pairs:
                total = total + dot_nt(act[a], wrows(u, cs))
            dacc[:, cs] = total

        thirds(cols)

    plan.work(0.7, lambda: times_back(((CQ, 4),)))
    by_weight[4].drain()
    plan.work(0.7, lambda: weight_grad(4, lambda: act[A2], lambda cs: act[CQ, :, cs]))
    launch(9)
    while not recycled >= {0, 1}:
        plan.step()
    plan.work(2.0, lambda: weight_grad(12, lambda: enc[...], lambda cs: kv[0, :FRAMES, cs]))
    launch(10)
    plan.work(2.0, lambda: weight_grad(8, lambda: enc[...], lambda cs: kv[1, :FRAMES, cs]))
    launch(11)
    gv[9:10, :] = colsum(act[CQ])
    gv[10:11, :] = colsum(kv[1])
    dpart, gg, gb = layer_norm_back(xs[0], vrow(2), dacc[...])
    gv[2:3, :] = gg
    gv[3:4, :] = gb
    dx[...] += dpart
    dr[...] = dx[...].astype(BF)
    gv[8:9, :] = colsum(dr[...])
    plan.now += 2.0
    plan.work(0.7, lambda: times_output(3))
    by_weight[3].drain()
    plan.work(0.7, lambda: weight_grad(3, lambda: act[O], lambda cs: dr[:, cs]))
    launch(12)
    delta[...] = head_delta(act[DO], act[O])
    plan.now += 0.5
    def self_pairs_back(i):
        heads_backward(
            act.at[Q], act.at[K], act.at[V_], act.at[DO], lse.at[0], delta, self_mask_t, TOK, 224, acc, 2 * i, 2
        )

    for i in range(3):
        plan.work(2.4, functools.partial(self_pairs_back, i))
    plan.work(1.8, lambda: times_back(((Q, 0), (K, 1), (V_, 2))))
    for r, a in ((13, Q), (14, K), (15, V_)):
        u = SUMS[r][0]
        by_weight[u].drain()
        plan.work(0.7, lambda: weight_grad(u, lambda: act[A1], lambda cs, a=a: act[a, :, cs]))
        launch(r)
    gv[6:7, :] = colsum(act[Q])
    gv[7:8, :] = colsum(act[V_])
    again.wait()
    dpart, gg, gb = layer_norm_back(gp[...].astype(F32), vrow(0), dacc[...])
    gv[0:1, :] = gg
    gv[1:2, :] = gb
    dx[...] += dpart
    store(dx, dtok_hbm)
    vecs.drain()
    table = jnp.transpose(jnp.concatenate([gv[...], jnp.zeros((104, D), F32)], 0))
    high = table.astype(BF)
    rest = table - high.astype(F32)
    mid = rest.astype(BF)
    low = (rest - mid.astype(F32)).astype(BF)
    spread = []
    for j in range(4):
        pick = (source == 13 + j).astype(F32).astype(BF)
        spread.append(dot(high, pick) + (dot(mid, pick) + dot(low, pick)))
    for b in range(4):
        for core in range(2):
            for j in range(4):
                at = b * 192 + core * 96 + j * ROWS
                block = jnp.where(lane < 13, table[at : at + ROWS], 0.0)
                for a in range(4):
                    src = (4 * a + b) * 48 + core * ROWS
                    block = jnp.where(lane == 13 + a, spread[j][src : src + ROWS], block)
                n = at // ROWS
                vgather[n // 8, n // 2 % 4, n % 2] = block
    plan.now += 4.0
    vsums.e0()
    for k, event in enumerate((vsums.e1, vsums.e2, lambda: vsums.e3(vkeep), lambda: vsums.e4(vkeep))):
        plan.at(plan.now + 2.0 + 3.5 * k, event, 0.3)

    chunks = [(a, min(a + 128, FRAMES)) for a in range(0, FRAMES, 128)]
    outs = {}

    def encoder_chunk(i):
        a, b = chunks[i]
        if i >= 2:
            outs[i - 2].wait()
        for k in range(3):
            cs = pl.ds(k * 256, 256)
            v = dot_nt(kv[0, a:b], wrows(5, cs)) + dot_nt(kv[1, a:b], wrows(6, cs))
            for h in range(2):
                denc[i % 2, pl.ds(2 * k + h, b - a, stride=6), :] = v[:, h * 128 : (h + 1) * 128]
        c = local(denc.at[i % 2, pl.ds(0, 6 * (b - a))], denc_hbm.at[pl.ds(6 * a, 6 * (b - a))], denc_sem.at[i % 2])
        c.start()
        outs[i] = c

    for i in range(len(chunks)):
        plan.work(0.45, functools.partial(encoder_chunk, i))
    while plan.queue:
        plan.step()
    vpad[:ROWS, :] = vkeep[...]
    vsmall[...] = jnp.transpose(vpad[...])[:nv, :nc]
    store(vsmall, gvsum_hbm)
    for c in swaps:
        c.wait_send()
    for u in (5, 6):
        by_weight[u].drain()
    for r, (u, _) in enumerate(SUMS):
        if r >= UNITS - SLOTS:
            sums[r].sent()
        final_swap(u).wait_send()
        final_own(u).wait()
    vsums.sent()
    outs[10].wait()
    outs[11].wait()
    for c in stores:
        c.wait()


def call_block(length, frames, x, enc, cot, attn_w, mlp_w, vec_w):
    any_ = pl.BlockSpec(memory_space=pl.ANY)
    smem = pl.BlockSpec(memory_space=pltpu.SMEM)
    t = lambda *s, dt=F32: jax.ShapeDtypeStruct(s, dt)
    v = pltpu.VMEM
    dma = pltpu.SemaphoreType.DMA
    n, rows = DEPTH, 2 * ROWS
    return pl.pallas_call(
        block_kernel,
        out_shape=[t(TOK, D, dt=BF), t(TOK, D), t(FRAMES * 6, 128), t(UNITS, ROWS, D), t(*vec_w.shape)],
        in_specs=[smem, smem] + [any_] * 6,
        out_specs=[any_] * 5,
        scratch_shapes=[
            v((UNITS, n, PLANE, rows, D), BF), v((n, PLANE, 2, ROWS, 128), F32), v((UNITS, 2, ROWS, HALF), F32),
            v((SLOTS, n, PLANE, rows, HALF), BF), v((UNITS, n, 2, rows, HALF), BF), v((UNITS, n, rows, HALF), BF),
            v((UNITS, 3, rows, HALF), BF),
            v((n, PLANE, ROWS, 128), F32), v((n, 2, ROWS, 128), F32), v((n, ROWS, 128), F32), v((3, ROWS, 128), F32),
            v((ROWS, 128), F32), v(vec_w.shape, F32), v((128, 128), F32),
            v((FRAMES, D), BF), v((TOK, D), BF), v((9, TOK, D), BF), v((2, PADDED, D), BF),
            v((2, 16, TOK), F32), v((16, TOK), F32), v((2, TOK, D), F32),
            v((TOK, D), BF), v((TOK, D), BF), v((TOK, D), F32), v((TOK, D), F32),
            v((2, 128 * 6, 128), F32), v((24, D), F32), v((24, D), F32),
            dma((6,)), dma((2, 4)), dma((UNITS, 10)), dma((UNITS, 10)), dma((2, 10)), dma((2, 10)),
            dma((UNITS, 8)), dma((UNITS, 8)), pltpu.SemaphoreType.REGULAR, dma((4,)), dma((2,)), dma((UNITS,)),
        ],
        compiler_params=pltpu.CompilerParams(collective_id=0, has_side_effects=True, vmem_limit_bytes=VMEM_LIMIT),
        name="block",
    )(length, frames, x, enc, cot, attn_w, mlp_w, vec_w)


beta_first = 0.9
beta_second = 0.999
adam_epsilon = 1e-08
weight_decay = 0.01
rate_attention = 0.06
rate_feedforward = 0.03
rate_vector = 0.35


def matmul(left, right):
    return jnp.dot(left, right, preferred_element_type=jnp.float32)


def inner_rows(left, right):
    return lax.dot_general(
        left, right, (((0,), (0,)), ((), ())), preferred_element_type=jnp.float32
    )


def outer_last(left, right):
    return lax.dot_general(
        left, right, (((1,), (1,)), ((), ())), preferred_element_type=jnp.float32
    )


def norm_apply(value, gain, shift):
    center = value - jnp.mean(value, -1, keepdims=True)
    spread = jnp.mean(center * center, -1, keepdims=True)
    return center * lax.rsqrt(spread + norm_epsilon) * gain + shift


def gelu_exact(value):
    return jax.nn.gelu(value, approximate=False)


def head_group():
    return 4


def grouped(value):
    width = head_group()
    return (
        value.reshape(value.shape[0], H, HD)
        .transpose(1, 0, 2)
        .reshape(H // width, width, value.shape[0], HD)
    )


def ungrouped(value):
    return value.reshape(H, value.shape[2], HD).transpose(1, 0, 2).reshape(value.shape[2], H * HD)


def attend_forward(query, keys, values, mask):

    def one_group(parts):
        q_group, k_group, v_group = parts
        scores = jnp.einsum("gtd,gsd->gts", q_group, k_group, preferred_element_type=jnp.float32)
        scores = jnp.where(mask[None], scores, -1e30)
        peak = jnp.max(scores, -1, keepdims=True)
        expo = jnp.exp(scores - peak)
        total = jnp.sum(expo, -1, keepdims=True)
        probs = (expo / total).astype(jnp.bfloat16)
        mixed = jnp.einsum("gts,gsd->gtd", probs, v_group, preferred_element_type=jnp.float32)
        return (mixed.astype(jnp.bfloat16), (peak + jnp.log(total))[..., 0])

    heads, summed = lax.map(one_group, (grouped(query), grouped(keys), grouped(values)))
    return (ungrouped(heads), summed)


def attend_backward(query, keys, values, summed, grad_out, mask):

    def one_group(parts):
        q_group, k_group, v_group, s_group, g_group = parts
        scores = jnp.einsum("gtd,gsd->gts", q_group, k_group, preferred_element_type=jnp.float32)
        probs = jnp.where(mask[None], jnp.exp(scores - s_group[..., None]), 0.0)
        grad_values = jnp.einsum(
            "gts,gtd->gsd", probs.astype(jnp.bfloat16), g_group, preferred_element_type=jnp.float32
        )
        grad_probs = jnp.einsum(
            "gtd,gsd->gts", g_group, v_group, preferred_element_type=jnp.float32
        )
        grad_scores = (
            probs * (grad_probs - jnp.sum(probs * grad_probs, -1, keepdims=True))
        ).astype(jnp.bfloat16)
        grad_query = jnp.einsum(
            "gts,gsd->gtd", grad_scores, k_group, preferred_element_type=jnp.float32
        ).astype(jnp.bfloat16)
        grad_keys = jnp.einsum(
            "gts,gtd->gsd", grad_scores, q_group, preferred_element_type=jnp.float32
        ).astype(jnp.bfloat16)
        return (grad_query, grad_keys, grad_values.astype(jnp.bfloat16))

    parts = (grouped(query), grouped(keys), grouped(values), summed, grouped(grad_out))
    grad_query, grad_keys, grad_values = lax.map(one_group, parts)
    return (ungrouped(grad_query), ungrouped(grad_keys), ungrouped(grad_values))


def make_masks(length, frames):
    place = jnp.arange(TOK)
    causal = (place[None, :] <= place[:, None]) & (place[None, :] < length)
    seen = jnp.broadcast_to(jnp.arange(FRAMES)[None, :] < frames, (TOK, FRAMES))
    return (place, causal, seen)


def clip_forward(weights, x_in, enc, length, frames):
    wa, wm, wv = weights
    vec = wv.astype(jnp.float32)
    scale = HD ** (-0.5)
    place, causal, seen = make_masks(length, frames)
    x = x_in.astype(jnp.float32)
    first = norm_apply(x, vec[0], vec[1]).astype(jnp.bfloat16)
    query = ((matmul(first, wa[0]) + vec[6]) * scale).astype(jnp.bfloat16)
    keys = matmul(first, wa[1]).astype(jnp.bfloat16)
    values = (matmul(first, wa[2]) + vec[7]).astype(jnp.bfloat16)
    mixed, summed_self = attend_forward(query, keys, values, causal)
    second_in = x + matmul(mixed, wa[3]) + vec[8]
    second = norm_apply(second_in, vec[2], vec[3]).astype(jnp.bfloat16)
    cross_query = ((matmul(second, wa[4]) + vec[9]) * scale).astype(jnp.bfloat16)
    cross_keys = matmul(enc, wa[5]).astype(jnp.bfloat16)
    cross_values = (matmul(enc, wa[6]) + vec[10]).astype(jnp.bfloat16)
    heard, summed_cross = attend_forward(cross_query, cross_keys, cross_values, seen)
    third_in = second_in + matmul(heard, wa[7]) + vec[11]
    third = norm_apply(third_in, vec[4], vec[5]).astype(jnp.bfloat16)
    hidden_pre = outer_last(third, wm[0]) + vec[13:].reshape(FF)
    hidden = gelu_exact(hidden_pre).astype(jnp.bfloat16)
    result = third_in + matmul(hidden, wm[1]) + vec[12]
    saved = (
        first,
        query,
        keys,
        values,
        mixed,
        summed_self,
        second_in,
        second,
        cross_query,
        cross_keys,
        cross_values,
        heard,
        summed_cross,
        third_in,
        third,
        hidden_pre,
        hidden,
    )
    return (result.astype(jnp.bfloat16), saved)


def clip_backward(weights, x_in, enc, length, frames, cot, saved):
    wa, wm, wv = weights
    vec = wv.astype(jnp.float32)
    scale = HD ** (-0.5)
    (
        first,
        query,
        keys,
        values,
        mixed,
        summed_self,
        second_in,
        second,
        cross_query,
        cross_keys,
        cross_values,
        heard,
        summed_cross,
        third_in,
        third,
        hidden_pre,
        hidden,
    ) = saved
    place, causal, seen = make_masks(length, frames)
    grad_y = cot.astype(jnp.float32) * (place < length).astype(jnp.float32)[:, None]
    out_three = grad_y.astype(jnp.bfloat16)
    g_down = inner_rows(hidden, out_three)
    g_b_down = jnp.sum(out_three.astype(jnp.float32), 0)
    grad_hidden = outer_last(out_three, wm[1])
    _, gelu_pull = jax.vjp(gelu_exact, hidden_pre)
    grad_pre = gelu_pull(grad_hidden)[0].astype(jnp.bfloat16)
    g_up = inner_rows(grad_pre, third)
    g_b_up = jnp.sum(grad_pre.astype(jnp.float32), 0)
    grad_third = matmul(grad_pre, wm[0])
    _, norm_pull = jax.vjp(norm_apply, third_in, vec[4], vec[5])
    part_three, g_gain_three, g_shift_three = norm_pull(grad_third)
    grad_third_in = grad_y + part_three
    out_two = grad_third_in.astype(jnp.bfloat16)
    g_cross_out = inner_rows(heard, out_two)
    g_b_cross_out = jnp.sum(out_two.astype(jnp.float32), 0)
    grad_heard = outer_last(out_two, wa[7]).astype(jnp.bfloat16)
    grad_cq, grad_ck, grad_cv = attend_backward(
        cross_query, cross_keys, cross_values, summed_cross, grad_heard, seen
    )
    grad_cq = grad_cq * scale
    g_cross_query = inner_rows(second, grad_cq)
    g_b_cross_query = jnp.sum(grad_cq.astype(jnp.float32), 0)
    g_cross_keys = inner_rows(enc, grad_ck)
    g_cross_values = inner_rows(enc, grad_cv)
    g_b_cross_values = jnp.sum(grad_cv.astype(jnp.float32), 0)
    grad_enc = outer_last(grad_ck, wa[5]) + outer_last(grad_cv, wa[6])
    grad_second = outer_last(grad_cq, wa[4])
    _, norm_pull = jax.vjp(norm_apply, second_in, vec[2], vec[3])
    part_two, g_gain_two, g_shift_two = norm_pull(grad_second)
    grad_second_in = grad_third_in + part_two
    out_one = grad_second_in.astype(jnp.bfloat16)
    g_self_out = inner_rows(mixed, out_one)
    g_b_self_out = jnp.sum(out_one.astype(jnp.float32), 0)
    grad_mixed = outer_last(out_one, wa[3]).astype(jnp.bfloat16)
    grad_q, grad_k, grad_v = attend_backward(query, keys, values, summed_self, grad_mixed, causal)
    grad_q = grad_q * scale
    g_self_query = inner_rows(first, grad_q)
    g_self_keys = inner_rows(first, grad_k)
    g_self_values = inner_rows(first, grad_v)
    g_b_self_query = jnp.sum(grad_q.astype(jnp.float32), 0)
    g_b_self_values = jnp.sum(grad_v.astype(jnp.float32), 0)
    grad_first = outer_last(grad_q, wa[0]) + outer_last(grad_k, wa[1]) + outer_last(grad_v, wa[2])
    _, norm_pull = jax.vjp(norm_apply, x_in.astype(jnp.float32), vec[0], vec[1])
    part_one, g_gain_one, g_shift_one = norm_pull(grad_first)
    grad_x = grad_second_in + part_one
    g_attn = jnp.stack(
        [
            g_self_query,
            g_self_keys,
            g_self_values,
            g_self_out,
            g_cross_query,
            g_cross_keys,
            g_cross_values,
            g_cross_out,
        ]
    )
    g_mlp = jnp.stack([g_up, g_down])
    g_vec = jnp.concatenate(
        [
            jnp.stack(
                [
                    g_gain_one,
                    g_shift_one,
                    g_gain_two,
                    g_shift_two,
                    g_gain_three,
                    g_shift_three,
                    g_b_self_query,
                    g_b_self_values,
                    g_b_self_out,
                    g_b_cross_query,
                    g_b_cross_values,
                    g_b_cross_out,
                    g_b_down,
                ]
            ),
            g_b_up.reshape(FF // D, D),
        ],
        0,
    )
    return ((g_attn, g_mlp, g_vec), grad_x, grad_enc)


def adam_update(weight, first, second, grad, rate):
    first_new = beta_first * first + (1.0 - beta_first) * grad
    second_new = beta_second * second + (1.0 - beta_second) * grad * grad
    ratio = (
        first_new
        / (1.0 - beta_first**STEP)
        / (jnp.sqrt(second_new / (1.0 - beta_second**STEP)) + adam_epsilon)
    )
    return (weight - rate * (ratio + weight_decay * weight), first_new, second_new)


def plain_body(
    tokens,
    enc_states,
    cotangent,
    tok_len,
    frame_count,
    attn_w,
    attn_m,
    attn_v,
    mlp_w,
    mlp_m,
    mlp_v,
    vec_w,
    vec_m,
    vec_v,
):
    shards = (attn_w.astype(jnp.bfloat16), mlp_w.astype(jnp.bfloat16), vec_w.astype(jnp.bfloat16))
    weights = (
        lax.all_gather(shards[0], ("dp", "fsdp"), axis=1, tiled=True),
        lax.all_gather(shards[1], ("dp", "fsdp"), axis=1, tiled=True),
        lax.all_gather(shards[2], ("dp", "fsdp"), axis=1, tiled=True),
    )

    def forward_one(items):
        x_in, enc, length, frames = items
        return clip_forward(weights, x_in, enc, length, frames)

    result, saved = lax.map(forward_one, (tokens, enc_states, tok_len, frame_count))
    back_weights = (
        lax.all_gather(shards[0], ("dp", "fsdp"), axis=1, tiled=True),
        lax.all_gather(shards[1], ("dp", "fsdp"), axis=1, tiled=True),
        lax.all_gather(shards[2], ("dp", "fsdp"), axis=1, tiled=True),
    )

    def backward_one(carry, items):
        x_in, enc, length, frames, cot, kept = items
        grads, grad_x, grad_enc = clip_backward(back_weights, x_in, enc, length, frames, cot, kept)
        return (jax.tree.map(jnp.add, carry, grads), (grad_x, grad_enc))

    zeros = (
        jnp.zeros(weights[0].shape, jnp.float32),
        jnp.zeros(weights[1].shape, jnp.float32),
        jnp.zeros(weights[2].shape, jnp.float32),
    )
    totals, (d_tokens, d_enc) = lax.scan(
        backward_one, zeros, (tokens, enc_states, tok_len, frame_count, cotangent, saved)
    )
    grad_attn, grad_mlp, grad_vec = (
        lax.psum_scatter(totals[0], ("dp", "fsdp"), scatter_dimension=1, tiled=True),
        lax.psum_scatter(totals[1], ("dp", "fsdp"), scatter_dimension=1, tiled=True),
        lax.psum_scatter(totals[2], ("dp", "fsdp"), scatter_dimension=1, tiled=True),
    )
    attn_new = adam_update(attn_w, attn_m, attn_v, grad_attn, rate_attention)
    mlp_new = adam_update(mlp_w, mlp_m, mlp_v, grad_mlp, rate_feedforward)
    vec_new = adam_update(vec_w, vec_m, vec_v, grad_vec, rate_vector)
    return (
        result,
        d_tokens,
        d_enc,
        attn_new[0],
        attn_new[1],
        attn_new[2],
        mlp_new[0],
        mlp_new[1],
        mlp_new[2],
        vec_new[0],
        vec_new[1],
        vec_new[2],
    )


def fused_body(tokens, enc_states, cotangent, tok_len, frame_count, attn_w, attn_m, attn_v, mlp_w, mlp_m, mlp_v, vec_w, vec_m, vec_v):
    out, d_tokens, d_enc, gsum, grad_vec = call_block(
        tok_len, frame_count, tokens[0], enc_states[0], cotangent[0], attn_w, mlp_w.reshape(8, ROWS, D), vec_w
    )
    attn_new = adam_update(attn_w, attn_m, attn_v, gsum[:8], rate_attention)
    mlp_new = adam_update(mlp_w, mlp_m, mlp_v, gsum[8:].reshape(mlp_w.shape), rate_feedforward)
    vec_new = adam_update(vec_w, vec_m, vec_v, grad_vec, rate_vector)
    return (out[None], d_tokens[None], d_enc.reshape(enc_states.shape), *attn_new, *mlp_new, *vec_new)


def solution(mesh):
    fused = mesh.shape["dp"] == DEPTH and mesh.shape["fsdp"] == 2 * PLANE
    return jax.shard_map(
        fused_body if fused else plain_body,
        mesh=mesh,
        in_specs=(
            P(("dp", "fsdp"), None, None),
            P(("dp", "fsdp"), None, None),
            P(("dp", "fsdp"), None, None),
            P(("dp", "fsdp")),
            P(("dp", "fsdp")),
            P(None, ("dp", "fsdp"), None),
            P(None, ("dp", "fsdp"), None),
            P(None, ("dp", "fsdp"), None),
            P(None, ("dp", "fsdp"), None),
            P(None, ("dp", "fsdp"), None),
            P(None, ("dp", "fsdp"), None),
            P(None, ("dp", "fsdp")),
            P(None, ("dp", "fsdp")),
            P(None, ("dp", "fsdp")),
        ),
        out_specs=(
            P(("dp", "fsdp"), None, None),
            P(("dp", "fsdp"), None, None),
            P(("dp", "fsdp"), None, None),
            P(None, ("dp", "fsdp"), None),
            P(None, ("dp", "fsdp"), None),
            P(None, ("dp", "fsdp"), None),
            P(None, ("dp", "fsdp"), None),
            P(None, ("dp", "fsdp"), None),
            P(None, ("dp", "fsdp"), None),
            P(None, ("dp", "fsdp")),
            P(None, ("dp", "fsdp")),
            P(None, ("dp", "fsdp")),
        ),
        check_vma=False,
    )
```
